32 devices in a mesh: dp: 4 (over y, core), ctx: 2 (over x), tensor: 4 (over z).
Axes of the slice: x: 2, y: 2, z: 4, core: 2. Of those that a mesh axis runs over, the one named last changes fastest.
Arguments:
- tokens: bfloat16 [4, 1024, 2048], P('dp', ('ctx', 'tensor')), may hold values from -6 to 6
- cotangent: bfloat16 [4, 1024, 2048], P('dp', ('ctx', 'tensor')), may hold values from -6 to 6
- norm_gains: float32 [2, 2, 2048], replicated, may hold values from 0.5 to 1.5
- norm_biases: float32 [2, 2, 2048], replicated, may hold values from -1.8 to 1.8
- qkv_weight: bfloat16 [2, 2048, 3, 2048], P(None, 'dp', None, 'tensor'), may hold values from -0.125 to 0.125
- qkv_bias: float32 [2, 3, 2048], replicated, may hold values from -3 to 3
- out_weight: bfloat16 [2, 2048, 2048], P(None, 'tensor', 'dp'), may hold values from -0.75 to 0.75
- gate_up_weight: bfloat16 [2, 2048, 2, 5632], P(None, 'dp', None, 'tensor'), may hold values from -0.125 to 0.125
- down_weight: bfloat16 [2, 5632, 2048], P(None, 'tensor', 'dp'), may hold values from -0.078125 to 0.078125
Outputs:
- out: bfloat16 [4, 1024, 2048], P('dp', ('ctx', 'tensor'))
- tokens_grad: bfloat16 [4, 1024, 2048], P('dp', ('ctx', 'tensor'))
- norm_gains_grad: float32 [2, 2, 2048], replicated
- norm_biases_grad: float32 [2, 2, 2048], replicated
- qkv_weight_grad: float32 [2, 2048, 3, 2048], P(None, 'dp', None, 'tensor')
- qkv_bias_grad: float32 [2, 3, 2048], replicated
- out_weight_grad: float32 [2, 2048, 2048], P(None, 'tensor', 'dp')
- gate_up_weight_grad: float32 [2, 2048, 2, 5632], P(None, 'dp', None, 'tensor')
- down_weight_grad: float32 [2, 5632, 2048], P(None, 'tensor', 'dp')
The draws below stay inside these ranges and needn't reach their ends.
All inputs are finite; a program needn't handle non-finite values.
Results may differ from the reference program's by a relative error of at most 0.03.
Values may be sent and summed in bfloat16 or wider, within the bound.
No kernel may reach another device: no remote copies, remote signals or barrier semaphores. Data moves between devices by JAX's collectives and lax.ppermute only.
A program may use at most 384 MiB of HBM per device.

```python
import jax
import jax.numpy as jnp
from jax import lax

D = 2048
H = 32
HD = 64
ROT = 16
FF = 5632
LAYERS = 2
LEN = 1024
SEQS = 4


def shard_levels(stream_key, dims, cuts, smallest, largest):
    def one(position, parts):
        heights = jax.random.uniform(jax.random.fold_in(jax.random.fold_in(stream_key, 6), position), (parts,), jnp.float32, smallest / len(cuts), largest / len(cuts))
        return jnp.repeat(jnp.exp(heights), dims[position] // parts).reshape((-1,) + (1,) * (len(dims) - position - 1))

    factor_of = one(*cuts[0])
    for cut in cuts[1:]:
        factor_of = factor_of * one(*cut)
    return factor_of


def noise(own_key, dims, scale, bound, split=(), kind=jnp.bfloat16):
    drawn = scale * jax.random.normal(own_key, dims, jnp.float32)
    if split:
        drawn = drawn * shard_levels(own_key, dims, split, -0.22, 0.18)
    return jnp.clip(drawn, -bound, bound).astype(kind)


def setup_inputs(seed: int = 0) -> dict:
    streams_of = jax.random.split(jax.random.key(seed), 10)
    tokens = noise(streams_of[0], (SEQS, LEN, D), 1.0, 6.0, ((0, 4), (1, 8)))
    cotangent = noise(streams_of[1], (SEQS, LEN, D), 1.0, 6.0, ((0, 4), (1, 8)))
    norm_gains = jnp.clip(1.0 + 0.1 * jax.random.normal(streams_of[2], (LAYERS, 2, D), jnp.float32), 0.5, 1.5)
    norm_biases = noise(streams_of[3], (LAYERS, 2, D), 0.3, 1.8, (), jnp.float32)
    qkv_weight = noise(streams_of[4], (LAYERS, D, 3, D), D ** -0.5, 0.125, ((1, 4), (3, 4)))
    qkv_bias = noise(streams_of[5], (LAYERS, 3, D), 0.5, 3.0, (), jnp.float32)
    out_weight = noise(streams_of[6], (LAYERS, D, D), HD ** -0.5, 0.75, ((1, 4), (2, 4)))
    gate_up_weight = noise(streams_of[7], (LAYERS, D, 2, FF), D ** -0.5, 0.125, ((1, 4), (3, 4)))
    down_weight = noise(streams_of[8], (LAYERS, FF, D), FF ** -0.5, 0.078125, ((1, 4), (2, 4)))
    return dict(tokens=tokens, cotangent=cotangent, norm_gains=norm_gains, norm_biases=norm_biases, qkv_weight=qkv_weight, qkv_bias=qkv_bias, out_weight=out_weight, gate_up_weight=gate_up_weight, down_weight=down_weight)


@jax.custom_vjp
def low(v):
    return lax.optimization_barrier(v.astype(jnp.bfloat16)).astype(jnp.float32)

@jax.custom_vjp
def low_back(v):
    return v

def low_keep(v):
    return (low(v), None)

def low_pass(kept, grad):
    return (grad,)

def back_keep(v):
    return (v, None)

def back_low(kept, grad):
    return (low(grad),)
low.defvjp(low_keep, low_pass)
low_back.defvjp(back_keep, back_low)
HIGHEST = lax.Precision.HIGHEST
MASKED = -1e+30
EPSILON = 1e-05

def layer_norm(stream, gain, bias):
    row_mean = lax.optimization_barrier(jnp.mean(stream, axis=-1, keepdims=True))
    centered = stream - row_mean
    inverse = lax.rsqrt(lax.optimization_barrier(jnp.mean(centered * centered, axis=-1, keepdims=True)) + EPSILON)
    return centered * inverse * gain + bias

def rotary(heads4):
    half_rot = ROT // 2
    frequency = 10000.0 ** (-(jnp.arange(half_rot, dtype=jnp.float32) * 2.0) / ROT)
    angles = jnp.arange(heads4.shape[1], dtype=jnp.float32)[:, None] * frequency[None, :]
    cosine_table = jnp.cos(angles)[:, None, :]
    sine_table = jnp.sin(angles)[:, None, :]
    front_part = heads4[..., :half_rot]
    back_part = heads4[..., half_rot:ROT]
    new_front = front_part * cosine_table - back_part * sine_table
    new_back = back_part * cosine_table + front_part * sine_table
    return jnp.concatenate([new_front, new_back, heads4[..., ROT:]], axis=-1)

def head_attention(head_inputs):
    queries, key_heads, value_heads = head_inputs
    scores = jnp.einsum('sqd,skd->sqk', queries, key_heads, precision=HIGHEST) * HD ** (-0.5)
    scores = low_back(scores)
    positions = jnp.arange(queries.shape[1])
    allowed = positions[None, :] <= positions[:, None]
    probabilities = jax.nn.softmax(jnp.where(allowed, scores, MASKED), axis=-1)
    return jnp.einsum('sqk,skd->sqd', low(probabilities), value_heads, precision=HIGHEST)

def block_forward(stream, layer_gains, layer_biases, qkv_full, qkv_row_bias, out_full, gate_up_full, down_full):
    seq_count = stream.shape[0]
    length = stream.shape[1]
    normed = low(layer_norm(stream, layer_gains[0], layer_biases[0]))
    projected = low_back(jnp.einsum('std,dce->stce', normed, qkv_full, precision=HIGHEST))
    biased = projected + qkv_row_bias
    queries = low(rotary(biased[:, :, 0].reshape(seq_count, length, H, HD)))
    key_heads = low(rotary(biased[:, :, 1].reshape(seq_count, length, H, HD)))
    value_heads = low(biased[:, :, 2].reshape(seq_count, length, H, HD))
    per_head = lax.map(jax.checkpoint(head_attention), (jnp.transpose(queries, (2, 0, 1, 3)), jnp.transpose(key_heads, (2, 0, 1, 3)), jnp.transpose(value_heads, (2, 0, 1, 3))))
    attended = low_back(low(jnp.transpose(per_head, (1, 2, 0, 3)).reshape(seq_count, length, D)))
    hidden = stream + low_back(jnp.einsum('stk,kd->std', attended, out_full, precision=HIGHEST))
    normed_two = low(layer_norm(hidden, layer_gains[1], layer_biases[1]))
    gate_up = low_back(jnp.einsum('std,dcf->stcf', normed_two, gate_up_full, precision=HIGHEST))
    activated = low(jax.nn.silu(gate_up[:, :, 0]) * gate_up[:, :, 1])
    return hidden + low_back(jnp.einsum('stf,fd->std', activated, down_full, precision=HIGHEST))

def reference(tokens, cotangent, norm_gains, norm_biases, qkv_weight, qkv_bias, out_weight, gate_up_weight, down_weight):

    def forward(stream_all, gains_all, biases_all, qkv_all, qkv_bias_all, out_all, gate_up_all, down_all):

        def sequence_forward(sequence):
            stream = sequence[None]
            for layer_index in range(LAYERS):
                stream = block_forward(stream, gains_all[layer_index], biases_all[layer_index], qkv_all[layer_index], qkv_bias_all[layer_index], out_all[layer_index], gate_up_all[layer_index], down_all[layer_index])
            return stream[0]
        return lax.map(jax.checkpoint(sequence_forward), stream_all)
    inputs = (tokens.astype(jnp.float32), norm_gains.astype(jnp.float32), norm_biases.astype(jnp.float32), qkv_weight.astype(jnp.float32), qkv_bias.astype(jnp.float32), out_weight.astype(jnp.float32), gate_up_weight.astype(jnp.float32), down_weight.astype(jnp.float32))
    result, pullback = jax.vjp(forward, *inputs)
    grads = pullback(cotangent.astype(jnp.float32))
    return (result.astype(jnp.bfloat16), grads[0].astype(jnp.bfloat16), grads[1], grads[2], grads[3], grads[4], grads[5], grads[6], grads[7])
```

```python
import functools

import jax
import jax.numpy as jnp
from jax import lax
from jax.experimental import pallas as pl
from jax.experimental.pallas import tpu as pltpu
from jax.sharding import PartitionSpec as P

HD = 64
ROT = 16
LAYERS = 2

MASKED = -1e30
EPSILON = 1e-05
LOW = jnp.bfloat16
WIDE = jnp.float32


def layer_norm_rows(stream, gain, bias):
    row_mean = jnp.mean(stream, axis=-1, keepdims=True)
    centered = stream - row_mean
    inverse = lax.rsqrt(jnp.mean(centered * centered, axis=-1, keepdims=True) + EPSILON)
    unit_rows = centered * inverse
    return (unit_rows * gain + bias, unit_rows, inverse)


def norm_backward(grad_rows, unit_rows, inverse, gain):
    grad_unit = grad_rows * gain
    first_mean = jnp.mean(grad_unit, axis=-1, keepdims=True)
    second_mean = jnp.mean(grad_unit * unit_rows, axis=-1, keepdims=True)
    grad_input = inverse * (grad_unit - first_mean - unit_rows * second_mean)
    return (grad_input, jnp.sum(grad_rows * unit_rows, axis=0), jnp.sum(grad_rows, axis=0))


def rotary_tables(positions):
    half_rot = ROT // 2
    frequency = 10000.0 ** (-(jnp.arange(half_rot, dtype=jnp.float32) * 2.0) / ROT)
    angles = positions.astype(jnp.float32)[:, None] * frequency[None, :]
    cosine, sine = jnp.cos(angles), jnp.sin(angles)
    rest = jnp.zeros((angles.shape[0], HD - ROT), WIDE)
    none = jnp.zeros_like(sine)
    heads = lambda *parts: jnp.tile(jnp.concatenate(parts, axis=1), (1, PAIR // HD))
    return (
        heads(cosine, cosine, rest + 1.0),
        heads(-sine, none, rest),
        heads(none, sine, rest),
    )


def rotated(flat, cos_ref, right_ref, left_ref):
    shift = ROT // 2
    found = []
    for start in range(0, flat.shape[1], PAIR):
        v = flat[:, start : start + PAIR]
        right, left = pltpu.roll(v, PAIR - shift, 1), pltpu.roll(v, shift, 1)
        found.append(v * cos_ref[...] + right * right_ref[...] + left * left_ref[...])
    return jnp.concatenate(found, axis=1)


def dot(a, b, dims):
    return lax.dot_general(a, b, (dims, ((), ())), preferred_element_type=WIDE)


PAIR = 128


NN = ((1,), (0,))
NT = ((1,), (1,))
TN = ((0,), (0,))


def total_of(terms):
    return functools.reduce(lambda a, b: a + b, terms)


def work(flops):
    return pl.CostEstimate(flops=int(flops), bytes_accessed=0, transcendentals=0)


TILE = 256


def tiled(kernel, name, steps, ins, outs, flops):
    return pl.pallas_call(
        kernel,
        grid=(steps,),
        in_specs=[pl.BlockSpec(block, index) for _, block, index in ins],
        out_specs=[pl.BlockSpec(block, index) for _, block, index in outs],
        out_shape=[shape for shape, _, _ in outs],
        compiler_params=pltpu.CompilerParams(vmem_limit_bytes=48 * 1024 * 1024),
        cost_estimate=work(2.5 * flops),
        name=name,
    )(*[array for array, _, _ in ins])


def whole_block(array):
    return (array, array.shape, lambda i: (0,) * array.ndim)


def column_block(array):
    return (array, (array.shape[0], TILE), lambda i: (0, i))


def row_block(array):
    return (array, (TILE, array.shape[1]), lambda i: (i, 0))


def gate_up_kernel(rows_ref, gate_w_ref, up_w_ref, gate_ref, up_ref, activated_ref):
    rows = rows_ref[...]
    gate = dot(rows, gate_w_ref[...], NN)
    up = dot(rows, up_w_ref[...], NN)
    gate_ref[...] = gate
    up_ref[...] = up
    activated_ref[...] = (gate * jax.nn.sigmoid(gate) * up).astype(LOW)


def gate_up_rows(rows, gate_weight, up_weight):
    count, hidden = rows.shape[0], gate_weight.shape[1]
    shapes = [jax.ShapeDtypeStruct((count, hidden), t) for t in (WIDE, WIDE, LOW)]
    return tiled(
        gate_up_kernel,
        "gate_up",
        pl.cdiv(hidden, TILE),
        [whole_block(rows), column_block(gate_weight), column_block(up_weight)],
        [column_block(s) for s in shapes],
        4 * rows.size * hidden,
    )


def back_sum(rows, weight_ref):
    width = weight_ref.shape[2]
    return total_of(
        dot(rows[:, r * width : (r + 1) * width], weight_ref[r], NT)
        for r in range(weight_ref.shape[0])
    )


def tall_block(array):
    return (array, (array.shape[0], TILE, array.shape[2]), lambda i: (0, i, 0))


def gate_up_back_kernel(rows_ref, weight_ref, gate_ref, up_ref, grad_gate_ref, grad_up_ref):
    grad = back_sum(rows_ref[...], weight_ref)
    gate, up = gate_ref[...], up_ref[...]
    s = jax.nn.sigmoid(gate)
    grad_gate_ref[...] = (grad * up * s * (1.0 + gate * (1.0 - s))).astype(LOW)
    grad_up_ref[...] = (grad * (gate * s)).astype(LOW)


def gate_up_back(rows, down_weight, gate, up):
    count, hidden = gate.shape
    shape = jax.ShapeDtypeStruct((count, hidden), LOW)
    return tiled(
        gate_up_back_kernel,
        "gate_up_back",
        pl.cdiv(hidden, TILE),
        [whole_block(rows), tall_block(down_weight), column_block(gate), column_block(up)],
        [column_block(shape)] * 2,
        2 * rows.size * hidden,
    )


def out_back_kernel(rows_ref, weight_ref, out_ref):
    out_ref[...] = back_sum(rows_ref[...], weight_ref).astype(LOW)


def out_back(rows, weight):
    shape = jax.ShapeDtypeStruct((rows.shape[0], weight.shape[1]), LOW)
    return tiled(
        out_back_kernel,
        "out_back",
        shape.shape[1] // TILE,
        [whole_block(rows), tall_block(weight)],
        [column_block(shape)],
        2 * rows.size * shape.shape[1],
    )[0]


def wide_kernel(rows_ref, weight_ref, out_ref):
    out_ref[...] = dot(rows_ref[...], weight_ref[0], NN).astype(LOW)


def times_wide(rows, weight, name):
    blocks, depth, width = weight.shape
    per = width // TILE
    shape = jax.ShapeDtypeStruct((rows.shape[0], blocks * width), LOW)
    return tiled(
        wide_kernel,
        name,
        blocks * per,
        [whole_block(rows), (weight, (1, depth, TILE), lambda i: (i // per, 0, i % per))],
        [column_block(shape)],
        2 * rows.size * blocks * width,
    )[0]


def gate_up_in_kernel(gate_ref, up_ref, gate_w_ref, up_w_ref, out_ref):
    total = dot(gate_ref[...], gate_w_ref[...], NT) + dot(up_ref[...], up_w_ref[...], NT)
    out_ref[...] = total.astype(LOW)


def gate_up_in(grad_gate, grad_up, gate_weight, up_weight):
    shape = jax.ShapeDtypeStruct((grad_gate.shape[0], gate_weight.shape[0]), LOW)
    return tiled(
        gate_up_in_kernel,
        "gate_up_in",
        shape.shape[1] // TILE,
        [whole_block(grad_gate), whole_block(grad_up), row_block(gate_weight), row_block(up_weight)],
        [column_block(shape)],
        4 * grad_gate.size * shape.shape[1],
    )[0]


def project_in_kernel(rows_ref, weight_ref, out_ref):
    width = weight_ref.shape[3]
    out_ref[...] = total_of(
        dot(rows_ref[:, c * width : (c + 1) * width], weight_ref[0, c], NT) for c in range(3)
    ).astype(LOW)


def project_in(rows, weight):
    blocks, three, depth, width = weight.shape
    per = depth // TILE
    shape = jax.ShapeDtypeStruct((rows.shape[0], blocks * depth), LOW)
    return tiled(
        project_in_kernel,
        "project_in",
        blocks * per,
        [whole_block(rows), (weight, (1, three, TILE, width), lambda i: (i // per, 0, i % per, 0))],
        [column_block(shape)],
        2 * rows.size * blocks * depth,
    )[0]


def project_kernel(rows_ref, weight_ref, bias_ref, cos_ref, right_ref, left_ref, q_ref, kv_ref):
    blocks, _, depth, width = weight_ref.shape
    flat = dot(rows_ref[...], weight_ref[...].reshape(blocks * depth, width), NN) + bias_ref[0]
    step = pl.program_id(0)

    @pl.when(step == 0)
    def _():
        kv_ref[...] = rotated(flat, cos_ref, right_ref, left_ref).astype(LOW)

    @pl.when(step == 1)
    def _():
        kv_ref[...] = flat.astype(LOW)

    @pl.when(step == 2)
    def _():
        q_ref[...] = rotated(flat, cos_ref, right_ref, left_ref).astype(LOW)


def project(rows, weight, bias, tables):
    count = rows.shape[0]
    blocks, _, depth, width = weight.shape
    fixed = lambda i: (0, 0)
    shapes = [jax.ShapeDtypeStruct((k * count, width), LOW) for k in (1, 2)]
    return tiled(
        project_kernel,
        "project",
        3,
        [
            whole_block(rows),
            (weight, (blocks, 1, depth, width), lambda i: (0, (i + 1) % 3, 0, 0)),
            (bias[:, None, :], (1, 1, width), lambda i: ((i + 1) % 3, 0, 0)),
        ]
        + [(t, (count, PAIR), fixed) for t in tables],
        [
            (shapes[0], (count, width), fixed),
            (shapes[1], (count, width), lambda i: (jnp.minimum(i, 1), 0)),
        ],
        6 * rows.size * width,
    )


def project_back_kernel(far, dq_ref, dkv_ref, *refs):
    far_refs = refs[:far]
    cos_ref, right_ref, left_ref, out_ref, sum_ref = refs[far:]
    step = pl.program_id(0)

    def put(value):
        out_ref[...] = value.astype(LOW)
        sum_ref[0] = jnp.sum(value, axis=0, keepdims=True)

    def key_value():
        return total_of([dkv_ref[...]] + [r[...].astype(WIDE) for r in far_refs])

    @pl.when(step == 0)
    def _():
        put(rotated(dq_ref[...], cos_ref, right_ref, left_ref))

    @pl.when(step == 1)
    def _():
        put(rotated(key_value(), cos_ref, right_ref, left_ref))

    @pl.when(step == 2)
    def _():
        put(key_value())


def project_back(dq, dkv, far, tables):
    count, width = dq.shape
    fixed = lambda i: (0, 0)
    lower = pl.BlockSpec((count, width), lambda i: (jnp.maximum(i - 1, 0), 0))
    out, sums = pl.pallas_call(
        functools.partial(project_back_kernel, len(far)),
        grid=(3,),
        in_specs=[pl.BlockSpec((count, width), fixed)]
        + [lower] * (1 + len(far))
        + [pl.BlockSpec((count, PAIR), fixed)] * 3,
        out_specs=[
            pl.BlockSpec((count, width), lambda i: (0, i)),
            pl.BlockSpec((1, 1, width), lambda i: (i, 0, 0)),
        ],
        out_shape=[
            jax.ShapeDtypeStruct((count, 3 * width), LOW),
            jax.ShapeDtypeStruct((3, 1, width), WIDE),
        ],
        compiler_params=pltpu.CompilerParams(vmem_limit_bytes=32 * 1024 * 1024),
        cost_estimate=work(14000 * count * width),
        name="project_back",
    )(dq, dkv, *far, *tables)
    return out, sums[:, 0]


def attend_kernel(blocks, qpos_ref, kpos_ref, q_ref, *refs):
    keys, values = refs[: 2 * blocks : 2], refs[1 : 2 * blocks : 2]
    out_ref, lse_ref = refs[2 * blocks :]
    allowed = [kpos_ref[b] <= qpos_ref[...] for b in range(blocks)]
    for half in range(PAIR // HD):
        lanes = slice(half * HD, (half + 1) * HD)
        q = q_ref[:, lanes] * jnp.asarray(HD**-0.5, LOW)
        top, total, acc = None, None, None
        for b in range(blocks):
            s = jnp.where(allowed[b], dot(q, keys[b][:, lanes], NT), MASKED)
            block_top = jnp.max(s, axis=1, keepdims=True)
            new_top = block_top if b == 0 else jnp.maximum(top, block_top)
            p = jnp.exp(s - new_top)
            block_total = jnp.sum(p, axis=1, keepdims=True)
            block_acc = dot(p.astype(LOW), values[b][:, lanes], NN)
            if b == 0:
                total, acc = block_total, block_acc
            else:
                factor = jnp.exp(top - new_top)
                total = total * factor + block_total
                acc = acc * factor + block_acc
            top = new_top
        out_ref[:, lanes] = acc / total
        lse_ref[half] = top + jnp.log(total)


def attend(qpos, kpos, q, pairs_of_rows):
    rows, width = q.shape
    key_rows = pairs_of_rows[0].shape[0] // 2
    blocks = len(pairs_of_rows)
    pairs = width // PAIR
    per_pair = PAIR // HD
    column = lambda i: (0, i)
    fixed = lambda i: (0, 0)
    key_specs = [pl.BlockSpec((key_rows, PAIR), lambda i, c=c: (c, i)) for c in range(2)]
    stacked = [rows_of for rows_of in pairs_of_rows for c in range(2)]
    return pl.pallas_call(
        functools.partial(attend_kernel, blocks),
        grid=(pairs,),
        in_specs=[
            pl.BlockSpec((rows, 1), fixed),
            pl.BlockSpec((blocks, 1, key_rows), lambda i: (0, 0, 0)),
            pl.BlockSpec((rows, PAIR), column),
        ]
        + key_specs * blocks,
        out_specs=[
            pl.BlockSpec((rows, PAIR), column),
            pl.BlockSpec((per_pair, rows, 1), lambda i: (i, 0, 0)),
        ],
        out_shape=[
            jax.ShapeDtypeStruct((rows, width), WIDE),
            jax.ShapeDtypeStruct((width // HD, rows, 1), WIDE),
        ],
        compiler_params=pltpu.CompilerParams(vmem_limit_bytes=32 * 1024 * 1024),
        cost_estimate=work(43 * rows * key_rows * blocks * width),
        name="attend",
    )(qpos, kpos, q, *stacked)


def attend_back_kernel(blocks, qpos_ref, kpos_ref, q_ref, grad_ref, out_ref, lse_ref, *refs):
    keys, values = refs[: 2 * blocks : 2], refs[1 : 2 * blocks : 2]
    dq_ref = refs[2 * blocks]
    dboth = refs[2 * blocks + 1 :]
    key_rows = keys[0].shape[0]
    allowed = [kpos_ref[b] <= qpos_ref[...] for b in range(blocks)]
    scale = HD**-0.5
    for half in range(PAIR // HD):
        lanes = slice(half * HD, (half + 1) * HD)
        q = q_ref[:, lanes] * jnp.asarray(scale, LOW)
        grad = grad_ref[:, lanes]
        lse = lse_ref[half]
        delta = jnp.sum(grad.astype(WIDE) * out_ref[:, lanes], axis=1, keepdims=True)
        dq = None
        for b in range(blocks):
            k = keys[b][:, lanes]
            s = jnp.where(allowed[b], dot(q, k, NT), MASKED)
            p = jnp.exp(s - lse)
            dp = dot(grad, values[b][:, lanes], NT)
            ds = (p * (dp - delta)).astype(LOW)
            kind = dboth[b].dtype
            dboth[b][key_rows:, lanes] = dot(p.astype(LOW), grad, TN).astype(kind)
            dboth[b][:key_rows, lanes] = dot(ds, q, TN).astype(kind)
            term = dot(ds, k, NN)
            dq = term if b == 0 else dq + term
        dq_ref[:, lanes] = dq * scale


def attend_back(qpos, kpos, q, grad, out, lse, pairs_of_rows):
    rows, width = q.shape
    key_rows = pairs_of_rows[0].shape[0] // 2
    blocks = len(pairs_of_rows)
    pairs = width // PAIR
    per_pair = PAIR // HD
    column = lambda i: (0, i)
    fixed = lambda i: (0, 0)
    row_spec = pl.BlockSpec((rows, PAIR), column)
    key_specs = [pl.BlockSpec((key_rows, PAIR), lambda i, c=c: (c, i)) for c in range(2)]
    stacked = [rows_of for rows_of in pairs_of_rows for c in range(2)]
    far = [jax.ShapeDtypeStruct((2 * key_rows, width), LOW)] * (blocks - 1)
    near = [jax.ShapeDtypeStruct((2 * key_rows, width), WIDE)]
    results = pl.pallas_call(
        functools.partial(attend_back_kernel, blocks),
        grid=(pairs,),
        in_specs=[
            pl.BlockSpec((rows, 1), fixed),
            pl.BlockSpec((blocks, 1, key_rows), lambda i: (0, 0, 0)),
            row_spec,
            row_spec,
            row_spec,
            pl.BlockSpec((per_pair, rows, 1), lambda i: (i, 0, 0)),
        ]
        + key_specs * blocks,
        out_specs=[row_spec] + [pl.BlockSpec((2 * key_rows, PAIR), column)] * blocks,
        out_shape=[jax.ShapeDtypeStruct((rows, width), WIDE)] + near + far,
        compiler_params=pltpu.CompilerParams(vmem_limit_bytes=40 * 1024 * 1024),
        cost_estimate=work(75 * rows * key_rows * blocks * width),
        name="attend_back",
    )(qpos, kpos, q, grad, out, lse, *stacked)
    return results[0], results[1], results[2:]


def bits_of(count):
    return [1 << k for k in range(count.bit_length() - 1)]


def swapped(value, axis, mask):
    count = lax.axis_size(axis)
    return lax.ppermute(value, axis, [(i, i ^ mask) for i in range(count)])


class Line:
    def __init__(self, own_rows):
        n_tensor, n_ctx = lax.axis_size("tensor"), lax.axis_size("ctx")
        tensor, ctx = lax.axis_index("tensor"), lax.axis_index("ctx")
        self.count, self.tensor = n_tensor, tensor
        row = jnp.arange(own_rows, dtype=jnp.int32)
        chip = (tensor + jnp.arange(n_tensor, dtype=jnp.int32)) % n_tensor
        place = (chip[:, None] * own_rows + row[None, :]).reshape(-1)
        block = n_tensor * own_rows
        self.places = ctx * block + place
        self.key_places = [self.places] + [
            jnp.where(ctx >= s, (ctx - s) * block + place, 1 << 30) for s in range(1, n_ctx)
        ]
        self.own_rows = own_rows

    def gather_rows(self, low):
        count, t = self.count, self.tensor
        send = lambda v, *route: lax.ppermute(v, "tensor", list(route))
        if count == 4:
            far = send(low, (0, 2), (2, 0), (1, 3), (3, 1))
            above = send(low, (0, 1), (1, 2), (2, 3))
            below = send(low, (1, 0), (2, 1), (3, 2))
            end = send(far, (2, 3), (1, 0))
            found = [low, jnp.where(t == 3, end, below), far, jnp.where(t == 0, end, above)]
        else:
            found = [low] + [
                send(low, *[((i + d) % count, i) for i in range(count)]) for d in range(1, count)
            ]
        return jnp.concatenate(found, axis=0)

    def sum_rows(self, low):
        rows, count, t = self.own_rows, self.count, self.tensor
        terms = [low[d * rows : (d + 1) * rows] for d in range(count)]
        send = lambda v, *route: lax.ppermute(v, "tensor", list(route))
        wide = lambda v: v.astype(WIDE)
        if count == 4:
            end = send(jnp.where(t == 0, terms[3], terms[1]), (0, 1), (3, 2))
            above = send(terms[1], (0, 1), (1, 2), (2, 3))
            below = send(terms[3], (3, 2), (2, 1), (1, 0))
            far = (wide(terms[2]) + wide(end)).astype(LOW)
            got = [send(far, (0, 2), (2, 0), (1, 3), (3, 1)), above, below]
        else:
            got = [
                send(terms[d], *[(i, (i + d) % count) for i in range(count)])
                for d in range(1, count)
            ]
        return total_of([wide(terms[0])] + [wide(g) for g in got])

    def owner(self, low):
        count = lax.axis_size("ctx")
        if count != 2:
            return lax.psum(low, "ctx").astype(WIDE) if count > 1 else low.astype(WIDE)
        got = yield swapped(low, "ctx", 1)
        return low.astype(WIDE) + got.astype(WIDE)

    def far_keys(self, value):
        count = lax.axis_size("ctx")
        return [
            lax.ppermute(value, "ctx", [(i, i + s) for i in range(count - s)])
            for s in range(1, count)
        ]

    def far_key_grads(self, values):
        count = lax.axis_size("ctx")
        return [
            lax.ppermute(values[s - 1], "ctx", [(i + s, i) for i in range(count - s)])
            for s in range(1, count)
        ]


def weight_stages(shard):
    shard = yield shard
    return (yield lax.all_gather(shard, "dp"))


def grad_stages(plan, value, axis):
    got = yield lax.psum_scatter(value.astype(LOW), "dp", scatter_dimension=axis, tiled=True)
    return (yield from plan.owner(got))


class Job:
    def __init__(self, stages):
        self.stages, self.value, self.result, self.done = stages, None, None, False
        self.advance(None)

    def advance(self, value):
        try:
            self.value = self.stages.send(value)
        except StopIteration as end:
            self.done, self.result, self.value = True, end.value, None

    def finish(self):
        while not self.done:
            self.advance(self.value)
        return self.result


def meanwhile(value, *jobs):
    open_jobs = [j for j in jobs if j is not None and not j.done]
    if not open_jobs:
        return value
    value, held = lax.optimization_barrier((value, tuple(j.value for j in open_jobs)))
    for job, got in zip(open_jobs, held):
        job.advance(got)
    return value


def held(value, *jobs):
    open_jobs = [j for j in jobs if j is not None and not j.done]
    if not open_jobs:
        return value
    value, kept = lax.optimization_barrier((value, tuple(j.value for j in open_jobs)))
    for job, got in zip(open_jobs, kept):
        job.value = got
    return value


def shards(
    tokens,
    cotangent,
    norm_gains,
    norm_biases,
    qkv_weight,
    qkv_bias,
    out_weight,
    gate_up_weight,
    down_weight,
):
    own_rows = tokens.shape[1]
    model = tokens.shape[2]
    heads_width = qkv_weight.shape[3]
    plan = Line(own_rows)
    tables = rotary_tables(plan.places)
    tables_back = (tables[0], -tables[1], -tables[2])
    qpos = plan.places[:, None]
    kpos = jnp.stack(plan.key_places)[:, None, :]
    gains = (norm_gains)
    biases = (norm_biases)
    qkv_bias_own = lax.dynamic_slice_in_dim(qkv_bias, lax.axis_index("tensor") * heads_width, heads_width, 2)

    def weight_jobs(layer, after):
        (qkv_all, out_all, gate_up_all, down_all), after = lax.optimization_barrier(
            ((qkv_weight, out_weight, gate_up_weight, down_weight), after)
        )
        matrices = {
            "qkv": jnp.transpose(qkv_all[layer], (1, 0, 2)),
            "out": out_all[layer],
            "gate": gate_up_all[layer, :, 0],
            "up": gate_up_all[layer, :, 1],
            "down": down_all[layer],
        }
        return {n: Job(weight_stages(v)) for n, v in matrices.items()}, after

    now, unused = weight_jobs(0, ())
    for name in ("qkv", "out", "gate", "up"):
        now[name].advance(now[name].value)
    stream = tokens[0].astype(WIDE)
    moved_cotangent = cotangent[0]
    later = {}
    saved = []
    for layer in range(LAYERS):
        last = layer + 1 == LAYERS
        normed_one, unit_one, inverse_one = layer_norm_rows(
            stream, gains[layer, 0], biases[layer, 0]
        )
        rows_one = plan.gather_rows(normed_one.astype(LOW))
        if layer == 0:
            rows_one = meanwhile(rows_one, now["qkv"], now["down"])
        else:
            rows_one = meanwhile(rows_one, now["out"], now["gate"], now["down"])
        qkv_full = now["qkv"].finish()
        queries, keys_values = project(rows_one, qkv_full, qkv_bias_own[layer], tables)
        all_kv = [keys_values] + plan.far_keys(keys_values)
        attended, lse = attend(qpos, kpos, queries, all_kv)
        attended_low = meanwhile(attended.astype(LOW), now["out"])
        if layer > 0:
            attended_low = meanwhile(attended_low, now["up"])
        out_full = now["out"].finish()
        mid = stream + plan.sum_rows(times_wide(attended_low, out_full, "out"))
        mid = meanwhile(mid, now["gate"], now["up"])
        if layer > 0:
            mid = meanwhile(mid, now["down"])
        else:
            later, mid = weight_jobs(layer + 1, mid)
        normed_two, unit_two, inverse_two = layer_norm_rows(mid, gains[layer, 1], biases[layer, 1])
        rows_two = plan.gather_rows(normed_two.astype(LOW))
        rows_two = meanwhile(rows_two, now["down"], later.get("qkv"))
        if last:
            moved_cotangent, rows_two = lax.optimization_barrier((moved_cotangent, rows_two))
            grad_stream = moved_cotangent.astype(WIDE)
            branch = plan.gather_rows(grad_stream.astype(LOW))
        flat = lambda v: v.reshape(v.shape[0] * v.shape[1], v.shape[2])
        gate_full, up_full = flat(now["gate"].finish()), flat(now["up"].finish())
        gate, up, activated = gate_up_rows(rows_two, gate_full, up_full)
        if last:
            activated, branch = lax.optimization_barrier((activated, branch))
        activated = meanwhile(activated, later.get("out"), later.get("gate"))
        down_full = now["down"].finish()
        stream = mid + plan.sum_rows(times_wide(activated, down_full, "down"))
        stream = meanwhile(stream, later.get("qkv"), later.get("up"))
        saved.append(
            (
                (qkv_full, out_full, gate_full, up_full, down_full),
                (rows_one, unit_one, inverse_one),
                (queries, all_kv, attended, attended_low, lse),
                (rows_two, unit_two, inverse_two),
                (gate, up, activated),
            )
        )
        now = later
    output = (stream).astype(LOW)[None]

    grad_jobs = [None] * LAYERS
    gain_grads = [None] * LAYERS
    bias_grads = [None] * LAYERS
    qkv_bias_grads = [None] * LAYERS
    for layer in range(LAYERS - 1, -1, -1):
        (
            (qkv_full, out_full, gate_full, up_full, down_full),
            (rows_one, unit_one, inverse_one),
            (queries, all_kv, attended, attended_low, lse),
            (rows_two, unit_two, inverse_two),
            (gate, up, activated),
        ) = saved[layer]
        mine = {}
        grad_jobs[layer] = mine
        above = grad_jobs[layer + 1] if layer + 1 < LAYERS else {}
        old = lambda *keys: [above.get(k) for k in keys]

        def in_job(a, b):
            return Job(grad_stages(plan, dot(a, b, TN), 0))

        def out_job(a, b):
            return Job(grad_stages(plan, dot(a, b, TN), 1))

        if layer + 1 < LAYERS:
            branch = plan.gather_rows(grad_stream.astype(LOW))
        branch = meanwhile(branch, *old("gate", "up", "out"))
        grad_gate, grad_up = gate_up_back(branch, down_full, gate, up)
        mine["down"] = out_job(activated, branch)
        mine["gate"] = in_job(rows_two, grad_gate)
        mine["up"] = in_job(rows_two, grad_up)
        partial_in = gate_up_in(grad_gate, grad_up, gate_full, up_full)
        grad_mid, gain_two, bias_two = norm_backward(
            plan.sum_rows(partial_in), unit_two, inverse_two, gains[layer, 1]
        )
        hidden_grad = grad_stream + grad_mid
        hidden_grad = meanwhile(hidden_grad, *old("up", "out", "qkv"))
        attention = plan.gather_rows(hidden_grad.astype(LOW))
        attention = meanwhile(attention, *old("qkv"))
        attention = held(attention, mine["down"])
        grad_attended = out_back(attention, out_full)
        grad_queries, grad_kv, far_grads = attend_back(
            qpos, kpos, queries, grad_attended, attended, lse, all_kv
        )
        mine["out"] = out_job(attended_low, attention)
        projected, qkv_bias_grads[layer] = project_back(
            grad_queries, grad_kv, plan.far_key_grads(far_grads), tables_back
        )
        projected = meanwhile(projected, mine["down"], mine["gate"])
        partial_in = project_in(projected, qkv_full)
        mine["qkv"] = in_job(rows_one, projected)
        grad_first, gain_one, bias_one = norm_backward(
            plan.sum_rows(partial_in), unit_one, inverse_one, gains[layer, 0]
        )
        grad_stream = hidden_grad + grad_first
        if layer > 0:
            grad_stream = held(meanwhile(grad_stream, mine["down"], mine["gate"]), mine["up"])
        gain_grads[layer] = jnp.stack([gain_one, gain_two])
        bias_grads[layer] = jnp.stack([bias_one, bias_two])

    tokens_grad = (grad_stream).astype(LOW)[None]
    padded_bias = lax.dynamic_update_slice_in_dim(
        jnp.zeros((LAYERS, 3, qkv_bias.shape[2]), WIDE),
        jnp.stack(qkv_bias_grads),
        lax.axis_index("tensor") * heads_width,
        2,
    )
    small = jnp.concatenate(
        [
            (jnp.stack(gain_grads)).reshape(LAYERS * 2, model),
            (jnp.stack(bias_grads)).reshape(LAYERS * 2, model),
            padded_bias.reshape(LAYERS * 3, qkv_bias.shape[2]),
        ],
        axis=0,
    )
    for axis in ("dp", "ctx", "tensor"):
        for bit in bits_of(lax.axis_size(axis)):
            small = small + swapped(small, axis, bit)
    sums = [{k: j.finish() for k, j in g.items()} for g in grad_jobs]
    return (
        output,
        tokens_grad,
        small[: LAYERS * 2].reshape(LAYERS, 2, model),
        small[LAYERS * 2 : LAYERS * 4].reshape(LAYERS, 2, model),
        jnp.stack([s["qkv"].reshape(-1, 3, heads_width) for s in sums]),
        small[LAYERS * 4 :].reshape(LAYERS, 3, qkv_bias.shape[2]),
        jnp.stack([s["out"] for s in sums]),
        jnp.stack([jnp.stack([s["gate"], s["up"]], axis=1) for s in sums]),
        jnp.stack([s["down"] for s in sums]),
    )


def solution(mesh):
    rows = P("dp", ("ctx", "tensor"), None)
    wide = P(None, "dp", None, "tensor")
    tall = P(None, "tensor", "dp")
    return jax.shard_map(
        shards,
        mesh=mesh,
        in_specs=(rows, rows, P(), P(), wide, P(), tall, wide, tall),
        out_specs=(rows, rows, P(), P(), wide, P(), tall, wide, tall),
        check_vma=False,
    )
```

```python
import functools

import jax
import jax.numpy as jnp
from jax import lax
from jax.experimental import pallas as pl
from jax.experimental.pallas import tpu as pltpu
from jax.sharding import PartitionSpec as P

HD = 64
ROT = 16
LAYERS = 2

MASKED = -1e30
EPSILON = 1e-05
LOW = jnp.bfloat16
WIDE = jnp.float32


def layer_norm_rows(stream, gain, bias):
    row_mean = jnp.mean(stream, axis=-1, keepdims=True)
    centered = stream - row_mean
    inverse = lax.rsqrt(jnp.mean(centered * centered, axis=-1, keepdims=True) + EPSILON)
    unit_rows = centered * inverse
    return (unit_rows * gain + bias, unit_rows, inverse)


def norm_backward(grad_rows, unit_rows, inverse, gain):
    grad_unit = grad_rows * gain
    first_mean = jnp.mean(grad_unit, axis=-1, keepdims=True)
    second_mean = jnp.mean(grad_unit * unit_rows, axis=-1, keepdims=True)
    grad_input = inverse * (grad_unit - first_mean - unit_rows * second_mean)
    return (grad_input, jnp.sum(grad_rows * unit_rows, axis=0), jnp.sum(grad_rows, axis=0))


def rotary_tables(positions):
    half_rot = ROT // 2
    frequency = 10000.0 ** (-(jnp.arange(half_rot, dtype=jnp.float32) * 2.0) / ROT)
    angles = positions.astype(jnp.float32)[:, None] * frequency[None, :]
    cosine, sine = jnp.cos(angles), jnp.sin(angles)
    rest = jnp.zeros((angles.shape[0], HD - ROT), WIDE)
    none = jnp.zeros_like(sine)
    heads = lambda *parts: jnp.tile(jnp.concatenate(parts, axis=1), (1, PAIR // HD))
    return (
        heads(cosine, cosine, rest + 1.0),
        heads(-sine, none, rest),
        heads(none, sine, rest),
    )


def rotated(flat, cos_ref, right_ref, left_ref):
    shift = ROT // 2
    found = []
    for start in range(0, flat.shape[1], PAIR):
        v = flat[:, start : start + PAIR]
        right, left = pltpu.roll(v, PAIR - shift, 1), pltpu.roll(v, shift, 1)
        found.append(v * cos_ref[...] + right * right_ref[...] + left * left_ref[...])
    return jnp.concatenate(found, axis=1)


def dot(a, b, dims):
    return lax.dot_general(a, b, (dims, ((), ())), preferred_element_type=WIDE)


PAIR = 128


NN = ((1,), (0,))
NT = ((1,), (1,))
TN = ((0,), (0,))


def total_of(terms):
    return functools.reduce(lambda a, b: a + b, terms)


def work(flops):
    return pl.CostEstimate(flops=int(flops), bytes_accessed=0, transcendentals=0)


TILE = 256


def tiled(kernel, name, steps, ins, outs, flops):
    return pl.pallas_call(
        kernel,
        grid=(steps,),
        in_specs=[pl.BlockSpec(block, index) for _, block, index in ins],
        out_specs=[pl.BlockSpec(block, index) for _, block, index in outs],
        out_shape=[shape for shape, _, _ in outs],
        compiler_params=pltpu.CompilerParams(vmem_limit_bytes=48 * 1024 * 1024),
        cost_estimate=work(2.5 * flops),
        name=name,
    )(*[array for array, _, _ in ins])


def whole_block(array):
    return (array, array.shape, lambda i: (0,) * array.ndim)


def column_block(array):
    return (array, (array.shape[0], TILE), lambda i: (0, i))


def row_block(array):
    return (array, (TILE, array.shape[1]), lambda i: (i, 0))


def gate_up_kernel(rows_ref, gate_w_ref, up_w_ref, gate_ref, up_ref, activated_ref):
    rows = rows_ref[...]
    gate = dot(rows, gate_w_ref[...], NN)
    up = dot(rows, up_w_ref[...], NN)
    gate_ref[...] = gate
    up_ref[...] = up
    activated_ref[...] = (gate * jax.nn.sigmoid(gate) * up).astype(LOW)


def gate_up_rows(rows, gate_weight, up_weight):
    count, hidden = rows.shape[0], gate_weight.shape[1]
    shapes = [jax.ShapeDtypeStruct((count, hidden), t) for t in (WIDE, WIDE, LOW)]
    return tiled(
        gate_up_kernel,
        "gate_up",
        pl.cdiv(hidden, TILE),
        [whole_block(rows), column_block(gate_weight), column_block(up_weight)],
        [column_block(s) for s in shapes],
        4 * rows.size * hidden,
    )


def back_sum(rows, weight_ref):
    width = weight_ref.shape[2]
    return total_of(
        dot(rows[:, r * width : (r + 1) * width], weight_ref[r], NT)
        for r in range(weight_ref.shape[0])
    )


def tall_block(array):
    return (array, (array.shape[0], TILE, array.shape[2]), lambda i: (0, i, 0))


def gate_up_back_kernel(rows_ref, weight_ref, gate_ref, up_ref, grad_gate_ref, grad_up_ref):
    grad = back_sum(rows_ref[...], weight_ref)
    gate, up = gate_ref[...], up_ref[...]
    s = jax.nn.sigmoid(gate)
    grad_gate_ref[...] = (grad * up * s * (1.0 + gate * (1.0 - s))).astype(LOW)
    grad_up_ref[...] = (grad * (gate * s)).astype(LOW)


def gate_up_back(rows, down_weight, gate, up):
    count, hidden = gate.shape
    shape = jax.ShapeDtypeStruct((count, hidden), LOW)
    return tiled(
        gate_up_back_kernel,
        "gate_up_back",
        pl.cdiv(hidden, TILE),
        [whole_block(rows), tall_block(down_weight), column_block(gate), column_block(up)],
        [column_block(shape)] * 2,
        2 * rows.size * hidden,
    )


def out_back_kernel(rows_ref, weight_ref, out_ref):
    out_ref[...] = back_sum(rows_ref[...], weight_ref).astype(LOW)


def out_back(rows, weight):
    shape = jax.ShapeDtypeStruct((rows.shape[0], weight.shape[1]), LOW)
    return tiled(
        out_back_kernel,
        "out_back",
        shape.shape[1] // TILE,
        [whole_block(rows), tall_block(weight)],
        [column_block(shape)],
        2 * rows.size * shape.shape[1],
    )[0]


def wide_kernel(rows_ref, weight_ref, out_ref):
    out_ref[...] = dot(rows_ref[...], weight_ref[0], NN).astype(LOW)


def times_wide(rows, weight, name):
    blocks, depth, width = weight.shape
    per = width // TILE
    shape = jax.ShapeDtypeStruct((rows.shape[0], blocks * width), LOW)
    return tiled(
        wide_kernel,
        name,
        blocks * per,
        [whole_block(rows), (weight, (1, depth, TILE), lambda i: (i // per, 0, i % per))],
        [column_block(shape)],
        2 * rows.size * blocks * width,
    )[0]


def gate_up_in_kernel(gate_ref, up_ref, gate_w_ref, up_w_ref, out_ref):
    total = dot(gate_ref[...], gate_w_ref[...], NT) + dot(up_ref[...], up_w_ref[...], NT)
    out_ref[...] = total.astype(LOW)


def gate_up_in(grad_gate, grad_up, gate_weight, up_weight):
    shape = jax.ShapeDtypeStruct((grad_gate.shape[0], gate_weight.shape[0]), LOW)
    return tiled(
        gate_up_in_kernel,
        "gate_up_in",
        shape.shape[1] // TILE,
        [whole_block(grad_gate), whole_block(grad_up), row_block(gate_weight), row_block(up_weight)],
        [column_block(shape)],
        4 * grad_gate.size * shape.shape[1],
    )[0]


def project_in_kernel(rows_ref, weight_ref, out_ref):
    width = weight_ref.shape[3]
    out_ref[...] = total_of(
        dot(rows_ref[:, c * width : (c + 1) * width], weight_ref[0, c], NT) for c in range(3)
    ).astype(LOW)


def project_in(rows, weight):
    blocks, three, depth, width = weight.shape
    per = depth // TILE
    shape = jax.ShapeDtypeStruct((rows.shape[0], blocks * depth), LOW)
    return tiled(
        project_in_kernel,
        "project_in",
        blocks * per,
        [whole_block(rows), (weight, (1, three, TILE, width), lambda i: (i // per, 0, i % per, 0))],
        [column_block(shape)],
        2 * rows.size * blocks * depth,
    )[0]


def outer_kernel(a_ref, b_ref, out_ref):
    out_ref[...] = dot(a_ref[...], b_ref[...], TN).astype(LOW)


def outer(a, b):
    shape = jax.ShapeDtypeStruct((a.shape[1], b.shape[1]), LOW)
    return tiled(
        outer_kernel,
        "outer",
        pl.cdiv(a.shape[1], TILE),
        [column_block(a), whole_block(b)],
        [row_block(shape)],
        a.size * b.shape[1] * 0.8,
    )[0]


def project_kernel(rows_ref, weight_ref, bias_ref, cos_ref, right_ref, left_ref, q_ref, kv_ref):
    blocks, _, depth, width = weight_ref.shape
    flat = dot(rows_ref[...], weight_ref[...].reshape(blocks * depth, width), NN) + bias_ref[0]
    step = pl.program_id(0)

    @pl.when(step == 0)
    def _():
        kv_ref[...] = rotated(flat, cos_ref, right_ref, left_ref).astype(LOW)

    @pl.when(step == 1)
    def _():
        kv_ref[...] = flat.astype(LOW)

    @pl.when(step == 2)
    def _():
        q_ref[...] = rotated(flat, cos_ref, right_ref, left_ref).astype(LOW)


def project(rows, weight, bias, tables):
    count = rows.shape[0]
    blocks, _, depth, width = weight.shape
    fixed = lambda i: (0, 0)
    shapes = [jax.ShapeDtypeStruct((k * count, width), LOW) for k in (1, 2)]
    return tiled(
        project_kernel,
        "project",
        3,
        [
            whole_block(rows),
            (weight, (blocks, 1, depth, width), lambda i: (0, (i + 1) % 3, 0, 0)),
            (bias[:, None, :], (1, 1, width), lambda i: ((i + 1) % 3, 0, 0)),
        ]
        + [(t, (count, PAIR), fixed) for t in tables],
        [
            (shapes[0], (count, width), fixed),
            (shapes[1], (count, width), lambda i: (jnp.minimum(i, 1), 0)),
        ],
        6 * rows.size * width,
    )


def project_back_kernel(far, dq_ref, dkv_ref, *refs):
    far_refs = refs[:far]
    cos_ref, right_ref, left_ref, out_ref, sum_ref = refs[far:]
    step = pl.program_id(0)

    def put(value):
        out_ref[...] = value.astype(LOW)
        sum_ref[0] = jnp.sum(value, axis=0, keepdims=True)

    def key_value():
        return total_of([dkv_ref[...]] + [r[...].astype(WIDE) for r in far_refs])

    @pl.when(step == 0)
    def _():
        put(rotated(dq_ref[...], cos_ref, right_ref, left_ref))

    @pl.when(step == 1)
    def _():
        put(rotated(key_value(), cos_ref, right_ref, left_ref))

    @pl.when(step == 2)
    def _():
        put(key_value())


def project_back(dq, dkv, far, tables):
    count, width = dq.shape
    fixed = lambda i: (0, 0)
    lower = pl.BlockSpec((count, width), lambda i: (jnp.maximum(i - 1, 0), 0))
    out, sums = pl.pallas_call(
        functools.partial(project_back_kernel, len(far)),
        grid=(3,),
        in_specs=[pl.BlockSpec((count, width), fixed)]
        + [lower] * (1 + len(far))
        + [pl.BlockSpec((count, PAIR), fixed)] * 3,
        out_specs=[
            pl.BlockSpec((count, width), lambda i: (0, i)),
            pl.BlockSpec((1, 1, width), lambda i: (i, 0, 0)),
        ],
        out_shape=[
            jax.ShapeDtypeStruct((count, 3 * width), LOW),
            jax.ShapeDtypeStruct((3, 1, width), WIDE),
        ],
        compiler_params=pltpu.CompilerParams(vmem_limit_bytes=32 * 1024 * 1024),
        cost_estimate=work(14000 * count * width),
        name="project_back",
    )(dq, dkv, *far, *tables)
    return out, sums[:, 0]


def attend_kernel(blocks, qpos_ref, kpos_ref, q_ref, *refs):
    keys, values = refs[: 2 * blocks : 2], refs[1 : 2 * blocks : 2]
    out_ref, lse_ref = refs[2 * blocks :]
    allowed = [kpos_ref[b] <= qpos_ref[...] for b in range(blocks)]
    for half in range(PAIR // HD):
        lanes = slice(half * HD, (half + 1) * HD)
        q = q_ref[:, lanes] * jnp.asarray(HD**-0.5, LOW)
        top, total, acc = None, None, None
        for b in range(blocks):
            s = jnp.where(allowed[b], dot(q, keys[b][:, lanes], NT), MASKED)
            block_top = jnp.max(s, axis=1, keepdims=True)
            new_top = block_top if b == 0 else jnp.maximum(top, block_top)
            p = jnp.exp(s - new_top)
            block_total = jnp.sum(p, axis=1, keepdims=True)
            block_acc = dot(p.astype(LOW), values[b][:, lanes], NN)
            if b == 0:
                total, acc = block_total, block_acc
            else:
                factor = jnp.exp(top - new_top)
                total = total * factor + block_total
                acc = acc * factor + block_acc
            top = new_top
        out_ref[:, lanes] = acc / total
        lse_ref[half] = top + jnp.log(total)


def attend(qpos, kpos, q, pairs_of_rows):
    rows, width = q.shape
    key_rows = pairs_of_rows[0].shape[0] // 2
    blocks = len(pairs_of_rows)
    pairs = width // PAIR
    per_pair = PAIR // HD
    column = lambda i: (0, i)
    fixed = lambda i: (0, 0)
    key_specs = [pl.BlockSpec((key_rows, PAIR), lambda i, c=c: (c, i)) for c in range(2)]
    stacked = [rows_of for rows_of in pairs_of_rows for c in range(2)]
    return pl.pallas_call(
        functools.partial(attend_kernel, blocks),
        grid=(pairs,),
        in_specs=[
            pl.BlockSpec((rows, 1), fixed),
            pl.BlockSpec((blocks, 1, key_rows), lambda i: (0, 0, 0)),
            pl.BlockSpec((rows, PAIR), column),
        ]
        + key_specs * blocks,
        out_specs=[
            pl.BlockSpec((rows, PAIR), column),
            pl.BlockSpec((per_pair, rows, 1), lambda i: (i, 0, 0)),
        ],
        out_shape=[
            jax.ShapeDtypeStruct((rows, width), WIDE),
            jax.ShapeDtypeStruct((width // HD, rows, 1), WIDE),
        ],
        compiler_params=pltpu.CompilerParams(vmem_limit_bytes=32 * 1024 * 1024),
        cost_estimate=work(43 * rows * key_rows * blocks * width),
        name="attend",
    )(qpos, kpos, q, *stacked)


def attend_back_kernel(blocks, qpos_ref, kpos_ref, q_ref, grad_ref, out_ref, lse_ref, *refs):
    keys, values = refs[: 2 * blocks : 2], refs[1 : 2 * blocks : 2]
    dq_ref = refs[2 * blocks]
    dboth = refs[2 * blocks + 1 :]
    key_rows = keys[0].shape[0]
    allowed = [kpos_ref[b] <= qpos_ref[...] for b in range(blocks)]
    scale = HD**-0.5
    for half in range(PAIR // HD):
        lanes = slice(half * HD, (half + 1) * HD)
        q = q_ref[:, lanes] * jnp.asarray(scale, LOW)
        grad = grad_ref[:, lanes]
        lse = lse_ref[half]
        delta = jnp.sum(grad.astype(WIDE) * out_ref[:, lanes], axis=1, keepdims=True)
        dq = None
        for b in range(blocks):
            k = keys[b][:, lanes]
            s = jnp.where(allowed[b], dot(q, k, NT), MASKED)
            p = jnp.exp(s - lse)
            dp = dot(grad, values[b][:, lanes], NT)
            ds = (p * (dp - delta)).astype(LOW)
            kind = dboth[b].dtype
            dboth[b][key_rows:, lanes] = dot(p.astype(LOW), grad, TN).astype(kind)
            dboth[b][:key_rows, lanes] = dot(ds, q, TN).astype(kind)
            term = dot(ds, k, NN)
            dq = term if b == 0 else dq + term
        dq_ref[:, lanes] = dq * scale


def attend_back(qpos, kpos, q, grad, out, lse, pairs_of_rows):
    rows, width = q.shape
    key_rows = pairs_of_rows[0].shape[0] // 2
    blocks = len(pairs_of_rows)
    pairs = width // PAIR
    per_pair = PAIR // HD
    column = lambda i: (0, i)
    fixed = lambda i: (0, 0)
    row_spec = pl.BlockSpec((rows, PAIR), column)
    key_specs = [pl.BlockSpec((key_rows, PAIR), lambda i, c=c: (c, i)) for c in range(2)]
    stacked = [rows_of for rows_of in pairs_of_rows for c in range(2)]
    far = [jax.ShapeDtypeStruct((2 * key_rows, width), LOW)] * (blocks - 1)
    near = [jax.ShapeDtypeStruct((2 * key_rows, width), WIDE)]
    results = pl.pallas_call(
        functools.partial(attend_back_kernel, blocks),
        grid=(pairs,),
        in_specs=[
            pl.BlockSpec((rows, 1), fixed),
            pl.BlockSpec((blocks, 1, key_rows), lambda i: (0, 0, 0)),
            row_spec,
            row_spec,
            row_spec,
            pl.BlockSpec((per_pair, rows, 1), lambda i: (i, 0, 0)),
        ]
        + key_specs * blocks,
        out_specs=[row_spec] + [pl.BlockSpec((2 * key_rows, PAIR), column)] * blocks,
        out_shape=[jax.ShapeDtypeStruct((rows, width), WIDE)] + near + far,
        compiler_params=pltpu.CompilerParams(vmem_limit_bytes=40 * 1024 * 1024),
        cost_estimate=work(75 * rows * key_rows * blocks * width),
        name="attend_back",
    )(qpos, kpos, q, grad, out, lse, *stacked)
    return results[0], results[1], results[2:]


def finish(buffer, layer, terms, make, steps, ins, out, name):
    shape, block, place = out

    def kernel(*refs):
        refs[-1][...] = make(*[r[...].astype(WIDE) for r in refs[: len(terms)]])

    operands = list(terms)
    specs = [pl.BlockSpec(b, index) for b, index in ins]
    if buffer is not None:
        operands.append(buffer)
        specs.append(pl.BlockSpec(memory_space=pl.ANY))
    return pl.pallas_call(
        kernel,
        grid=(steps,),
        in_specs=specs,
        out_specs=pl.BlockSpec((1,) + block, lambda i: (layer,) + place(i)),
        out_shape=jax.ShapeDtypeStruct(shape, WIDE),
        input_output_aliases={} if buffer is None else {len(terms): 0},
        compiler_params=pltpu.CompilerParams(vmem_limit_bytes=48 * 1024 * 1024),
        cost_estimate=work(1e9),
        name=name,
    )(*operands)


def finish_matrix(buffer, layer, terms, name):
    rows, columns = terms[0].shape
    block = (rows // 4, columns)
    place = lambda i: (i, 0)
    out = ((LAYERS, rows, columns), block, place)
    make = lambda *t: total_of(t)[None]
    return finish(buffer, layer, terms, make, 4, [(block, place)] * len(terms), out, name)


def finish_projections(buffer, layer, terms):
    rows, columns = terms[0].shape
    width = columns // 3
    out = ((LAYERS, 3, rows, width), (1, rows, width), lambda i: (i, 0, 0))
    make = lambda *t: total_of(t)[None, None]
    ins = [((rows, width), lambda i: (0, i))] * len(terms)
    return finish(buffer, layer, terms, make, 3, ins, out, "finish_qkv")


def finish_gate_up(buffer, layer, gate_terms, up_terms):
    rows, columns = gate_terms[0].shape
    steps = 8
    block = (rows // steps, columns)
    out = ((LAYERS, rows, 2, columns), (rows // steps, 2, columns), lambda i: (i, 0, 0))
    count = len(gate_terms)
    make = lambda *t: jnp.stack([total_of(t[:count]), total_of(t[count:])], axis=1)[None]
    ins = [(block, lambda i: (i, 0))] * (2 * count)
    return finish(buffer, layer, gate_terms + up_terms, make, steps, ins, out, "finish_gate_up")


def bits_of(count):
    return [1 << k for k in range(count.bit_length() - 1)]


def swapped(value, axis, mask):
    count = lax.axis_size(axis)
    return lax.ppermute(value, axis, [(i, i ^ mask) for i in range(count)])


def joined(pieces, axis):
    return pieces[0] if len(pieces) == 1 else jnp.concatenate(pieces, axis=axis)


class Line:
    def __init__(self, own_rows):
        n_tensor, n_ctx = lax.axis_size("tensor"), lax.axis_size("ctx")
        tensor, ctx = lax.axis_index("tensor"), lax.axis_index("ctx")
        self.count, self.tensor = n_tensor, tensor
        row = jnp.arange(own_rows, dtype=jnp.int32)
        chip = (tensor + jnp.arange(n_tensor, dtype=jnp.int32)) % n_tensor
        place = (chip[:, None] * own_rows + row[None, :]).reshape(-1)
        block = n_tensor * own_rows
        self.places = ctx * block + place
        self.key_places = [self.places] + [
            jnp.where(ctx >= s, (ctx - s) * block + place, 1 << 30) for s in range(1, n_ctx)
        ]
        self.own_rows = own_rows

    def gather_rows(self, low):
        count, t = self.count, self.tensor
        send = lambda v, *route: lax.ppermute(v, "tensor", list(route))
        if count == 4:
            far = send(low, (0, 2), (2, 0), (1, 3), (3, 1))
            above = send(low, (0, 1), (1, 2), (2, 3))
            below = send(low, (1, 0), (2, 1), (3, 2))
            end = send(far, (2, 3), (1, 0))
            found = [low, jnp.where(t == 3, end, below), far, jnp.where(t == 0, end, above)]
        else:
            found = [low] + [
                send(low, *[((i + d) % count, i) for i in range(count)]) for d in range(1, count)
            ]
        return jnp.concatenate(found, axis=0)

    def sum_rows(self, low):
        rows, count, t = self.own_rows, self.count, self.tensor
        terms = [low[d * rows : (d + 1) * rows] for d in range(count)]
        send = lambda v, *route: lax.ppermute(v, "tensor", list(route))
        wide = lambda v: v.astype(WIDE)
        if count == 4:
            end = send(jnp.where(t == 0, terms[3], terms[1]), (0, 1), (3, 2))
            above = send(terms[1], (0, 1), (1, 2), (2, 3))
            below = send(terms[3], (3, 2), (2, 1), (1, 0))
            far = (wide(terms[2]) + wide(end)).astype(LOW)
            got = [send(far, (0, 2), (2, 0), (1, 3), (3, 1)), above, below]
        else:
            got = [
                send(terms[d], *[(i, (i + d) % count) for i in range(count)])
                for d in range(1, count)
            ]
        return total_of([wide(terms[0])] + [wide(g) for g in got])

    def owner(self, low):
        count = lax.axis_size("ctx")
        if count != 2:
            return (lax.psum(low, "ctx") if count > 1 else low,)
        got = yield swapped(low, "ctx", 1)
        return (low, got)

    def far_keys(self, value):
        count = lax.axis_size("ctx")
        return [
            lax.ppermute(value, "ctx", [(i, i + s) for i in range(count - s)])
            for s in range(1, count)
        ]

    def far_key_grads(self, values):
        count = lax.axis_size("ctx")
        return [
            lax.ppermute(values[s - 1], "ctx", [(i + s, i) for i in range(count - s)])
            for s in range(1, count)
        ]


def weight_stages(shard):
    shard = yield shard
    return (yield lax.all_gather(shard, "dp"))


def grad_stages(plan, value, axis):
    got = yield lax.psum_scatter(value.astype(LOW), "dp", scatter_dimension=axis, tiled=True)
    return (yield from plan.owner(got))


def low_first(count):
    width = count.bit_length() - 1
    return sorted(range(count), key=lambda r: int(format(r, "b").zfill(width)[::-1] or "0", 2))


def pair_stages(plan, terms_of, axis):
    count = lax.axis_size("dp")

    def term(parts):
        factors = [terms_of(r) for r in parts]
        a = joined([f[0] for f in factors], 1) if axis == 0 else factors[0][0]
        b = joined([f[1] for f in factors], 1) if axis == 1 else factors[0][1]
        return outer(a, b)

    order = low_first(count)
    kept = None
    for bit in bits_of(count):
        if kept is None:
            sent = yield term(order[count // 2 :])
        else:
            kept, sent = jnp.split(kept, 2, axis=axis)
        got = yield swapped(sent.astype(LOW), "dp", bit)
        kept = (term(order[: count // 2]).astype(WIDE) if kept is None else kept) + got.astype(WIDE)
    return (yield from plan.owner(kept.astype(LOW)))


class Job:
    def __init__(self, stages):
        self.stages, self.value, self.result, self.done = stages, None, None, False
        self.advance(None)

    def advance(self, value):
        try:
            self.value = self.stages.send(value)
        except StopIteration as end:
            self.done, self.result, self.value = True, end.value, None

    def finish(self):
        while not self.done:
            self.advance(self.value)
        return self.result


def meanwhile(value, *jobs):
    open_jobs = [j for j in jobs if j is not None and not j.done]
    if not open_jobs:
        return value
    value, held = lax.optimization_barrier((value, tuple(j.value for j in open_jobs)))
    for job, got in zip(open_jobs, held):
        job.advance(got)
    return value


def held(value, *jobs):
    open_jobs = [j for j in jobs if j is not None and not j.done]
    if not open_jobs:
        return value
    value, kept = lax.optimization_barrier((value, tuple(j.value for j in open_jobs)))
    for job, got in zip(open_jobs, kept):
        job.value = got
    return value


def shards(
    tokens,
    cotangent,
    norm_gains,
    norm_biases,
    qkv_weight,
    qkv_bias,
    out_weight,
    gate_up_weight,
    down_weight,
):
    own_rows = tokens.shape[1]
    model = tokens.shape[2]
    heads_width = qkv_weight.shape[3]
    plan = Line(own_rows)
    tables = rotary_tables(plan.places)
    tables_back = (tables[0], -tables[1], -tables[2])
    qpos = plan.places[:, None]
    kpos = jnp.stack(plan.key_places)[:, None, :]
    gains = (norm_gains)
    biases = (norm_biases)
    qkv_bias_own = lax.dynamic_slice_in_dim(qkv_bias, lax.axis_index("tensor") * heads_width, heads_width, 2)

    def weight_jobs(layer, after):
        (qkv_all, out_all, gate_up_all, down_all), after = lax.optimization_barrier(
            ((qkv_weight, out_weight, gate_up_weight, down_weight), after)
        )
        matrices = {
            "qkv": jnp.transpose(qkv_all[layer], (1, 0, 2)),
            "out": out_all[layer],
            "gate": gate_up_all[layer, :, 0],
            "up": gate_up_all[layer, :, 1],
            "down": down_all[layer],
        }
        return {n: Job(weight_stages(v)) for n, v in matrices.items()}, after

    now, unused = weight_jobs(0, ())
    for name in ("qkv", "out", "gate", "up"):
        now[name].advance(now[name].value)
    stream = tokens[0].astype(WIDE)
    later = {}
    saved = []
    for layer in range(LAYERS):
        last = layer + 1 == LAYERS
        normed_one, unit_one, inverse_one = layer_norm_rows(
            stream, gains[layer, 0], biases[layer, 0]
        )
        rows_one = plan.gather_rows(normed_one.astype(LOW))
        if layer == 0:
            rows_one = meanwhile(rows_one, now["qkv"], now["down"])
        else:
            rows_one = meanwhile(rows_one, now["out"], now["gate"], now["down"])
        qkv_full = now["qkv"].finish()
        queries, keys_values = project(rows_one, qkv_full, qkv_bias_own[layer], tables)
        if layer == 0:
            late_cotangent, queries = lax.optimization_barrier((cotangent[0], queries))
            grad_stream = late_cotangent.astype(WIDE)
            branch = plan.gather_rows(late_cotangent)
        all_kv = [keys_values] + plan.far_keys(keys_values)
        attended, lse = attend(qpos, kpos, queries, all_kv)
        attended_low = meanwhile(attended.astype(LOW), now["out"])
        if layer == 0:
            attended_low, branch = lax.optimization_barrier((attended_low, branch))
        else:
            attended_low = meanwhile(attended_low, now["up"])
        out_full = now["out"].finish()
        mid = stream + plan.sum_rows(times_wide(attended_low, out_full, "out"))
        mid = meanwhile(mid, now["gate"], now["up"])
        if layer > 0:
            mid = meanwhile(mid, now["down"])
        else:
            later, mid = weight_jobs(layer + 1, mid)
        normed_two, unit_two, inverse_two = layer_norm_rows(mid, gains[layer, 1], biases[layer, 1])
        rows_two = plan.gather_rows(normed_two.astype(LOW))
        rows_two = meanwhile(rows_two, now["down"], later.get("qkv"))
        flat = lambda v: v.reshape(v.shape[0] * v.shape[1], v.shape[2])
        gate_full, up_full = flat(now["gate"].finish()), flat(now["up"].finish())
        gate, up, activated = gate_up_rows(rows_two, gate_full, up_full)
        activated = meanwhile(activated, later.get("out"), later.get("gate"))
        down_full = now["down"].finish()
        if not last:
            stream = mid + plan.sum_rows(times_wide(activated, down_full, "down"))
            stream = meanwhile(stream, later.get("qkv"), later.get("up"))
        saved.append(
            (
                (qkv_full, out_full, gate_full, up_full, down_full),
                (rows_one, unit_one, inverse_one),
                (queries, all_kv, attended, attended_low, lse),
                (rows_two, unit_two, inverse_two),
                (gate, up, activated),
            )
        )
        now = later
    grad_jobs = [None] * LAYERS
    gain_grads = [None] * LAYERS
    bias_grads = [None] * LAYERS
    qkv_bias_grads = [None] * LAYERS
    for layer in range(LAYERS - 1, -1, -1):
        (
            (qkv_full, out_full, gate_full, up_full, down_full),
            (rows_one, unit_one, inverse_one),
            (queries, all_kv, attended, attended_low, lse),
            (rows_two, unit_two, inverse_two),
            (gate, up, activated),
        ) = saved[layer]
        mine = {}
        grad_jobs[layer] = mine
        above = grad_jobs[layer + 1] if layer + 1 < LAYERS else {}
        old = lambda *keys: [above.get(k) for k in keys]

        def own_part(value, r):
            index = lax.axis_index("dp") ^ r
            width = value.shape[1] // lax.axis_size("dp")
            return lax.dynamic_slice_in_dim(value, index * width, width, 1)

        def in_job(a, b):
            return Job(grad_stages(plan, outer(a, b), 0))

        def out_job(a, b):
            return Job(grad_stages(plan, outer(a, b), 1))

        if layer + 1 < LAYERS:
            branch = plan.gather_rows(grad_stream.astype(LOW))
        branch = meanwhile(branch, *old("gate", "up", "out"))
        if layer == 0:
            down_grad, branch = lax.optimization_barrier(
                (outer(activated, branch), branch)
            )
            mine["down"] = Job(grad_stages(plan, down_grad, 1))
        grad_gate, grad_up = gate_up_back(branch, down_full, gate, up)
        partial_in = gate_up_in(grad_gate, grad_up, gate_full, up_full)
        summed = plan.sum_rows(partial_in)
        if layer > 0:
            summed, (branch, grad_gate, grad_up) = lax.optimization_barrier(
                (summed, (branch, grad_gate, grad_up))
            )
        if layer > 0:
            mine["down"] = out_job(activated, branch)
        mine["gate"] = in_job(rows_two, grad_gate)
        mine["up"] = in_job(rows_two, grad_up)
        grad_mid, gain_two, bias_two = norm_backward(
            summed, unit_two, inverse_two, gains[layer, 1]
        )
        hidden_grad = grad_stream + grad_mid
        hidden_grad = meanwhile(hidden_grad, *old("up", "out", "qkv"))
        top = layer + 1 == LAYERS
        if top:
            late, hidden_grad = lax.optimization_barrier((activated, hidden_grad))
            partial_out = times_wide(late, down_full, "down")
        attention = plan.gather_rows(hidden_grad.astype(LOW))
        attention = meanwhile(attention, *old("qkv"))
        if layer == 0:
            attention = meanwhile(attention, mine["down"])
        if top:
            attention, partial_out = lax.optimization_barrier((attention, partial_out))
            output = (mid + plan.sum_rows(partial_out)).astype(LOW)[None]
        grad_attended = out_back(attention, out_full)
        grad_queries, grad_kv, far_grads = attend_back(
            qpos, kpos, queries, grad_attended, attended, lse, all_kv
        )
        grad_queries, attention = lax.optimization_barrier((grad_queries, attention))
        if layer == 0:
            mine["out"] = Job(
                pair_stages(plan, lambda r, a=attention: (attended_low, own_part(a, r)), 1)
            )
        else:
            mine["out"] = out_job(attended_low, attention)
        projected, qkv_bias_grads[layer] = project_back(
            grad_queries, grad_kv, plan.far_key_grads(far_grads), tables_back
        )
        projected = meanwhile(projected, mine["down"], *old("qkv"))
        if not top:
            above_done, projected = lax.optimization_barrier(
                ({k: j.finish() for k, j in above.items()}, projected)
            )
            sums = above_done
            results = [
                finish_projections(None, layer + 1, sums["qkv"]),
                finish_matrix(None, layer + 1, sums["out"], "finish_out"),
                finish_gate_up(None, layer + 1, sums["gate"], sums["up"]),
                finish_matrix(None, layer + 1, sums["down"], "finish_down"),
            ]
        if layer == 0:
            mine["qkv"] = Job(
                pair_stages(plan, lambda r, b=projected: (own_part(rows_one, r), b), 0)
            )
            projected = meanwhile(projected, *map(mine.get, ("qkv", "out", "gate")))
        partial_in = project_in(projected, qkv_full)
        if top:
            partial_in, output = lax.optimization_barrier((partial_in, output))
        if layer == 0:
            partial_in = meanwhile(partial_in, *map(mine.get, ("up", "out", "qkv")))
        summed = plan.sum_rows(partial_in)
        if layer > 0:
            summed, projected = lax.optimization_barrier((summed, projected))
            mine["qkv"] = in_job(rows_one, projected)
        else:
            summed, results = lax.optimization_barrier((summed, results))
        grad_first, gain_one, bias_one = norm_backward(
            summed, unit_one, inverse_one, gains[layer, 0]
        )
        grad_stream = hidden_grad + grad_first
        if layer > 0:
            grad_stream = meanwhile(grad_stream, mine["down"], mine["gate"])
        else:
            grad_stream = meanwhile(grad_stream, *map(mine.get, ("gate", "up", "out", "qkv")))
        gain_grads[layer] = jnp.stack([gain_one, gain_two])
        bias_grads[layer] = jnp.stack([bias_one, bias_two])

    tokens_grad = (grad_stream).astype(LOW)[None]
    padded_bias = lax.dynamic_update_slice_in_dim(
        jnp.zeros((LAYERS, 3, qkv_bias.shape[2]), WIDE),
        jnp.stack(qkv_bias_grads),
        lax.axis_index("tensor") * heads_width,
        2,
    )
    small = jnp.concatenate(
        [
            (jnp.stack(gain_grads)).reshape(LAYERS * 2, model),
            (jnp.stack(bias_grads)).reshape(LAYERS * 2, model),
            padded_bias.reshape(LAYERS * 3, qkv_bias.shape[2]),
        ],
        axis=0,
    )
    for axis in ("ctx", "dp", "tensor"):
        for bit in bits_of(lax.axis_size(axis)):
            small = small + swapped(small, axis, bit)
    sums = {k: j.finish() for k, j in grad_jobs[0].items()}
    results = [
        finish_projections(results[0], 0, sums["qkv"]),
        finish_matrix(results[1], 0, sums["out"], "finish_out"),
        finish_gate_up(results[2], 0, sums["gate"], sums["up"]),
        finish_matrix(results[3], 0, sums["down"], "finish_down"),
    ]
    return (
        output,
        tokens_grad,
        small[: LAYERS * 2].reshape(LAYERS, 2, model),
        small[LAYERS * 2 : LAYERS * 4].reshape(LAYERS, 2, model),
        jnp.transpose(results[0], (0, 2, 1, 3)),
        small[LAYERS * 4 :].reshape(LAYERS, 3, qkv_bias.shape[2]),
        *results[1:],
    )


def solution(mesh):
    rows = P("dp", ("ctx", "tensor"), None)
    wide = P(None, "dp", None, "tensor")
    tall = P(None, "tensor", "dp")
    return jax.shard_map(
        shards,
        mesh=mesh,
        in_specs=(rows, rows, P(), P(), wide, P(), tall, wide, tall),
        out_specs=(rows, rows, P(), P(), wide, P(), tall, wide, tall),
        check_vma=False,
    )
```

```python
import functools

import jax
import jax.numpy as jnp
from jax import lax
from jax.experimental import pallas as pl
from jax.experimental.pallas import tpu as pltpu
from jax.sharding import PartitionSpec as P

HD = 64
ROT = 16
LAYERS = 2

MASKED = -1e30
EPSILON = 1e-05
LOW = jnp.bfloat16
WIDE = jnp.float32


def layer_norm_rows(stream, gain, bias):
    row_mean = jnp.mean(stream, axis=-1, keepdims=True)
    centered = stream - row_mean
    inverse = lax.rsqrt(jnp.mean(centered * centered, axis=-1, keepdims=True) + EPSILON)
    unit_rows = centered * inverse
    return (unit_rows * gain + bias, unit_rows, inverse)


def rotary_tables(positions):
    half_rot = ROT // 2
    frequency = 10000.0 ** (-(jnp.arange(half_rot, dtype=jnp.float32) * 2.0) / ROT)
    angles = positions.astype(jnp.float32)[:, None] * frequency[None, :]
    cosine, sine = jnp.cos(angles), jnp.sin(angles)
    rest = jnp.zeros((angles.shape[0], HD - ROT), WIDE)
    none = jnp.zeros_like(sine)
    heads = lambda *parts: jnp.tile(jnp.concatenate(parts, axis=1), (1, PAIR // HD))
    return (
        heads(cosine, cosine, rest + 1.0),
        heads(-sine, none, rest),
        heads(none, sine, rest),
    )


def rotated(flat, cos_ref, right_ref, left_ref):
    shift = ROT // 2
    found = []
    for start in range(0, flat.shape[1], PAIR):
        v = flat[:, start : start + PAIR]
        right, left = pltpu.roll(v, PAIR - shift, 1), pltpu.roll(v, shift, 1)
        found.append(v * cos_ref[...] + right * right_ref[...] + left * left_ref[...])
    return jnp.concatenate(found, axis=1)


def dot(a, b, dims):
    return lax.dot_general(a, b, (dims, ((), ())), preferred_element_type=WIDE)


PAIR = 128


NN = ((1,), (0,))
NT = ((1,), (1,))
TN = ((0,), (0,))


def total_of(terms):
    return functools.reduce(lambda a, b: a + b, terms)


def work(flops):
    return pl.CostEstimate(flops=int(flops), bytes_accessed=0, transcendentals=0)


TILE = 512


def tiled(kernel, name, steps, ins, outs, flops):
    return pl.pallas_call(
        kernel,
        grid=(steps,),
        in_specs=[pl.BlockSpec(block, index) for _, block, index in ins],
        out_specs=[pl.BlockSpec(block, index) for _, block, index in outs],
        out_shape=[shape for shape, _, _ in outs],
        compiler_params=pltpu.CompilerParams(vmem_limit_bytes=48 * 1024 * 1024),
        cost_estimate=work(2.5 * flops),
        name=name,
    )(*[array for array, _, _ in ins])


def whole_block(array):
    return (array, array.shape, lambda i: (0,) * array.ndim)


def column_block(array):
    return (array, (array.shape[0], TILE), lambda i: (0, i))


def row_block(array):
    return (array, (TILE, array.shape[1]), lambda i: (i, 0))


def gate_up_kernel(rows_ref, gate_w_ref, up_w_ref, gate_ref, up_ref, activated_ref):
    rows = rows_ref[...]
    gate = dot(rows, gate_w_ref[...], NN)
    up = dot(rows, up_w_ref[...], NN)
    gate_ref[...] = gate
    up_ref[...] = up
    activated_ref[...] = (gate * jax.nn.sigmoid(gate) * up).astype(LOW)


def gate_up_rows(rows, gate_weight, up_weight):
    count, hidden = rows.shape[0], gate_weight.shape[1]
    shapes = [jax.ShapeDtypeStruct((count, hidden), t) for t in (WIDE, WIDE, LOW)]
    return tiled(
        gate_up_kernel,
        "gate_up",
        pl.cdiv(hidden, TILE),
        [whole_block(rows), column_block(gate_weight), column_block(up_weight)],
        [column_block(s) for s in shapes],
        4 * rows.size * hidden,
    )


def back_sum(rows, weight_ref):
    width = weight_ref.shape[2]
    return total_of(
        dot(rows[:, r * width : (r + 1) * width], weight_ref[r], NT)
        for r in range(weight_ref.shape[0])
    )


def tall_block(array):
    return (array, (array.shape[0], TILE, array.shape[2]), lambda i: (0, i, 0))


def gate_up_back_kernel(rows_ref, weight_ref, gate_ref, up_ref, grad_gate_ref, grad_up_ref):
    grad = back_sum(rows_ref[...], weight_ref)
    gate, up = gate_ref[...], up_ref[...]
    s = jax.nn.sigmoid(gate)
    grad_gate_ref[...] = (grad * up * s * (1.0 + gate * (1.0 - s))).astype(LOW)
    grad_up_ref[...] = (grad * (gate * s)).astype(LOW)


def gate_up_back(rows, down_weight, gate, up):
    count, hidden = gate.shape
    shape = jax.ShapeDtypeStruct((count, hidden), LOW)
    return tiled(
        gate_up_back_kernel,
        "gate_up_back",
        pl.cdiv(hidden, TILE),
        [whole_block(rows), tall_block(down_weight), column_block(gate), column_block(up)],
        [column_block(shape)] * 2,
        2 * rows.size * hidden,
    )


def out_back_kernel(rows_ref, weight_ref, out_ref):
    out_ref[...] = back_sum(rows_ref[...], weight_ref).astype(LOW)


def out_back(rows, weight):
    shape = jax.ShapeDtypeStruct((rows.shape[0], weight.shape[1]), LOW)
    return tiled(
        out_back_kernel,
        "out_back",
        shape.shape[1] // TILE,
        [whole_block(rows), tall_block(weight)],
        [column_block(shape)],
        2 * rows.size * shape.shape[1],
    )[0]


def wide_kernel(rows_ref, weight_ref, out_ref):
    out_ref[...] = dot(rows_ref[...], weight_ref[0], NN).astype(LOW)


def times_wide(rows, weight, name):
    blocks, depth, width = weight.shape
    per = width // TILE
    shape = jax.ShapeDtypeStruct((rows.shape[0], blocks * width), LOW)
    return tiled(
        wide_kernel,
        name,
        blocks * per,
        [whole_block(rows), (weight, (1, depth, TILE), lambda i: (i // per, 0, i % per))],
        [column_block(shape)],
        2 * rows.size * blocks * width,
    )[0]


def gate_up_in_kernel(gate_ref, up_ref, gate_w_ref, up_w_ref, out_ref):
    total = dot(gate_ref[...], gate_w_ref[...], NT) + dot(up_ref[...], up_w_ref[...], NT)
    out_ref[...] = total.astype(LOW)


def gate_up_in(grad_gate, grad_up, gate_weight, up_weight):
    shape = jax.ShapeDtypeStruct((grad_gate.shape[0], gate_weight.shape[0]), LOW)
    return tiled(
        gate_up_in_kernel,
        "gate_up_in",
        shape.shape[1] // TILE,
        [whole_block(grad_gate), whole_block(grad_up), row_block(gate_weight), row_block(up_weight)],
        [column_block(shape)],
        4 * grad_gate.size * shape.shape[1],
    )[0]


def project_in_kernel(rows_ref, weight_ref, out_ref):
    width = weight_ref.shape[3]
    out_ref[...] = total_of(
        dot(rows_ref[:, c * width : (c + 1) * width], weight_ref[0, c], NT) for c in range(3)
    ).astype(LOW)


def project_in(rows, weight):
    blocks, three, depth, width = weight.shape
    per = depth // TILE
    shape = jax.ShapeDtypeStruct((rows.shape[0], blocks * depth), LOW)
    return tiled(
        project_in_kernel,
        "project_in",
        blocks * per,
        [whole_block(rows), (weight, (1, three, TILE, width), lambda i: (i // per, 0, i % per, 0))],
        [column_block(shape)],
        2 * rows.size * blocks * depth,
    )[0]


def outer_kernel(a_ref, b_ref, out_ref):
    out_ref[...] = dot(a_ref[...], b_ref[...], TN).astype(LOW)


def outer(a, b):
    shape = jax.ShapeDtypeStruct((a.shape[1], b.shape[1]), LOW)
    return tiled(
        outer_kernel,
        "outer",
        pl.cdiv(a.shape[1], TILE),
        [column_block(a), whole_block(b)],
        [row_block(shape)],
        a.size * b.shape[1] * 0.8,
    )[0]


def project_kernel(rows_ref, weight_ref, bias_ref, cos_ref, right_ref, left_ref, q_ref, kv_ref):
    blocks, _, depth, width = weight_ref.shape
    flat = dot(rows_ref[...], weight_ref[...].reshape(blocks * depth, width), NN) + bias_ref[0]
    step = pl.program_id(0)

    @pl.when(step == 0)
    def _():
        kv_ref[...] = rotated(flat, cos_ref, right_ref, left_ref).astype(LOW)

    @pl.when(step == 1)
    def _():
        kv_ref[...] = flat.astype(LOW)

    @pl.when(step == 2)
    def _():
        q_ref[...] = rotated(flat, cos_ref, right_ref, left_ref).astype(LOW)


def project(rows, weight, bias, tables):
    count = rows.shape[0]
    blocks, _, depth, width = weight.shape
    fixed = lambda i: (0, 0)
    shapes = [jax.ShapeDtypeStruct((k * count, width), LOW) for k in (1, 2)]
    return tiled(
        project_kernel,
        "project",
        3,
        [
            whole_block(rows),
            (weight, (blocks, 1, depth, width), lambda i: (0, (i + 1) % 3, 0, 0)),
            (bias[:, None, :], (1, 1, width), lambda i: ((i + 1) % 3, 0, 0)),
        ]
        + [(t, (count, PAIR), fixed) for t in tables],
        [
            (shapes[0], (count, width), fixed),
            (shapes[1], (count, width), lambda i: (jnp.minimum(i, 1), 0)),
        ],
        6 * rows.size * width,
    )


def project_back_kernel(far, dq_ref, dkv_ref, *refs):
    far_refs = refs[:far]
    cos_ref, right_ref, left_ref, out_ref, sum_ref = refs[far:]
    step = pl.program_id(0)

    def put(value):
        out_ref[...] = value.astype(LOW)
        sum_ref[0] = jnp.sum(value, axis=0, keepdims=True)

    def key_value():
        return total_of([dkv_ref[...]] + [r[...].astype(WIDE) for r in far_refs])

    @pl.when(step == 0)
    def _():
        put(rotated(dq_ref[...], cos_ref, right_ref, left_ref))

    @pl.when(step == 1)
    def _():
        put(rotated(key_value(), cos_ref, right_ref, left_ref))

    @pl.when(step == 2)
    def _():
        put(key_value())


def project_back(dq, dkv, far, tables):
    count, width = dq.shape
    fixed = lambda i: (0, 0)
    lower = pl.BlockSpec((count, width), lambda i: (jnp.maximum(i - 1, 0), 0))
    out, sums = pl.pallas_call(
        functools.partial(project_back_kernel, len(far)),
        grid=(3,),
        in_specs=[pl.BlockSpec((count, width), fixed)]
        + [lower] * (1 + len(far))
        + [pl.BlockSpec((count, PAIR), fixed)] * 3,
        out_specs=[
            pl.BlockSpec((count, width), lambda i: (0, i)),
            pl.BlockSpec((1, 1, width), lambda i: (i, 0, 0)),
        ],
        out_shape=[
            jax.ShapeDtypeStruct((count, 3 * width), LOW),
            jax.ShapeDtypeStruct((3, 1, width), WIDE),
        ],
        compiler_params=pltpu.CompilerParams(vmem_limit_bytes=32 * 1024 * 1024),
        cost_estimate=work(14000 * count * width),
        name="project_back",
    )(dq, dkv, *far, *tables)
    return out, sums[:, 0]


def attend_kernel(blocks, ctx_ref, qpos_ref, kpos_ref, q_ref, *refs):
    keys, values = refs[: 2 * blocks : 2], refs[1 : 2 * blocks : 2]
    out_ref, lse_ref, acc_ref, top_ref, total_ref = refs[2 * blocks :]
    allowed = kpos_ref[...] <= qpos_ref[...]
    for half in range(PAIR // HD):
        lanes = slice(half * HD, (half + 1) * HD)
        q = q_ref[:, lanes] * jnp.asarray(HD**-0.5, LOW)
        s = jnp.where(allowed, dot(q, keys[0][:, lanes], NT), MASKED)
        top = jnp.max(s, axis=1, keepdims=True)
        p = jnp.exp(s - top)
        top_ref[half] = top
        total_ref[half] = jnp.sum(p, axis=1, keepdims=True)
        acc_ref[half] = dot(p.astype(LOW), values[0][:, lanes], NN)
        for b in range(1, blocks):

            @pl.when(ctx_ref[0] >= b)
            def _():
                s = dot(q, keys[b][:, lanes], NT)
                top = top_ref[half]
                new_top = jnp.maximum(top, jnp.max(s, axis=1, keepdims=True))
                p = jnp.exp(s - new_top)
                factor = jnp.exp(top - new_top)
                top_ref[half] = new_top
                total_ref[half] = total_ref[half] * factor + jnp.sum(p, axis=1, keepdims=True)
                acc_ref[half] = acc_ref[half] * factor + dot(
                    p.astype(LOW), values[b][:, lanes], NN
                )

        out_ref[:, lanes] = acc_ref[half] / total_ref[half]
        lse_ref[half] = top_ref[half] + jnp.log(total_ref[half])


def attention_specs(rows, key_rows, blocks):
    column = lambda i: (0, i)
    fixed = lambda i: (0, 0)
    common = [
        pl.BlockSpec(memory_space=pltpu.SMEM),
        pl.BlockSpec((rows, 1), fixed),
        pl.BlockSpec((1, key_rows), fixed),
    ]
    row = pl.BlockSpec((rows, PAIR), column)
    lse = pl.BlockSpec((PAIR // HD, rows, 1), lambda i: (i, 0, 0))
    halves = [pl.BlockSpec((key_rows, PAIR), lambda i, c=c: (c, i)) for c in range(2)]
    return common, row, lse, halves * blocks


def attend(ctx, qpos, kpos, q, pairs_of_rows):
    rows, width = q.shape
    key_rows, blocks, heads = pairs_of_rows[0].shape[0] // 2, len(pairs_of_rows), width // HD
    common, row, lse, keys = attention_specs(rows, key_rows, blocks)
    per_pair = PAIR // HD
    return pl.pallas_call(
        functools.partial(attend_kernel, blocks),
        grid=(width // PAIR,),
        in_specs=common + [row] + keys,
        out_specs=[row, lse],
        out_shape=[
            jax.ShapeDtypeStruct((rows, width), WIDE),
            jax.ShapeDtypeStruct((heads, rows, 1), WIDE),
        ],
        scratch_shapes=[
            pltpu.VMEM((per_pair, rows, HD), WIDE),
            pltpu.VMEM((per_pair, rows, 1), WIDE),
            pltpu.VMEM((per_pair, rows, 1), WIDE),
        ],
        compiler_params=pltpu.CompilerParams(vmem_limit_bytes=32 * 1024 * 1024),
        cost_estimate=work(43 * rows * key_rows * blocks * width),
        name="attend",
    )(ctx, qpos, kpos, q, *[p for p in pairs_of_rows for c in range(2)])


def attend_back_kernel(
    blocks, ctx_ref, qpos_ref, kpos_ref, q_ref, grad_ref, out_ref, lse_ref, *refs
):
    keys, values = refs[: 2 * blocks : 2], refs[1 : 2 * blocks : 2]
    dq_ref = refs[2 * blocks]
    dboth = refs[2 * blocks + 1 :]
    key_rows = keys[0].shape[0]
    allowed = kpos_ref[...] <= qpos_ref[...]
    scale = HD**-0.5
    for half in range(PAIR // HD):
        lanes = slice(half * HD, (half + 1) * HD)
        q = q_ref[:, lanes] * jnp.asarray(scale, LOW)
        grad = grad_ref[:, lanes]
        lse = lse_ref[half]
        delta = jnp.sum(grad.astype(WIDE) * out_ref[:, lanes], axis=1, keepdims=True)

        def block(b):
            k = keys[b][:, lanes]
            s = dot(q, k, NT)
            if b == 0:
                s = jnp.where(allowed, s, MASKED)
            p = jnp.exp(s - lse)
            dp = dot(grad, values[b][:, lanes], NT)
            ds = (p * (dp - delta)).astype(LOW)
            kind = dboth[b].dtype
            dboth[b][key_rows:, lanes] = dot(p.astype(LOW), grad, TN).astype(kind)
            dboth[b][:key_rows, lanes] = dot(ds, q, TN).astype(kind)
            return dot(ds, k, NN) * scale

        dq_ref[:, lanes] = block(0)
        for b in range(1, blocks):

            @pl.when(ctx_ref[0] >= b)
            def _():
                dq_ref[:, lanes] += block(b)

            @pl.when(ctx_ref[0] < b)
            def _():
                dboth[b][:, lanes] = jnp.zeros((2 * key_rows, HD), LOW)


def attend_back(ctx, qpos, kpos, q, grad, out, lse, pairs_of_rows):
    rows, width = q.shape
    key_rows, blocks = pairs_of_rows[0].shape[0] // 2, len(pairs_of_rows)
    common, row, lse_spec, keys = attention_specs(rows, key_rows, blocks)
    both = pl.BlockSpec((2 * key_rows, PAIR), lambda i: (0, i))
    near = [jax.ShapeDtypeStruct((2 * key_rows, width), WIDE)]
    far = [jax.ShapeDtypeStruct((2 * key_rows, width), LOW)] * (blocks - 1)
    results = pl.pallas_call(
        functools.partial(attend_back_kernel, blocks),
        grid=(width // PAIR,),
        in_specs=common + [row, row, row, lse_spec] + keys,
        out_specs=[row] + [both] * blocks,
        out_shape=[jax.ShapeDtypeStruct((rows, width), WIDE)] + near + far,
        compiler_params=pltpu.CompilerParams(vmem_limit_bytes=40 * 1024 * 1024),
        cost_estimate=work(75 * rows * key_rows * blocks * width),
        name="attend_back",
    )(ctx, qpos, kpos, q, grad, out, lse, *[p for p in pairs_of_rows for c in range(2)])
    return results[0], results[1], results[2:]


def norm_back_kernel(count, *refs):
    terms = refs[:count]
    unit_ref, inverse_ref, gain_ref, base_ref = refs[count : count + 4]
    grad_ref, low_ref, gain_out_ref, bias_out_ref = refs[count + 4 :]
    grad_rows = total_of([t[...].astype(WIDE) for t in terms])
    unit = unit_ref[...]
    grad_unit = grad_rows * gain_ref[...]
    first_mean = jnp.mean(grad_unit, axis=-1, keepdims=True)
    second_mean = jnp.mean(grad_unit * unit, axis=-1, keepdims=True)
    total = base_ref[...] + inverse_ref[...] * (grad_unit - first_mean - unit * second_mean)
    grad_ref[...] = total
    low_ref[...] = total.astype(LOW)
    gain_out_ref[...] = jnp.sum(grad_rows * unit, axis=0, keepdims=True)
    bias_out_ref[...] = jnp.sum(grad_rows, axis=0, keepdims=True)


def norm_back(terms, unit, inverse, gain, base):
    rows, model = unit.shape
    fixed = lambda i: (0, 0)
    line = (1, model)
    operands = [*terms, unit, inverse, gain[None], base]
    shapes = [(rows, model)] * (len(terms) + 1) + [(rows, 1), line, (rows, model)]
    outs = [((rows, model), WIDE), ((rows, model), LOW), (line, WIDE), (line, WIDE)]
    results = tiled(
        functools.partial(norm_back_kernel, len(terms)),
        "norm_back",
        1,
        [(o, s, fixed) for o, s in zip(operands, shapes)],
        [(jax.ShapeDtypeStruct(s, t), s, fixed) for s, t in outs],
        1e9,
    )
    return results[0], results[1], results[2][0], results[3][0]


def finish(buffer, layer, terms, make, steps, ins, out, name):
    shape, block, place = out

    def kernel(*refs):
        refs[-1][...] = make(*[r[...].astype(WIDE) for r in refs[: len(terms)]])

    operands = list(terms)
    specs = [pl.BlockSpec(b, index) for b, index in ins]
    if buffer is not None:
        operands.append(buffer)
        specs.append(pl.BlockSpec(memory_space=pl.ANY))
    return pl.pallas_call(
        kernel,
        grid=(steps,),
        in_specs=specs,
        out_specs=pl.BlockSpec((1,) + block, lambda i: (layer,) + place(i)),
        out_shape=jax.ShapeDtypeStruct(shape, WIDE),
        input_output_aliases={} if buffer is None else {len(terms): 0},
        compiler_params=pltpu.CompilerParams(vmem_limit_bytes=48 * 1024 * 1024),
        cost_estimate=work(1e9),
        name=name,
    )(*operands)


def finish_matrix(buffer, layer, terms, name):
    rows, columns = terms[0].shape
    block = (rows // 4, columns)
    place = lambda i: (i, 0)
    out = ((LAYERS, rows, columns), block, place)
    make = lambda *t: total_of(t)[None]
    return finish(buffer, layer, terms, make, 4, [(block, place)] * len(terms), out, name)


def finish_projections(buffer, layer, terms):
    rows, columns = terms[0].shape
    width = columns // 3
    out = ((LAYERS, 3, rows, width), (1, rows, width), lambda i: (i, 0, 0))
    make = lambda *t: total_of(t)[None, None]
    ins = [((rows, width), lambda i: (0, i))] * len(terms)
    return finish(buffer, layer, terms, make, 3, ins, out, "finish_qkv")


def finish_gate_up(buffer, layer, gate_terms, up_terms):
    rows, columns = gate_terms[0].shape
    steps = 8
    block = (rows // steps, columns)
    out = ((LAYERS, rows, 2, columns), (rows // steps, 2, columns), lambda i: (i, 0, 0))
    count = len(gate_terms)
    make = lambda *t: jnp.stack([total_of(t[:count]), total_of(t[count:])], axis=1)[None]
    ins = [(block, lambda i: (i, 0))] * (2 * count)
    return finish(buffer, layer, gate_terms + up_terms, make, steps, ins, out, "finish_gate_up")


def bits_of(count):
    return [1 << k for k in range(count.bit_length() - 1)]


def swapped(value, axis, mask):
    count = lax.axis_size(axis)
    return lax.ppermute(value, axis, [(i, i ^ mask) for i in range(count)])


def joined(pieces, axis):
    return pieces[0] if len(pieces) == 1 else jnp.concatenate(pieces, axis=axis)


class Line:
    def __init__(self, own_rows):
        n_tensor = lax.axis_size("tensor")
        tensor, ctx = lax.axis_index("tensor"), lax.axis_index("ctx")
        self.count, self.tensor = n_tensor, tensor
        row = jnp.arange(own_rows, dtype=jnp.int32)
        chip = (tensor + jnp.arange(n_tensor, dtype=jnp.int32)) % n_tensor
        place = (chip[:, None] * own_rows + row[None, :]).reshape(-1)
        block = n_tensor * own_rows
        self.places = ctx * block + place
        self.ctx = ctx.astype(jnp.int32).reshape(1)
        self.own_rows = own_rows

    def gather_rows(self, low):
        count, t = self.count, self.tensor
        send = lambda v, *route: lax.ppermute(v, "tensor", list(route))
        if count == 4:
            far = send(low, (0, 2), (2, 0), (1, 3), (3, 1))
            above = send(low, (0, 1), (1, 2), (2, 3))
            below = send(low, (1, 0), (2, 1), (3, 2))
            end = send(far, (2, 3), (1, 0))
            found = [low, jnp.where(t == 3, end, below), far, jnp.where(t == 0, end, above)]
        else:
            found = [low] + [
                send(low, *[((i + d) % count, i) for i in range(count)]) for d in range(1, count)
            ]
        return jnp.concatenate(found, axis=0)

    def sum_rows(self, low):
        rows, count, t = self.own_rows, self.count, self.tensor
        terms = [low[d * rows : (d + 1) * rows] for d in range(count)]
        send = lambda v, *route: lax.ppermute(v, "tensor", list(route))
        wide = lambda v: v.astype(WIDE)
        if count == 4:
            end = send(jnp.where(t == 0, terms[3], terms[1]), (0, 1), (3, 2))
            above = send(terms[1], (0, 1), (1, 2), (2, 3))
            below = send(terms[3], (3, 2), (2, 1), (1, 0))
            far = (wide(terms[2]) + wide(end)).astype(LOW)
            got = [send(far, (0, 2), (2, 0), (1, 3), (3, 1)), above, below]
        else:
            got = [
                send(terms[d], *[(i, (i + d) % count) for i in range(count)])
                for d in range(1, count)
            ]
        return (low, *got)

    def sum_of(self, terms):
        return total_of([terms[0][: self.own_rows].astype(WIDE)] + [t.astype(WIDE) for t in terms[1:]])

    def owner(self, low):
        count = lax.axis_size("ctx")
        if count != 2:
            return (lax.psum(low, "ctx") if count > 1 else low,)
        got = yield swapped(low, "ctx", 1)
        return (low, got)

    def far_keys(self, value):
        count = lax.axis_size("ctx")
        return [
            lax.ppermute(value, "ctx", [(i, i + s) for i in range(count - s)])
            for s in range(1, count)
        ]

    def far_key_grads(self, values):
        count = lax.axis_size("ctx")
        return [
            lax.ppermute(values[s - 1], "ctx", [(i + s, i) for i in range(count - s)])
            for s in range(1, count)
        ]


def weight_stages(shard):
    shard = yield shard
    return (yield lax.all_gather(shard, "dp"))


def grad_stages(plan, value, axis):
    got = yield lax.psum_scatter(value.astype(LOW), "dp", scatter_dimension=axis, tiled=True)
    return (yield from plan.owner(got))


def low_first(count):
    width = count.bit_length() - 1
    return sorted(range(count), key=lambda r: int(format(r, "b").zfill(width)[::-1] or "0", 2))


def pair_stages(plan, terms_of, axis):
    count = lax.axis_size("dp")

    def term(parts):
        factors = [terms_of(r) for r in parts]
        a = joined([f[0] for f in factors], 1) if axis == 0 else factors[0][0]
        b = joined([f[1] for f in factors], 1) if axis == 1 else factors[0][1]
        return outer(a, b)

    order = low_first(count)
    kept = None
    for bit in bits_of(count):
        if kept is None:
            sent = yield term(order[count // 2 :])
        else:
            kept, sent = jnp.split(kept, 2, axis=axis)
        got = yield swapped(sent.astype(LOW), "dp", bit)
        kept = (term(order[: count // 2]).astype(WIDE) if kept is None else kept) + got.astype(WIDE)
    return (yield from plan.owner(kept.astype(LOW)))


class Job:
    def __init__(self, stages):
        self.stages, self.value, self.result, self.done = stages, None, None, False
        self.advance(None)

    def advance(self, value):
        try:
            self.value = self.stages.send(value)
        except StopIteration as end:
            self.done, self.result, self.value = True, end.value, None

    def finish(self):
        while not self.done:
            self.advance(self.value)
        return self.result


def meanwhile(value, *jobs):
    open_jobs = [j for j in jobs if j is not None and not j.done]
    if not open_jobs:
        return value
    value, held = lax.optimization_barrier((value, tuple(j.value for j in open_jobs)))
    for job, got in zip(open_jobs, held):
        job.advance(got)
    return value


def held(value, *jobs):
    open_jobs = [j for j in jobs if j is not None and not j.done]
    if not open_jobs:
        return value
    value, kept = lax.optimization_barrier((value, tuple(j.value for j in open_jobs)))
    for job, got in zip(open_jobs, kept):
        job.value = got
    return value


def shards(
    tokens,
    cotangent,
    norm_gains,
    norm_biases,
    qkv_weight,
    qkv_bias,
    out_weight,
    gate_up_weight,
    down_weight,
):
    own_rows = tokens.shape[1]
    model = tokens.shape[2]
    heads_width = qkv_weight.shape[3]
    plan = Line(own_rows)
    tables = rotary_tables(plan.places)
    tables_back = (tables[0], -tables[1], -tables[2])
    qpos = plan.places[:, None]
    kpos = plan.places[None, :]
    gains = (norm_gains)
    biases = (norm_biases)
    qkv_bias_own = lax.dynamic_slice_in_dim(qkv_bias, lax.axis_index("tensor") * heads_width, heads_width, 2)

    def weight_jobs(layer, after):
        (qkv_all, out_all, gate_up_all, down_all), after = lax.optimization_barrier(
            ((qkv_weight, out_weight, gate_up_weight, down_weight), after)
        )
        matrices = {
            "qkv": jnp.transpose(qkv_all[layer], (1, 0, 2)),
            "out": out_all[layer],
            "gate": gate_up_all[layer, :, 0],
            "up": gate_up_all[layer, :, 1],
            "down": down_all[layer],
        }
        return {n: Job(weight_stages(v)) for n, v in matrices.items()}, after

    now, unused = weight_jobs(0, ())
    for name in ("qkv", "out", "gate", "up"):
        now[name].advance(now[name].value)
    stream = tokens[0].astype(WIDE)
    later = {}
    saved = []
    for layer in range(LAYERS):
        last = layer + 1 == LAYERS
        normed_one, unit_one, inverse_one = layer_norm_rows(
            stream, gains[layer, 0], biases[layer, 0]
        )
        rows_one = plan.gather_rows(normed_one.astype(LOW))
        if layer == 0:
            rows_one = meanwhile(rows_one, now["qkv"], now["down"])
        else:
            rows_one = meanwhile(rows_one, now["out"], now["gate"], now["down"])
        qkv_full = now["qkv"].finish()
        queries, keys_values = project(rows_one, qkv_full, qkv_bias_own[layer], tables)
        if layer == 0:
            late_cotangent, queries = lax.optimization_barrier((cotangent[0], queries))
            grad_stream = late_cotangent.astype(WIDE)
            branch = plan.gather_rows(late_cotangent)
        all_kv = [keys_values] + plan.far_keys(keys_values)
        attended, lse = attend(plan.ctx, qpos, kpos, queries, all_kv)
        attended_low = meanwhile(attended.astype(LOW), now["out"])
        if layer == 0:
            attended_low, branch = lax.optimization_barrier((attended_low, branch))
        else:
            attended_low = meanwhile(attended_low, now["up"])
        out_full = now["out"].finish()
        mid = stream + plan.sum_of(plan.sum_rows(times_wide(attended_low, out_full, "out")))
        mid = meanwhile(mid, now["gate"], now["up"])
        if layer > 0:
            mid = meanwhile(mid, now["down"])
        else:
            later, mid = weight_jobs(layer + 1, mid)
        normed_two, unit_two, inverse_two = layer_norm_rows(mid, gains[layer, 1], biases[layer, 1])
        rows_two = plan.gather_rows(normed_two.astype(LOW))
        rows_two = meanwhile(rows_two, now["down"], later.get("qkv"))
        flat = lambda v: v.reshape(v.shape[0] * v.shape[1], v.shape[2])
        gate_full, up_full = flat(now["gate"].finish()), flat(now["up"].finish())
        gate, up, activated = gate_up_rows(rows_two, gate_full, up_full)
        activated = meanwhile(activated, later.get("out"), later.get("gate"))
        down_full = now["down"].finish()
        if not last:
            stream = mid + plan.sum_of(
                plan.sum_rows(times_wide(activated, down_full, "down"))
            )
            stream = meanwhile(stream, later.get("qkv"), later.get("up"))
        saved.append(
            (
                (qkv_full, out_full, gate_full, up_full, down_full),
                (rows_one, unit_one, inverse_one),
                (queries, all_kv, attended, attended_low, lse),
                (rows_two, unit_two, inverse_two),
                (gate, up, activated),
            )
        )
        now = later
    grad_jobs = [None] * LAYERS
    gain_grads = [None] * LAYERS
    bias_grads = [None] * LAYERS
    qkv_bias_grads = [None] * LAYERS
    for layer in range(LAYERS - 1, -1, -1):
        (
            (qkv_full, out_full, gate_full, up_full, down_full),
            (rows_one, unit_one, inverse_one),
            (queries, all_kv, attended, attended_low, lse),
            (rows_two, unit_two, inverse_two),
            (gate, up, activated),
        ) = saved[layer]
        mine = {}
        grad_jobs[layer] = mine
        above = grad_jobs[layer + 1] if layer + 1 < LAYERS else {}
        old = lambda *keys: [above.get(k) for k in keys]

        def own_part(value, r):
            index = lax.axis_index("dp") ^ r
            width = value.shape[1] // lax.axis_size("dp")
            return lax.dynamic_slice_in_dim(value, index * width, width, 1)

        def in_job(a, b):
            return Job(grad_stages(plan, outer(a, b), 0))

        def out_job(a, b):
            return Job(grad_stages(plan, outer(a, b), 1))

        if layer + 1 < LAYERS:
            branch = plan.gather_rows(grad_low)
        branch = meanwhile(branch, *old("gate", "up", "out"))
        if layer == 0:
            down_grad, branch = lax.optimization_barrier(
                (outer(activated, branch), branch)
            )
            mine["down"] = Job(grad_stages(plan, down_grad, 1))
        grad_gate, grad_up = gate_up_back(branch, down_full, gate, up)
        partial_in = gate_up_in(grad_gate, grad_up, gate_full, up_full)
        summed = plan.sum_rows(partial_in)
        summed = meanwhile(summed, *old("up", "out", "qkv"))
        hidden_grad, hidden_low, gain_two, bias_two = norm_back(
            summed, unit_two, inverse_two, gains[layer, 1], grad_stream
        )
        hidden_low, (branch, grad_gate, grad_up) = lax.optimization_barrier(
            (hidden_low, (branch, grad_gate, grad_up))
        )
        if layer > 0:
            mine["down"] = out_job(activated, branch)
        mine["gate"] = in_job(rows_two, grad_gate)
        mine["up"] = in_job(rows_two, grad_up)
        top = layer + 1 == LAYERS
        if top:
            late, hidden_low = lax.optimization_barrier((activated, hidden_low))
            partial_out = times_wide(late, down_full, "down")
        attention = plan.gather_rows(hidden_low)
        attention = meanwhile(attention, *old("qkv"))
        if layer == 0:
            attention = meanwhile(attention, mine["down"])
        if top:
            attention, partial_out = lax.optimization_barrier((attention, partial_out))
            output = (mid + plan.sum_of(plan.sum_rows(partial_out))).astype(LOW)[None]
        grad_attended = out_back(attention, out_full)
        grad_queries, grad_kv, far_grads = attend_back(
            plan.ctx, qpos, kpos, queries, grad_attended, attended, lse, all_kv
        )
        grad_queries, attention = lax.optimization_barrier((grad_queries, attention))
        if layer == 0:
            mine["out"] = Job(
                pair_stages(plan, lambda r, a=attention: (attended_low, own_part(a, r)), 1)
            )
        else:
            mine["out"] = out_job(attended_low, attention)
        projected, qkv_bias_grads[layer] = project_back(
            grad_queries, grad_kv, plan.far_key_grads(far_grads), tables_back
        )
        projected = meanwhile(projected, mine["down"], *old("qkv"))
        if not top:
            above_done, projected = lax.optimization_barrier(
                ({k: j.finish() for k, j in above.items()}, projected)
            )
            sums = above_done
            results = [
                finish_projections(None, layer + 1, sums["qkv"]),
                finish_matrix(None, layer + 1, sums["out"], "finish_out"),
                finish_gate_up(None, layer + 1, sums["gate"], sums["up"]),
                finish_matrix(None, layer + 1, sums["down"], "finish_down"),
            ]
        if layer == 0:
            mine["qkv"] = Job(
                pair_stages(plan, lambda r, b=projected: (own_part(rows_one, r), b), 0)
            )
            projected = meanwhile(projected, *map(mine.get, ("qkv", "out", "gate")))
        partial_in = project_in(projected, qkv_full)
        if top:
            partial_in, output = lax.optimization_barrier((partial_in, output))
        if layer == 0:
            partial_in = held(meanwhile(partial_in, mine["up"], mine["qkv"]), mine["out"])
        summed = plan.sum_rows(partial_in)
        if layer > 0:
            summed = meanwhile(summed, mine["down"])
        else:
            summed = meanwhile(summed, *map(mine.get, ("gate", "out", "qkv")))
        grad_stream, grad_low, gain_one, bias_one = norm_back(
            summed, unit_one, inverse_one, gains[layer, 0], hidden_grad
        )
        if layer > 0:
            grad_low, projected = lax.optimization_barrier((grad_low, projected))
            mine["qkv"] = in_job(rows_one, projected)
            grad_low = meanwhile(grad_low, mine["gate"])
        gain_grads[layer] = jnp.stack([gain_one, gain_two])
        bias_grads[layer] = jnp.stack([bias_one, bias_two])

    tokens_grad = grad_low[None]
    padded_bias = lax.dynamic_update_slice_in_dim(
        jnp.zeros((LAYERS, 3, qkv_bias.shape[2]), WIDE),
        jnp.stack(qkv_bias_grads),
        lax.axis_index("tensor") * heads_width,
        2,
    )
    small = jnp.concatenate(
        [
            (jnp.stack(gain_grads)).reshape(LAYERS * 2, model),
            (jnp.stack(bias_grads)).reshape(LAYERS * 2, model),
            padded_bias.reshape(LAYERS * 3, qkv_bias.shape[2]),
        ],
        axis=0,
    )
    for axis in ("ctx", "dp", "tensor"):
        for bit in bits_of(lax.axis_size(axis)):
            small = small + swapped(small, axis, bit)
        small, results = lax.optimization_barrier((small, results))
    sums = {k: j.finish() for k, j in grad_jobs[0].items()}
    results = [
        finish_projections(results[0], 0, sums["qkv"]),
        finish_matrix(results[1], 0, sums["out"], "finish_out"),
        finish_gate_up(results[2], 0, sums["gate"], sums["up"]),
        finish_matrix(results[3], 0, sums["down"], "finish_down"),
    ]
    return (
        output,
        tokens_grad,
        small[: LAYERS * 2].reshape(LAYERS, 2, model),
        small[LAYERS * 2 : LAYERS * 4].reshape(LAYERS, 2, model),
        jnp.transpose(results[0], (0, 2, 1, 3)),
        small[LAYERS * 4 :].reshape(LAYERS, 3, qkv_bias.shape[2]),
        *results[1:],
    )


def solution(mesh):
    rows = P("dp", ("ctx", "tensor"), None)
    wide = P(None, "dp", None, "tensor")
    tall = P(None, "tensor", "dp")
    return jax.shard_map(
        shards,
        mesh=mesh,
        in_specs=(rows, rows, P(), P(), wide, P(), tall, wide, tall),
        out_specs=(rows, rows, P(), P(), wide, P(), tall, wide, tall),
        check_vma=False,
    )
```

```python
import functools

import jax
import jax.numpy as jnp
from jax import lax
from jax.experimental import pallas as pl
from jax.experimental.pallas import tpu as pltpu
from jax.sharding import PartitionSpec as P

HD = 64
ROT = 16
LAYERS = 2

MASKED = -1e30
EPSILON = 1e-05
LOW = jnp.bfloat16
WIDE = jnp.float32


def layer_norm_rows(stream, gain, bias):
    row_mean = jnp.mean(stream, axis=-1, keepdims=True)
    centered = stream - row_mean
    inverse = lax.rsqrt(jnp.mean(centered * centered, axis=-1, keepdims=True) + EPSILON)
    unit_rows = centered * inverse
    return (unit_rows * gain + bias, unit_rows, inverse)


def rotary_tables(positions):
    half_rot = ROT // 2
    frequency = 10000.0 ** (-(jnp.arange(half_rot, dtype=jnp.float32) * 2.0) / ROT)
    angles = positions.astype(jnp.float32)[:, None] * frequency[None, :]
    cosine, sine = jnp.cos(angles), jnp.sin(angles)
    rest = jnp.zeros((angles.shape[0], HD - ROT), WIDE)
    none = jnp.zeros_like(sine)
    heads = lambda *parts: jnp.tile(jnp.concatenate(parts, axis=1), (1, PAIR // HD))
    return (
        heads(cosine, cosine, rest + 1.0),
        heads(-sine, none, rest),
        heads(none, sine, rest),
    )


def rotated(flat, cos_ref, right_ref, left_ref):
    shift = ROT // 2
    found = []
    for start in range(0, flat.shape[1], PAIR):
        v = flat[:, start : start + PAIR]
        right, left = pltpu.roll(v, PAIR - shift, 1), pltpu.roll(v, shift, 1)
        found.append(v * cos_ref[...] + right * right_ref[...] + left * left_ref[...])
    return jnp.concatenate(found, axis=1)


def dot(a, b, dims):
    return lax.dot_general(a, b, (dims, ((), ())), preferred_element_type=WIDE)


PAIR = 128


NN = ((1,), (0,))
NT = ((1,), (1,))
TN = ((0,), (0,))


def total_of(terms):
    return functools.reduce(lambda a, b: a + b, terms)


def work(flops):
    return pl.CostEstimate(flops=int(flops), bytes_accessed=0, transcendentals=0)


TILE = 512


def tiled(kernel, name, steps, ins, outs, flops):
    return pl.pallas_call(
        kernel,
        grid=(steps,),
        in_specs=[pl.BlockSpec(block, index) for _, block, index in ins],
        out_specs=[pl.BlockSpec(block, index) for _, block, index in outs],
        out_shape=[shape for shape, _, _ in outs],
        compiler_params=pltpu.CompilerParams(vmem_limit_bytes=48 * 1024 * 1024),
        cost_estimate=work(2.5 * flops),
        name=name,
    )(*[array for array, _, _ in ins])


def whole_block(array):
    return (array, array.shape, lambda i: (0,) * array.ndim)


def column_block(array):
    return (array, (array.shape[0], TILE), lambda i: (0, i))


def row_block(array):
    return (array, (TILE, array.shape[1]), lambda i: (i, 0))


def gate_up_kernel(rows_ref, gate_w_ref, up_w_ref, gate_ref, up_ref, activated_ref):
    rows = rows_ref[...]
    gate = dot(rows, gate_w_ref[...], NN)
    up = dot(rows, up_w_ref[...], NN)
    gate_ref[...] = gate
    up_ref[...] = up
    activated_ref[...] = (gate * jax.nn.sigmoid(gate) * up).astype(LOW)


def gate_up_rows(rows, gate_weight, up_weight):
    count, hidden = rows.shape[0], gate_weight.shape[1]
    shapes = [jax.ShapeDtypeStruct((count, hidden), t) for t in (WIDE, WIDE, LOW)]
    return tiled(
        gate_up_kernel,
        "gate_up",
        pl.cdiv(hidden, TILE),
        [whole_block(rows), column_block(gate_weight), column_block(up_weight)],
        [column_block(s) for s in shapes],
        4 * rows.size * hidden,
    )


def back_sum(rows, weight_ref):
    width = weight_ref.shape[2]
    return total_of(
        dot(rows[:, r * width : (r + 1) * width], weight_ref[r], NT)
        for r in range(weight_ref.shape[0])
    )


def tall_block(array):
    return (array, (array.shape[0], TILE, array.shape[2]), lambda i: (0, i, 0))


def gate_up_back_kernel(rows_ref, weight_ref, gate_ref, up_ref, grad_gate_ref, grad_up_ref):
    grad = back_sum(rows_ref[...], weight_ref)
    gate, up = gate_ref[...], up_ref[...]
    s = jax.nn.sigmoid(gate)
    grad_gate_ref[...] = (grad * up * s * (1.0 + gate * (1.0 - s))).astype(LOW)
    grad_up_ref[...] = (grad * (gate * s)).astype(LOW)


def gate_up_back(rows, down_weight, gate, up):
    count, hidden = gate.shape
    shape = jax.ShapeDtypeStruct((count, hidden), LOW)
    return tiled(
        gate_up_back_kernel,
        "gate_up_back",
        pl.cdiv(hidden, TILE),
        [whole_block(rows), tall_block(down_weight), column_block(gate), column_block(up)],
        [column_block(shape)] * 2,
        2 * rows.size * hidden,
    )


def out_back_kernel(rows_ref, weight_ref, out_ref):
    out_ref[...] = back_sum(rows_ref[...], weight_ref).astype(LOW)


def out_back(rows, weight):
    shape = jax.ShapeDtypeStruct((rows.shape[0], weight.shape[1]), LOW)
    return tiled(
        out_back_kernel,
        "out_back",
        shape.shape[1] // TILE,
        [whole_block(rows), tall_block(weight)],
        [column_block(shape)],
        2 * rows.size * shape.shape[1],
    )[0]


def wide_kernel(rows_ref, weight_ref, out_ref):
    out_ref[...] = dot(rows_ref[...], weight_ref[0], NN).astype(LOW)


def times_wide(rows, weight, name):
    blocks, depth, width = weight.shape
    per = width // TILE
    shape = jax.ShapeDtypeStruct((rows.shape[0], blocks * width), LOW)
    return tiled(
        wide_kernel,
        name,
        blocks * per,
        [whole_block(rows), (weight, (1, depth, TILE), lambda i: (i // per, 0, i % per))],
        [column_block(shape)],
        2 * rows.size * blocks * width,
    )[0]


def gate_up_in_kernel(gate_ref, up_ref, gate_w_ref, up_w_ref, out_ref):
    total = dot(gate_ref[...], gate_w_ref[...], NT) + dot(up_ref[...], up_w_ref[...], NT)
    out_ref[...] = total.astype(LOW)


def gate_up_in(grad_gate, grad_up, gate_weight, up_weight):
    shape = jax.ShapeDtypeStruct((grad_gate.shape[0], gate_weight.shape[0]), LOW)
    return tiled(
        gate_up_in_kernel,
        "gate_up_in",
        shape.shape[1] // TILE,
        [whole_block(grad_gate), whole_block(grad_up), row_block(gate_weight), row_block(up_weight)],
        [column_block(shape)],
        4 * grad_gate.size * shape.shape[1],
    )[0]


def project_in_kernel(rows_ref, weight_ref, out_ref):
    width = weight_ref.shape[3]
    out_ref[...] = total_of(
        dot(rows_ref[:, c * width : (c + 1) * width], weight_ref[0, c], NT) for c in range(3)
    ).astype(LOW)


def project_in(rows, weight):
    blocks, three, depth, width = weight.shape
    per = depth // TILE
    shape = jax.ShapeDtypeStruct((rows.shape[0], blocks * depth), LOW)
    return tiled(
        project_in_kernel,
        "project_in",
        blocks * per,
        [whole_block(rows), (weight, (1, three, TILE, width), lambda i: (i // per, 0, i % per, 0))],
        [column_block(shape)],
        2 * rows.size * blocks * depth,
    )[0]


def outer_kernel(a_ref, b_ref, out_ref):
    out_ref[...] = dot(a_ref[...], b_ref[...], TN).astype(LOW)


def outer(a, b):
    shape = jax.ShapeDtypeStruct((a.shape[1], b.shape[1]), LOW)
    return tiled(
        outer_kernel,
        "outer",
        pl.cdiv(a.shape[1], TILE),
        [column_block(a), whole_block(b)],
        [row_block(shape)],
        a.size * b.shape[1] * 0.8,
    )[0]


def project_kernel(rows_ref, weight_ref, bias_ref, cos_ref, right_ref, left_ref, q_ref, kv_ref):
    blocks, _, depth, width = weight_ref.shape
    flat = dot(rows_ref[...], weight_ref[...].reshape(blocks * depth, width), NN) + bias_ref[0]
    step = pl.program_id(0)

    @pl.when(step == 0)
    def _():
        kv_ref[...] = rotated(flat, cos_ref, right_ref, left_ref).astype(LOW)

    @pl.when(step == 1)
    def _():
        kv_ref[...] = flat.astype(LOW)

    @pl.when(step == 2)
    def _():
        q_ref[...] = rotated(flat, cos_ref, right_ref, left_ref).astype(LOW)


def project(rows, weight, bias, tables):
    count = rows.shape[0]
    blocks, _, depth, width = weight.shape
    fixed = lambda i: (0, 0)
    shapes = [jax.ShapeDtypeStruct((k * count, width), LOW) for k in (1, 2)]
    return tiled(
        project_kernel,
        "project",
        3,
        [
            whole_block(rows),
            (weight, (blocks, 1, depth, width), lambda i: (0, (i + 1) % 3, 0, 0)),
            (bias[:, None, :], (1, 1, width), lambda i: ((i + 1) % 3, 0, 0)),
        ]
        + [(t, (count, PAIR), fixed) for t in tables],
        [
            (shapes[0], (count, width), fixed),
            (shapes[1], (count, width), lambda i: (jnp.minimum(i, 1), 0)),
        ],
        6 * rows.size * width,
    )


def project_back_kernel(far, dq_ref, dkv_ref, *refs):
    far_refs = refs[:far]
    cos_ref, right_ref, left_ref, out_ref, sum_ref = refs[far:]
    step = pl.program_id(0)

    def put(value):
        out_ref[...] = value.astype(LOW)
        sum_ref[0] = jnp.sum(value, axis=0, keepdims=True)

    def key_value():
        return total_of([dkv_ref[...]] + [r[...].astype(WIDE) for r in far_refs])

    @pl.when(step == 0)
    def _():
        put(rotated(dq_ref[...], cos_ref, right_ref, left_ref))

    @pl.when(step == 1)
    def _():
        put(rotated(key_value(), cos_ref, right_ref, left_ref))

    @pl.when(step == 2)
    def _():
        put(key_value())


def project_back(dq, dkv, far, tables):
    count, width = dq.shape
    fixed = lambda i: (0, 0)
    lower = pl.BlockSpec((count, width), lambda i: (jnp.maximum(i - 1, 0), 0))
    out, sums = pl.pallas_call(
        functools.partial(project_back_kernel, len(far)),
        grid=(3,),
        in_specs=[pl.BlockSpec((count, width), fixed)]
        + [lower] * (1 + len(far))
        + [pl.BlockSpec((count, PAIR), fixed)] * 3,
        out_specs=[
            pl.BlockSpec((count, width), lambda i: (0, i)),
            pl.BlockSpec((1, 1, width), lambda i: (i, 0, 0)),
        ],
        out_shape=[
            jax.ShapeDtypeStruct((count, 3 * width), LOW),
            jax.ShapeDtypeStruct((3, 1, width), WIDE),
        ],
        compiler_params=pltpu.CompilerParams(vmem_limit_bytes=32 * 1024 * 1024),
        cost_estimate=work(14000 * count * width),
        name="project_back",
    )(dq, dkv, *far, *tables)
    return out, sums[:, 0]


def attend_near_kernel(qpos_ref, kpos_ref, q_ref, key_ref, value_ref, acc_ref, top_ref, total_ref):
    allowed = kpos_ref[0] <= qpos_ref[...]
    for half in range(PAIR // HD):
        lanes = slice(half * HD, (half + 1) * HD)
        q = q_ref[:, lanes] * jnp.asarray(HD**-0.5, LOW)
        s = jnp.where(allowed, dot(q, key_ref[:, lanes], NT), MASKED)
        top = jnp.max(s, axis=1, keepdims=True)
        p = jnp.exp(s - top)
        top_ref[half] = top
        total_ref[half] = jnp.sum(p, axis=1, keepdims=True)
        acc_ref[:, lanes] = dot(p.astype(LOW), value_ref[:, lanes], NN)


def attend_far_kernel(blocks, qpos_ref, kpos_ref, q_ref, acc_in_ref, top_in_ref, total_in_ref, *refs):
    keys, values = refs[: 2 * blocks : 2], refs[1 : 2 * blocks : 2]
    out_ref, lse_ref = refs[2 * blocks :]
    allowed = [kpos_ref[b] <= qpos_ref[...] for b in range(blocks)]
    for half in range(PAIR // HD):
        lanes = slice(half * HD, (half + 1) * HD)
        q = q_ref[:, lanes] * jnp.asarray(HD**-0.5, LOW)
        top, total, acc = top_in_ref[half], total_in_ref[half], acc_in_ref[:, lanes]
        for b in range(blocks):
            s = jnp.where(allowed[b], dot(q, keys[b][:, lanes], NT), MASKED)
            new_top = jnp.maximum(top, jnp.max(s, axis=1, keepdims=True))
            p = jnp.exp(s - new_top)
            factor = jnp.exp(top - new_top)
            total = total * factor + jnp.sum(p, axis=1, keepdims=True)
            acc = acc * factor + dot(p.astype(LOW), values[b][:, lanes], NN)
            top = new_top
        out_ref[:, lanes] = acc / total
        lse_ref[half] = top + jnp.log(total)


def pair_call(kernel, name, rows, width, kpos, operands, stacked, outs, flops):
    blocks, _, key_rows = kpos.shape
    column = lambda i: (0, i)
    specs = {
        "row": pl.BlockSpec((rows, PAIR), column),
        "head": pl.BlockSpec((PAIR // HD, rows, 1), lambda i: (i, 0, 0)),
        "keys": pl.BlockSpec((2 * key_rows, PAIR), column),
    }
    shapes = {"row": (rows, width), "head": (width // HD, rows, 1), "keys": (2 * key_rows, width)}
    halves = [pl.BlockSpec((key_rows, PAIR), lambda i, c=c: (c, i)) for c in range(2)]
    common = [
        pl.BlockSpec((rows, 1), lambda i: (0, 0)),
        pl.BlockSpec((blocks, 1, key_rows), lambda i: (0, 0, 0)),
    ]
    return pl.pallas_call(
        kernel,
        grid=(width // PAIR,),
        in_specs=common + [specs[k] for k, _ in operands[1:]] + halves * len(stacked),
        out_specs=[specs[k] for k, _ in outs],
        out_shape=[jax.ShapeDtypeStruct(shapes[k], t) for k, t in outs],
        compiler_params=pltpu.CompilerParams(vmem_limit_bytes=40 * 1024 * 1024),
        cost_estimate=work(flops * rows * key_rows * blocks * width),
        name=name,
    )(operands[0], kpos, *[v for _, v in operands[1:]], *[s for s in stacked for c in range(2)])


def attend_near(qpos, kpos, q, own):
    rows, width = q.shape
    outs = [("row", WIDE), ("head", WIDE), ("head", WIDE)]
    return pair_call(
        attend_near_kernel, "attend_near", rows, width, kpos, [qpos, ("row", q)], [own], outs, 43
    )


def attend_far(qpos, kpos, q, near, far):
    rows, width = q.shape
    kinds = ("row", "head", "head")
    operands = [qpos, ("row", q), *zip(kinds, near)]
    return pair_call(
        functools.partial(attend_far_kernel, len(far)),
        "attend_far",
        rows,
        width,
        kpos,
        operands,
        far,
        [("row", WIDE), ("head", WIDE)],
        43,
    )


def attend_back_kernel(blocks, more, qpos_ref, kpos_ref, q_ref, grad_ref, out_ref, lse_ref, *refs):
    before, refs = refs[:more], refs[more:]
    keys, values = refs[: 2 * blocks : 2], refs[1 : 2 * blocks : 2]
    dq_ref = refs[2 * blocks]
    dboth = refs[2 * blocks + 1 :]
    key_rows = keys[0].shape[0]
    allowed = [kpos_ref[b] <= qpos_ref[...] for b in range(blocks)]
    scale = HD**-0.5
    for half in range(PAIR // HD):
        lanes = slice(half * HD, (half + 1) * HD)
        q = q_ref[:, lanes] * jnp.asarray(scale, LOW)
        grad = grad_ref[:, lanes]
        lse = lse_ref[half]
        delta = jnp.sum(grad.astype(WIDE) * out_ref[:, lanes], axis=1, keepdims=True)
        dq = []
        for b in range(blocks):
            k = keys[b][:, lanes]
            s = jnp.where(allowed[b], dot(q, k, NT), MASKED)
            p = jnp.exp(s - lse)
            dp = dot(grad, values[b][:, lanes], NT)
            ds = (p * (dp - delta)).astype(LOW)
            kind = dboth[b].dtype
            dboth[b][key_rows:, lanes] = dot(p.astype(LOW), grad, TN).astype(kind)
            dboth[b][:key_rows, lanes] = dot(ds, q, TN).astype(kind)
            dq.append(dot(ds, k, NN))
        dq_ref[:, lanes] = total_of([total_of(dq) * scale] + [r[:, lanes] for r in before])


def attend_back(qpos, kpos, q, grad, out, lse, stacked, kind, before):
    rows, width = q.shape
    rest = [("row", v) for v in (q, grad, out)] + [("head", lse)] + [("row", v) for v in before]
    results = pair_call(
        functools.partial(attend_back_kernel, len(stacked), len(before)),
        "attend_back",
        rows,
        width,
        kpos,
        [qpos] + rest,
        stacked,
        [("row", WIDE)] + [("keys", kind)] * len(stacked),
        75,
    )
    return results[0], results[1:]


def norm_back_kernel(count, *refs):
    terms = refs[:count]
    unit_ref, inverse_ref, gain_ref, base_ref = refs[count : count + 4]
    grad_ref, low_ref, gain_out_ref, bias_out_ref = refs[count + 4 :]
    grad_rows = total_of([t[...].astype(WIDE) for t in terms])
    unit = unit_ref[...]
    grad_unit = grad_rows * gain_ref[...]
    first_mean = jnp.mean(grad_unit, axis=-1, keepdims=True)
    second_mean = jnp.mean(grad_unit * unit, axis=-1, keepdims=True)
    total = base_ref[...] + inverse_ref[...] * (grad_unit - first_mean - unit * second_mean)
    grad_ref[...] = total
    low_ref[...] = total.astype(LOW)
    gain_out_ref[...] = jnp.sum(grad_rows * unit, axis=0, keepdims=True)
    bias_out_ref[...] = jnp.sum(grad_rows, axis=0, keepdims=True)


def norm_back(terms, unit, inverse, gain, base):
    rows, model = unit.shape
    fixed = lambda i: (0, 0)
    line = (1, model)
    operands = [*terms, unit, inverse, gain[None], base]
    shapes = [(rows, model)] * (len(terms) + 1) + [(rows, 1), line, (rows, model)]
    outs = [((rows, model), WIDE), ((rows, model), LOW), (line, WIDE), (line, WIDE)]
    results = tiled(
        functools.partial(norm_back_kernel, len(terms)),
        "norm_back",
        1,
        [(o, s, fixed) for o, s in zip(operands, shapes)],
        [(jax.ShapeDtypeStruct(s, t), s, fixed) for s, t in outs],
        1e9,
    )
    return results[0], results[1], results[2][0], results[3][0]


def finish(buffer, layer, terms, make, steps, ins, out, name):
    shape, block, place = out

    def kernel(*refs):
        refs[-1][...] = make(*[r[...].astype(WIDE) for r in refs[: len(terms)]])

    operands = list(terms)
    specs = [pl.BlockSpec(b, index) for b, index in ins]
    if buffer is not None:
        operands.append(buffer)
        specs.append(pl.BlockSpec(memory_space=pl.ANY))
    return pl.pallas_call(
        kernel,
        grid=(steps,),
        in_specs=specs,
        out_specs=pl.BlockSpec((1,) + block, lambda i: (layer,) + place(i)),
        out_shape=jax.ShapeDtypeStruct(shape, WIDE),
        input_output_aliases={} if buffer is None else {len(terms): 0},
        compiler_params=pltpu.CompilerParams(vmem_limit_bytes=48 * 1024 * 1024),
        cost_estimate=work(1e9),
        name=name,
    )(*operands)


def finish_matrix(buffer, layer, terms, name):
    rows, columns = terms[0].shape
    block = (rows // 4, columns)
    place = lambda i: (i, 0)
    out = ((LAYERS, rows, columns), block, place)
    make = lambda *t: total_of(t)[None]
    return finish(buffer, layer, terms, make, 4, [(block, place)] * len(terms), out, name)


def finish_projections(buffer, layer, terms):
    rows, columns = terms[0].shape
    width = columns // 3
    out = ((LAYERS, 3, rows, width), (1, rows, width), lambda i: (i, 0, 0))
    make = lambda *t: total_of(t)[None, None]
    ins = [((rows, width), lambda i: (0, i))] * len(terms)
    return finish(buffer, layer, terms, make, 3, ins, out, "finish_qkv")


def finish_gate_up(buffer, layer, gate_terms, up_terms):
    rows, columns = gate_terms[0].shape
    steps = 8
    block = (rows // steps, columns)
    out = ((LAYERS, rows, 2, columns), (rows // steps, 2, columns), lambda i: (i, 0, 0))
    count = len(gate_terms)
    make = lambda *t: jnp.stack([total_of(t[:count]), total_of(t[count:])], axis=1)[None]
    ins = [(block, lambda i: (i, 0))] * (2 * count)
    return finish(buffer, layer, gate_terms + up_terms, make, steps, ins, out, "finish_gate_up")


def bits_of(count):
    return [1 << k for k in range(count.bit_length() - 1)]


def swapped(value, axis, mask):
    count = lax.axis_size(axis)
    return lax.ppermute(value, axis, [(i, i ^ mask) for i in range(count)])


def joined(pieces, axis):
    return pieces[0] if len(pieces) == 1 else jnp.concatenate(pieces, axis=axis)


class Line:
    def __init__(self, own_rows):
        n_tensor, n_ctx = lax.axis_size("tensor"), lax.axis_size("ctx")
        tensor, ctx = lax.axis_index("tensor"), lax.axis_index("ctx")
        self.count, self.tensor = n_tensor, tensor
        row = jnp.arange(own_rows, dtype=jnp.int32)
        chip = (tensor + jnp.arange(n_tensor, dtype=jnp.int32)) % n_tensor
        place = (chip[:, None] * own_rows + row[None, :]).reshape(-1)
        block = n_tensor * own_rows
        self.places = ctx * block + place
        self.far_places = [
            jnp.where(ctx >= s, (ctx - s) * block + place, 1 << 30) for s in range(1, n_ctx)
        ]
        self.own_rows = own_rows

    def gather_rows(self, low):
        count, t = self.count, self.tensor
        send = lambda v, *route: lax.ppermute(v, "tensor", list(route))
        if count == 4:
            far = send(low, (0, 2), (2, 0), (1, 3), (3, 1))
            above = send(low, (0, 1), (1, 2), (2, 3))
            below = send(low, (1, 0), (2, 1), (3, 2))
            end = send(far, (2, 3), (1, 0))
            found = [low, jnp.where(t == 3, end, below), far, jnp.where(t == 0, end, above)]
        else:
            found = [low] + [
                send(low, *[((i + d) % count, i) for i in range(count)]) for d in range(1, count)
            ]
        return jnp.concatenate(found, axis=0)

    def sum_rows(self, low):
        rows, count, t = self.own_rows, self.count, self.tensor
        terms = [low[d * rows : (d + 1) * rows] for d in range(count)]
        send = lambda v, *route: lax.ppermute(v, "tensor", list(route))
        wide = lambda v: v.astype(WIDE)
        if count == 4:
            end = send(jnp.where(t == 0, terms[3], terms[1]), (0, 1), (3, 2))
            above = send(terms[1], (0, 1), (1, 2), (2, 3))
            below = send(terms[3], (3, 2), (2, 1), (1, 0))
            far = (wide(terms[2]) + wide(end)).astype(LOW)
            got = [send(far, (0, 2), (2, 0), (1, 3), (3, 1)), above, below]
        else:
            got = [
                send(terms[d], *[(i, (i + d) % count) for i in range(count)])
                for d in range(1, count)
            ]
        return (low, *got)

    def sum_of(self, terms):
        return total_of([terms[0][: self.own_rows].astype(WIDE)] + [t.astype(WIDE) for t in terms[1:]])

    def owner(self, low):
        count = lax.axis_size("ctx")
        if count != 2:
            return (lax.psum(low, "ctx") if count > 1 else low,)
        got = yield swapped(low, "ctx", 1)
        return (low, got)

    def far_keys(self, value):
        count = lax.axis_size("ctx")
        return [
            lax.ppermute(value, "ctx", [(i, i + s) for i in range(count - s)])
            for s in range(1, count)
        ]

    def far_key_grads(self, values):
        count = lax.axis_size("ctx")
        return [
            lax.ppermute(values[s - 1], "ctx", [(i + s, i) for i in range(count - s)])
            for s in range(1, count)
        ]


def weight_stages(shard):
    shard = yield shard
    return (yield lax.all_gather(shard, "dp"))


def grad_stages(plan, value, axis):
    got = yield lax.psum_scatter(value.astype(LOW), "dp", scatter_dimension=axis, tiled=True)
    return (yield from plan.owner(got))


def low_first(count):
    width = count.bit_length() - 1
    return sorted(range(count), key=lambda r: int(format(r, "b").zfill(width)[::-1] or "0", 2))


def pair_stages(plan, terms_of, axis):
    count = lax.axis_size("dp")

    def term(parts):
        factors = [terms_of(r) for r in parts]
        a = joined([f[0] for f in factors], 1) if axis == 0 else factors[0][0]
        b = joined([f[1] for f in factors], 1) if axis == 1 else factors[0][1]
        return outer(a, b)

    order = low_first(count)
    kept = None
    for bit in bits_of(count):
        if kept is None:
            sent = yield term(order[count // 2 :])
        else:
            kept, sent = jnp.split(kept, 2, axis=axis)
        got = yield swapped(sent.astype(LOW), "dp", bit)
        kept = (term(order[: count // 2]).astype(WIDE) if kept is None else kept) + got.astype(WIDE)
    return (yield from plan.owner(kept.astype(LOW)))


class Job:
    def __init__(self, stages):
        self.stages, self.value, self.result, self.done = stages, None, None, False
        self.advance(None)

    def advance(self, value):
        try:
            self.value = self.stages.send(value)
        except StopIteration as end:
            self.done, self.result, self.value = True, end.value, None

    def finish(self):
        while not self.done:
            self.advance(self.value)
        return self.result


def meanwhile(value, *jobs):
    open_jobs = [j for j in jobs if j is not None and not j.done]
    if not open_jobs:
        return value
    value, held = lax.optimization_barrier((value, tuple(j.value for j in open_jobs)))
    for job, got in zip(open_jobs, held):
        job.advance(got)
    return value


def held(value, *jobs):
    open_jobs = [j for j in jobs if j is not None and not j.done]
    if not open_jobs:
        return value
    value, kept = lax.optimization_barrier((value, tuple(j.value for j in open_jobs)))
    for job, got in zip(open_jobs, kept):
        job.value = got
    return value


def shards(
    tokens,
    cotangent,
    norm_gains,
    norm_biases,
    qkv_weight,
    qkv_bias,
    out_weight,
    gate_up_weight,
    down_weight,
):
    own_rows = tokens.shape[1]
    model = tokens.shape[2]
    heads_width = qkv_weight.shape[3]
    plan = Line(own_rows)
    tables = rotary_tables(plan.places)
    tables_back = (tables[0], -tables[1], -tables[2])
    qpos = plan.places[:, None]
    near_places = plan.places[None, None, :]
    far_places = jnp.stack(plan.far_places)[:, None, :]
    gains = (norm_gains)
    biases = (norm_biases)
    qkv_bias_own = lax.dynamic_slice_in_dim(qkv_bias, lax.axis_index("tensor") * heads_width, heads_width, 2)

    def weight_jobs(layer, after):
        (qkv_all, out_all, gate_up_all, down_all), after = lax.optimization_barrier(
            ((qkv_weight, out_weight, gate_up_weight, down_weight), after)
        )
        matrices = {
            "qkv": jnp.transpose(qkv_all[layer], (1, 0, 2)),
            "out": out_all[layer],
            "gate": gate_up_all[layer, :, 0],
            "up": gate_up_all[layer, :, 1],
            "down": down_all[layer],
        }
        return {n: Job(weight_stages(v)) for n, v in matrices.items()}, after

    now, unused = weight_jobs(0, ())
    for name in ("qkv", "out", "gate", "up"):
        now[name].advance(now[name].value)
    stream = tokens[0].astype(WIDE)
    later = {}
    saved = []
    for layer in range(LAYERS):
        last = layer + 1 == LAYERS
        normed_one, unit_one, inverse_one = layer_norm_rows(
            stream, gains[layer, 0], biases[layer, 0]
        )
        rows_one = plan.gather_rows(normed_one.astype(LOW))
        if layer == 0:
            rows_one = meanwhile(rows_one, now["qkv"], now["down"])
        else:
            rows_one = meanwhile(rows_one, now["out"], now["gate"], now["down"])
        qkv_full = now["qkv"].finish()
        queries, keys_values = project(rows_one, qkv_full, qkv_bias_own[layer], tables)
        if layer == 0:
            late_cotangent, queries = lax.optimization_barrier((cotangent[0], queries))
            grad_stream = late_cotangent.astype(WIDE)
            branch = plan.gather_rows(late_cotangent)
        prepared = {}
        if not last:
            prepared, queries = weight_jobs(layer + 1, queries)
        far_kv = plan.far_keys(keys_values)
        near = attend_near(qpos, near_places, queries, keys_values)
        attended, lse = attend_far(qpos, far_places, queries, near, far_kv)
        attended_low = meanwhile(attended.astype(LOW), now["out"])
        attended_low = held(attended_low, *map(prepared.get, ("gate", "up")))
        if layer == 0:
            attended_low, branch = lax.optimization_barrier((attended_low, branch))
        else:
            attended_low = meanwhile(attended_low, now["up"])
        out_full = now["out"].finish()
        mid = stream + plan.sum_of(plan.sum_rows(times_wide(attended_low, out_full, "out")))
        mid = meanwhile(mid, now["gate"])
        if layer > 0:
            mid = meanwhile(mid, now["down"])
        else:
            later = prepared
        normed_two, unit_two, inverse_two = layer_norm_rows(mid, gains[layer, 1], biases[layer, 1])
        rows_two = plan.gather_rows(normed_two.astype(LOW))
        rows_two = meanwhile(rows_two, now["up"], now["down"], later.get("qkv"))
        flat = lambda v: v.reshape(v.shape[0] * v.shape[1], v.shape[2])
        gate_full, up_full = flat(now["gate"].finish()), flat(now["up"].finish())
        gate, up, activated = gate_up_rows(rows_two, gate_full, up_full)
        activated = meanwhile(activated, later.get("out"), later.get("gate"))
        down_full = now["down"].finish()
        if not last:
            stream = mid + plan.sum_of(
                plan.sum_rows(times_wide(activated, down_full, "down"))
            )
            stream = meanwhile(stream, later.get("qkv"), later.get("up"))
        saved.append(
            (
                (qkv_full, out_full, gate_full, up_full, down_full),
                (rows_one, unit_one, inverse_one),
                (queries, keys_values, far_kv, attended, attended_low, lse),
                (rows_two, unit_two, inverse_two),
                (gate, up, activated),
            )
        )
        now = later
    grad_jobs = [None] * LAYERS
    gain_grads = [None] * LAYERS
    bias_grads = [None] * LAYERS
    qkv_bias_grads = [None] * LAYERS
    for layer in range(LAYERS - 1, -1, -1):
        (
            (qkv_full, out_full, gate_full, up_full, down_full),
            (rows_one, unit_one, inverse_one),
            (queries, keys_values, far_kv, attended, attended_low, lse),
            (rows_two, unit_two, inverse_two),
            (gate, up, activated),
        ) = saved[layer]
        mine = {}
        grad_jobs[layer] = mine
        above = grad_jobs[layer + 1] if layer + 1 < LAYERS else {}
        old = lambda *keys: [above.get(k) for k in keys]

        def own_part(value, r):
            index = lax.axis_index("dp") ^ r
            width = value.shape[1] // lax.axis_size("dp")
            return lax.dynamic_slice_in_dim(value, index * width, width, 1)

        def in_job(a, b):
            return Job(grad_stages(plan, outer(a, b), 0))

        def out_job(a, b):
            return Job(grad_stages(plan, outer(a, b), 1))

        if layer + 1 < LAYERS:
            branch = plan.gather_rows(grad_low)
        branch = meanwhile(branch, *old("gate", "up", "out"))
        if layer == 0:
            down_grad, branch = lax.optimization_barrier(
                (outer(activated, branch), branch)
            )
            mine["down"] = Job(grad_stages(plan, down_grad, 1))
        grad_gate, grad_up = gate_up_back(branch, down_full, gate, up)
        partial_in = gate_up_in(grad_gate, grad_up, gate_full, up_full)
        summed = plan.sum_rows(partial_in)
        summed = meanwhile(summed, *old("up", "out", "qkv"))
        hidden_grad, hidden_low, gain_two, bias_two = norm_back(
            summed, unit_two, inverse_two, gains[layer, 1], grad_stream
        )
        hidden_low, (branch, grad_gate, grad_up) = lax.optimization_barrier(
            (hidden_low, (branch, grad_gate, grad_up))
        )
        if layer > 0:
            mine["down"] = out_job(activated, branch)
        mine["gate"] = in_job(rows_two, grad_gate)
        if layer == 0:
            mine["up"] = in_job(rows_two, grad_up)
        top = layer + 1 == LAYERS
        if top:
            late, hidden_low = lax.optimization_barrier((activated, hidden_low))
            partial_out = times_wide(late, down_full, "down")
        attention = plan.gather_rows(hidden_low)
        attention = meanwhile(attention, *old("qkv"))
        if layer == 0:
            attention = meanwhile(attention, mine["down"])
        if top:
            attention, partial_out = lax.optimization_barrier((attention, partial_out))
            output = (mid + plan.sum_of(plan.sum_rows(partial_out))).astype(LOW)[None]
        grad_attended = out_back(attention, out_full)
        shared = (queries, grad_attended, attended, lse)
        far_queries, far_grads = attend_back(qpos, far_places, *shared, far_kv, LOW, [])
        returned = plan.far_key_grads(far_grads)
        grad_queries, grad_kv = attend_back(
            qpos, near_places, *shared, [keys_values], WIDE, [far_queries]
        )
        if top:
            grad_queries, output = lax.optimization_barrier((grad_queries, output))
        projected, qkv_bias_grads[layer] = project_back(
            grad_queries, grad_kv[0], returned, tables_back
        )
        projected, (attention, grad_up) = lax.optimization_barrier(
            (projected, (attention, grad_up))
        )
        if layer > 0:
            mine["up"] = in_job(rows_two, grad_up)
        if layer == 0:
            mine["out"] = Job(
                pair_stages(plan, lambda r, a=attention: (attended_low, own_part(a, r)), 1)
            )
        else:
            mine["out"] = out_job(attended_low, attention)
        projected = meanwhile(projected, mine["down"] if layer > 0 else None, *old("qkv"))
        if not top:
            above_done, projected = lax.optimization_barrier(
                ({k: j.finish() for k, j in above.items()}, projected)
            )
            sums = above_done
            results = [
                finish_projections(None, layer + 1, sums["qkv"]),
                finish_matrix(None, layer + 1, sums["out"], "finish_out"),
                finish_gate_up(None, layer + 1, sums["gate"], sums["up"]),
                finish_matrix(None, layer + 1, sums["down"], "finish_down"),
            ]
        if layer == 0:
            mine["qkv"] = Job(
                pair_stages(plan, lambda r, b=projected: (own_part(rows_one, r), b), 0)
            )
            projected = meanwhile(projected, *map(mine.get, ("qkv", "out", "gate")))
        partial_in = project_in(projected, qkv_full)
        if layer == 0:
            partial_in = meanwhile(partial_in, *map(mine.get, ("down", "up", "qkv")))
            partial_in = held(partial_in, mine["out"])
        summed = plan.sum_rows(partial_in)
        if layer > 0:
            summed = meanwhile(summed, mine["down"])
        else:
            summed = meanwhile(summed, *map(mine.get, ("gate", "out", "qkv")))
        grad_stream, grad_low, gain_one, bias_one = norm_back(
            summed, unit_one, inverse_one, gains[layer, 0], hidden_grad
        )
        if layer > 0:
            grad_low, projected = lax.optimization_barrier((grad_low, projected))
            mine["qkv"] = in_job(rows_one, projected)
            grad_low = meanwhile(grad_low, mine["gate"])
        gain_grads[layer] = jnp.stack([gain_one, gain_two])
        bias_grads[layer] = jnp.stack([bias_one, bias_two])

    tokens_grad = grad_low[None]
    padded_bias = lax.dynamic_update_slice_in_dim(
        jnp.zeros((LAYERS, 3, qkv_bias.shape[2]), WIDE),
        jnp.stack(qkv_bias_grads),
        lax.axis_index("tensor") * heads_width,
        2,
    )
    small = jnp.concatenate(
        [
            (jnp.stack(gain_grads)).reshape(LAYERS * 2, model),
            (jnp.stack(bias_grads)).reshape(LAYERS * 2, model),
            padded_bias.reshape(LAYERS * 3, qkv_bias.shape[2]),
        ],
        axis=0,
    )
    for axis in ("ctx", "dp", "tensor"):
        for bit in bits_of(lax.axis_size(axis)):
            small = small + swapped(small, axis, bit)
        small, results = lax.optimization_barrier((small, results))
    sums = {k: j.finish() for k, j in grad_jobs[0].items()}
    results = [
        finish_projections(results[0], 0, sums["qkv"]),
        finish_matrix(results[1], 0, sums["out"], "finish_out"),
        finish_gate_up(results[2], 0, sums["gate"], sums["up"]),
        finish_matrix(results[3], 0, sums["down"], "finish_down"),
    ]
    return (
        output,
        tokens_grad,
        small[: LAYERS * 2].reshape(LAYERS, 2, model),
        small[LAYERS * 2 : LAYERS * 4].reshape(LAYERS, 2, model),
        jnp.transpose(results[0], (0, 2, 1, 3)),
        small[LAYERS * 4 :].reshape(LAYERS, 3, qkv_bias.shape[2]),
        *results[1:],
    )


def solution(mesh):
    rows = P("dp", ("ctx", "tensor"), None)
    wide = P(None, "dp", None, "tensor")
    tall = P(None, "tensor", "dp")
    return jax.shard_map(
        shards,
        mesh=mesh,
        in_specs=(rows, rows, P(), P(), wide, P(), tall, wide, tall),
        out_specs=(rows, rows, P(), P(), wide, P(), tall, wide, tall),
        check_vma=False,
    )
```

```python
import functools

import jax
import jax.numpy as jnp
from jax import lax
from jax.experimental import pallas as pl
from jax.experimental.pallas import tpu as pltpu
from jax.sharding import PartitionSpec as P

HD = 64
ROT = 16
LAYERS = 2

MASKED = -1e30
EPSILON = 1e-05
LOW = jnp.bfloat16
WIDE = jnp.float32


def layer_norm_rows(stream, gain, bias):
    row_mean = jnp.mean(stream, axis=-1, keepdims=True)
    centered = stream - row_mean
    inverse = lax.rsqrt(jnp.mean(centered * centered, axis=-1, keepdims=True) + EPSILON)
    unit_rows = centered * inverse
    return (unit_rows * gain + bias, unit_rows, inverse)


def rotary_tables(positions):
    half_rot = ROT // 2
    frequency = 10000.0 ** (-(jnp.arange(half_rot, dtype=jnp.float32) * 2.0) / ROT)
    angles = positions.astype(jnp.float32)[:, None] * frequency[None, :]
    cosine, sine = jnp.cos(angles), jnp.sin(angles)
    rest = jnp.zeros((angles.shape[0], HD - ROT), WIDE)
    none = jnp.zeros_like(sine)
    heads = lambda *parts: jnp.tile(jnp.concatenate(parts, axis=1), (1, PAIR // HD))
    return (
        heads(cosine, cosine, rest + 1.0),
        heads(-sine, none, rest),
        heads(none, sine, rest),
    )


def rotated(flat, cos_ref, right_ref, left_ref):
    shift = ROT // 2
    found = []
    for start in range(0, flat.shape[1], PAIR):
        v = flat[:, start : start + PAIR]
        right, left = pltpu.roll(v, PAIR - shift, 1), pltpu.roll(v, shift, 1)
        found.append(v * cos_ref[...] + right * right_ref[...] + left * left_ref[...])
    return jnp.concatenate(found, axis=1)


def dot(a, b, dims):
    return lax.dot_general(a, b, (dims, ((), ())), preferred_element_type=WIDE)


PAIR = 128


NN = ((1,), (0,))
NT = ((1,), (1,))
TN = ((0,), (0,))


def total_of(terms):
    return functools.reduce(lambda a, b: a + b, terms)


def work(flops):
    return pl.CostEstimate(flops=int(flops), bytes_accessed=0, transcendentals=0)


TILE = 512


def tiled(kernel, name, steps, ins, outs, flops):
    return pl.pallas_call(
        kernel,
        grid=(steps,),
        in_specs=[pl.BlockSpec(block, index) for _, block, index in ins],
        out_specs=[pl.BlockSpec(block, index) for _, block, index in outs],
        out_shape=[shape for shape, _, _ in outs],
        compiler_params=pltpu.CompilerParams(vmem_limit_bytes=48 * 1024 * 1024),
        cost_estimate=work(2.5 * flops),
        name=name,
    )(*[array for array, _, _ in ins])


def whole_block(array):
    return (array, array.shape, lambda i: (0,) * array.ndim)


def column_block(array):
    return (array, (array.shape[0], TILE), lambda i: (0, i))


def row_block(array):
    return (array, (TILE, array.shape[1]), lambda i: (i, 0))


def gate_up_kernel(rows_ref, gate_w_ref, up_w_ref, gate_ref, up_ref, activated_ref):
    rows = rows_ref[...]
    gate = dot(rows, gate_w_ref[...], NN)
    up = dot(rows, up_w_ref[...], NN)
    gate_ref[...] = gate
    up_ref[...] = up
    activated_ref[...] = (gate * jax.nn.sigmoid(gate) * up).astype(LOW)


def gate_up_rows(rows, gate_weight, up_weight):
    count, hidden = rows.shape[0], gate_weight.shape[1]
    shapes = [jax.ShapeDtypeStruct((count, hidden), t) for t in (WIDE, WIDE, LOW)]
    return tiled(
        gate_up_kernel,
        "gate_up",
        pl.cdiv(hidden, TILE),
        [whole_block(rows), column_block(gate_weight), column_block(up_weight)],
        [column_block(s) for s in shapes],
        4 * rows.size * hidden,
    )


def back_sum(rows, weight_ref):
    width = weight_ref.shape[2]
    return total_of(
        dot(rows[:, r * width : (r + 1) * width], weight_ref[r], NT)
        for r in range(weight_ref.shape[0])
    )


def tall_block(array):
    return (array, (array.shape[0], TILE, array.shape[2]), lambda i: (0, i, 0))


def gate_up_back_kernel(rows_ref, weight_ref, gate_ref, up_ref, grad_gate_ref, grad_up_ref):
    grad = back_sum(rows_ref[...], weight_ref)
    gate, up = gate_ref[...], up_ref[...]
    s = jax.nn.sigmoid(gate)
    grad_gate_ref[...] = (grad * up * s * (1.0 + gate * (1.0 - s))).astype(LOW)
    grad_up_ref[...] = (grad * (gate * s)).astype(LOW)


def gate_up_back(rows, down_weight, gate, up):
    count, hidden = gate.shape
    shape = jax.ShapeDtypeStruct((count, hidden), LOW)
    return tiled(
        gate_up_back_kernel,
        "gate_up_back",
        pl.cdiv(hidden, TILE),
        [whole_block(rows), tall_block(down_weight), column_block(gate), column_block(up)],
        [column_block(shape)] * 2,
        2 * rows.size * hidden,
    )


def out_back_kernel(rows_ref, weight_ref, out_ref):
    out_ref[...] = back_sum(rows_ref[...], weight_ref).astype(LOW)


def out_back(rows, weight):
    shape = jax.ShapeDtypeStruct((rows.shape[0], weight.shape[1]), LOW)
    return tiled(
        out_back_kernel,
        "out_back",
        shape.shape[1] // TILE,
        [whole_block(rows), tall_block(weight)],
        [column_block(shape)],
        2 * rows.size * shape.shape[1],
    )[0]


def wide_kernel(rows_ref, weight_ref, out_ref):
    out_ref[...] = dot(rows_ref[...], weight_ref[0], NN).astype(LOW)


def times_wide(rows, weight, name):
    blocks, depth, width = weight.shape
    per = width // TILE
    shape = jax.ShapeDtypeStruct((rows.shape[0], blocks * width), LOW)
    return tiled(
        wide_kernel,
        name,
        blocks * per,
        [whole_block(rows), (weight, (1, depth, TILE), lambda i: (i // per, 0, i % per))],
        [column_block(shape)],
        2 * rows.size * blocks * width,
    )[0]


def gate_up_in_kernel(gate_ref, up_ref, gate_w_ref, up_w_ref, out_ref):
    total = dot(gate_ref[...], gate_w_ref[...], NT) + dot(up_ref[...], up_w_ref[...], NT)
    out_ref[...] = total.astype(LOW)


def gate_up_in(grad_gate, grad_up, gate_weight, up_weight):
    shape = jax.ShapeDtypeStruct((grad_gate.shape[0], gate_weight.shape[0]), LOW)
    return tiled(
        gate_up_in_kernel,
        "gate_up_in",
        shape.shape[1] // TILE,
        [whole_block(grad_gate), whole_block(grad_up), row_block(gate_weight), row_block(up_weight)],
        [column_block(shape)],
        4 * grad_gate.size * shape.shape[1],
    )[0]


def project_in_kernel(rows_ref, weight_ref, out_ref):
    width = weight_ref.shape[3]
    out_ref[...] = total_of(
        dot(rows_ref[:, c * width : (c + 1) * width], weight_ref[0, c], NT) for c in range(3)
    ).astype(LOW)


def project_in(rows, weight):
    blocks, three, depth, width = weight.shape
    per = depth // TILE
    shape = jax.ShapeDtypeStruct((rows.shape[0], blocks * depth), LOW)
    return tiled(
        project_in_kernel,
        "project_in",
        blocks * per,
        [whole_block(rows), (weight, (1, three, TILE, width), lambda i: (i // per, 0, i % per, 0))],
        [column_block(shape)],
        2 * rows.size * blocks * depth,
    )[0]


def outer_kernel(a_ref, b_ref, out_ref):
    out_ref[...] = dot(a_ref[...], b_ref[...], TN).astype(LOW)


def outer(a, b):
    shape = jax.ShapeDtypeStruct((a.shape[1], b.shape[1]), LOW)
    return tiled(
        outer_kernel,
        "outer",
        pl.cdiv(a.shape[1], TILE),
        [column_block(a), whole_block(b)],
        [row_block(shape)],
        a.size * b.shape[1] * 0.8,
    )[0]


def project_kernel(rows_ref, weight_ref, bias_ref, cos_ref, right_ref, left_ref, q_ref, kv_ref):
    blocks, _, depth, width = weight_ref.shape
    flat = dot(rows_ref[...], weight_ref[...].reshape(blocks * depth, width), NN) + bias_ref[0]
    step = pl.program_id(0)

    @pl.when(step == 0)
    def _():
        kv_ref[...] = rotated(flat, cos_ref, right_ref, left_ref).astype(LOW)

    @pl.when(step == 1)
    def _():
        kv_ref[...] = flat.astype(LOW)

    @pl.when(step == 2)
    def _():
        q_ref[...] = rotated(flat, cos_ref, right_ref, left_ref).astype(LOW)


def project(rows, weight, bias, tables):
    count = rows.shape[0]
    blocks, _, depth, width = weight.shape
    fixed = lambda i: (0, 0)
    shapes = [jax.ShapeDtypeStruct((k * count, width), LOW) for k in (1, 2)]
    return tiled(
        project_kernel,
        "project",
        3,
        [
            whole_block(rows),
            (weight, (blocks, 1, depth, width), lambda i: (0, (i + 1) % 3, 0, 0)),
            (bias[:, None, :], (1, 1, width), lambda i: ((i + 1) % 3, 0, 0)),
        ]
        + [(t, (count, PAIR), fixed) for t in tables],
        [
            (shapes[0], (count, width), fixed),
            (shapes[1], (count, width), lambda i: (jnp.minimum(i, 1), 0)),
        ],
        6 * rows.size * width,
    )


def project_back_kernel(far, dq_ref, dkv_ref, *refs):
    far_refs = refs[:far]
    cos_ref, right_ref, left_ref, out_ref, sum_ref = refs[far:]
    step = pl.program_id(0)

    def put(value):
        out_ref[...] = value.astype(LOW)
        sum_ref[0] = jnp.sum(value, axis=0, keepdims=True)

    def key_value():
        return total_of([dkv_ref[...]] + [r[...].astype(WIDE) for r in far_refs])

    @pl.when(step == 0)
    def _():
        put(rotated(dq_ref[...], cos_ref, right_ref, left_ref))

    @pl.when(step == 1)
    def _():
        put(rotated(key_value(), cos_ref, right_ref, left_ref))

    @pl.when(step == 2)
    def _():
        put(key_value())


def project_back(dq, dkv, far, tables):
    count, width = dq.shape
    fixed = lambda i: (0, 0)
    lower = pl.BlockSpec((count, width), lambda i: (jnp.maximum(i - 1, 0), 0))
    out, sums = pl.pallas_call(
        functools.partial(project_back_kernel, len(far)),
        grid=(3,),
        in_specs=[pl.BlockSpec((count, width), fixed)]
        + [lower] * (1 + len(far))
        + [pl.BlockSpec((count, PAIR), fixed)] * 3,
        out_specs=[
            pl.BlockSpec((count, width), lambda i: (0, i)),
            pl.BlockSpec((1, 1, width), lambda i: (i, 0, 0)),
        ],
        out_shape=[
            jax.ShapeDtypeStruct((count, 3 * width), LOW),
            jax.ShapeDtypeStruct((3, 1, width), WIDE),
        ],
        compiler_params=pltpu.CompilerParams(vmem_limit_bytes=32 * 1024 * 1024),
        cost_estimate=work(14000 * count * width),
        name="project_back",
    )(dq, dkv, *far, *tables)
    return out, sums[:, 0]


def attend_near_kernel(qpos_ref, kpos_ref, q_ref, key_ref, value_ref, acc_ref, top_ref, total_ref):
    allowed = kpos_ref[0] <= qpos_ref[...]
    for half in range(PAIR // HD):
        lanes = slice(half * HD, (half + 1) * HD)
        q = q_ref[:, lanes] * jnp.asarray(HD**-0.5, LOW)
        s = jnp.where(allowed, dot(q, key_ref[:, lanes], NT), MASKED)
        top = jnp.max(s, axis=1, keepdims=True)
        p = jnp.exp(s - top)
        spread = (top.shape[0], HD)
        top_ref[:, lanes] = jnp.broadcast_to(top, spread)
        total_ref[:, lanes] = jnp.broadcast_to(jnp.sum(p, axis=1, keepdims=True), spread)
        acc_ref[:, lanes] = dot(p.astype(LOW), value_ref[:, lanes], NN)


def attend_far_kernel(blocks, qpos_ref, kpos_ref, q_ref, acc_in_ref, top_in_ref, total_in_ref, *refs):
    keys, values = refs[: 2 * blocks : 2], refs[1 : 2 * blocks : 2]
    out_ref, lse_ref = refs[2 * blocks :]
    allowed = [kpos_ref[b] <= qpos_ref[...] for b in range(blocks)]
    for half in range(PAIR // HD):
        lanes = slice(half * HD, (half + 1) * HD)
        q = q_ref[:, lanes] * jnp.asarray(HD**-0.5, LOW)
        first = slice(half * HD, half * HD + 1)
        top, total, acc = top_in_ref[:, first], total_in_ref[:, first], acc_in_ref[:, lanes]
        for b in range(blocks):
            s = jnp.where(allowed[b], dot(q, keys[b][:, lanes], NT), MASKED)
            new_top = jnp.maximum(top, jnp.max(s, axis=1, keepdims=True))
            p = jnp.exp(s - new_top)
            factor = jnp.exp(top - new_top)
            total = total * factor + jnp.sum(p, axis=1, keepdims=True)
            acc = acc * factor + dot(p.astype(LOW), values[b][:, lanes], NN)
            top = new_top
        out_ref[:, lanes] = acc / total
        lse_ref[:, lanes] = jnp.broadcast_to(top + jnp.log(total), acc.shape)


def pair_call(kernel, name, rows, width, kpos, operands, stacked, outs, flops):
    blocks, _, key_rows = kpos.shape
    column = lambda i: (0, i)
    specs = {
        "row": pl.BlockSpec((rows, PAIR), column),
        "keys": pl.BlockSpec((2 * key_rows, PAIR), column),
    }
    shapes = {"row": (rows, width), "keys": (2 * key_rows, width)}
    halves = [pl.BlockSpec((key_rows, PAIR), lambda i, c=c: (c, i)) for c in range(2)]
    common = [
        pl.BlockSpec((rows, 1), lambda i: (0, 0)),
        pl.BlockSpec((blocks, 1, key_rows), lambda i: (0, 0, 0)),
    ]
    return pl.pallas_call(
        kernel,
        grid=(width // PAIR,),
        in_specs=common + [specs["row"]] * (len(operands) - 1) + halves * len(stacked),
        out_specs=[specs[k] for k, _ in outs],
        out_shape=[jax.ShapeDtypeStruct(shapes[k], t) for k, t in outs],
        compiler_params=pltpu.CompilerParams(vmem_limit_bytes=40 * 1024 * 1024),
        cost_estimate=work(flops * rows * key_rows * blocks * width),
        name=name,
    )(operands[0], kpos, *operands[1:], *[s for s in stacked for c in range(2)])


def attend_near(qpos, kpos, q, own):
    rows, width = q.shape
    outs = [("row", WIDE)] * 3
    return pair_call(attend_near_kernel, "attend_near", rows, width, kpos, [qpos, q], [own], outs, 43)


def attend_far(qpos, kpos, q, near, far):
    rows, width = q.shape
    return pair_call(
        functools.partial(attend_far_kernel, len(far)),
        "attend_far",
        rows,
        width,
        kpos,
        [qpos, q, *near],
        far,
        [("row", WIDE)] * 2,
        43,
    )


def attend_back_kernel(blocks, more, qpos_ref, kpos_ref, q_ref, grad_ref, out_ref, lse_ref, *refs):
    before, refs = refs[:more], refs[more:]
    keys, values = refs[: 2 * blocks : 2], refs[1 : 2 * blocks : 2]
    dq_ref = refs[2 * blocks]
    dboth = refs[2 * blocks + 1 :]
    key_rows = keys[0].shape[0]
    allowed = [kpos_ref[b] <= qpos_ref[...] for b in range(blocks)]
    scale = HD**-0.5
    for half in range(PAIR // HD):
        lanes = slice(half * HD, (half + 1) * HD)
        q = q_ref[:, lanes] * jnp.asarray(scale, LOW)
        grad = grad_ref[:, lanes]
        lse = lse_ref[:, half * HD : half * HD + 1]
        delta = jnp.sum(grad.astype(WIDE) * out_ref[:, lanes], axis=1, keepdims=True)
        dq = []
        for b in range(blocks):
            k = keys[b][:, lanes]
            s = jnp.where(allowed[b], dot(q, k, NT), MASKED)
            p = jnp.exp(s - lse)
            dp = dot(grad, values[b][:, lanes], NT)
            ds = (p * (dp - delta)).astype(LOW)
            kind = dboth[b].dtype
            dboth[b][key_rows:, lanes] = dot(p.astype(LOW), grad, TN).astype(kind)
            dboth[b][:key_rows, lanes] = dot(ds, q, TN).astype(kind)
            dq.append(dot(ds, k, NN))
        dq_ref[:, lanes] = total_of([total_of(dq) * scale] + [r[:, lanes] for r in before])


def attend_back(qpos, kpos, q, grad, out, lse, stacked, kind, before):
    rows, width = q.shape
    results = pair_call(
        functools.partial(attend_back_kernel, len(stacked), len(before)),
        "attend_back",
        rows,
        width,
        kpos,
        [qpos, q, grad, out, lse, *before],
        stacked,
        [("row", WIDE)] + [("keys", kind)] * len(stacked),
        75,
    )
    return results[0], results[1:]


def norm_back_kernel(count, *refs):
    terms = refs[:count]
    unit_ref, inverse_ref, gain_ref, base_ref = refs[count : count + 4]
    grad_ref, low_ref, gain_out_ref, bias_out_ref = refs[count + 4 :]
    grad_rows = total_of([t[...].astype(WIDE) for t in terms])
    unit = unit_ref[...]
    grad_unit = grad_rows * gain_ref[...]
    first_mean = jnp.mean(grad_unit, axis=-1, keepdims=True)
    second_mean = jnp.mean(grad_unit * unit, axis=-1, keepdims=True)
    total = base_ref[...] + inverse_ref[...] * (grad_unit - first_mean - unit * second_mean)
    grad_ref[...] = total
    low_ref[...] = total.astype(LOW)
    gain_out_ref[...] = jnp.sum(grad_rows * unit, axis=0, keepdims=True)
    bias_out_ref[...] = jnp.sum(grad_rows, axis=0, keepdims=True)


def norm_back(terms, unit, inverse, gain, base):
    rows, model = unit.shape
    fixed = lambda i: (0, 0)
    line = (1, model)
    operands = [*terms, unit, inverse, gain[None], base]
    shapes = [(rows, model)] * (len(terms) + 1) + [(rows, 1), line, (rows, model)]
    outs = [((rows, model), WIDE), ((rows, model), LOW), (line, WIDE), (line, WIDE)]
    results = tiled(
        functools.partial(norm_back_kernel, len(terms)),
        "norm_back",
        1,
        [(o, s, fixed) for o, s in zip(operands, shapes)],
        [(jax.ShapeDtypeStruct(s, t), s, fixed) for s, t in outs],
        1e9,
    )
    return results[0], results[1], results[2][0], results[3][0]


def finish(buffer, layer, terms, make, steps, ins, out, name):
    shape, block, place = out

    def kernel(*refs):
        refs[-1][...] = make(*[r[...].astype(WIDE) for r in refs[: len(terms)]])

    operands = list(terms)
    specs = [pl.BlockSpec(b, index) for b, index in ins]
    if buffer is not None:
        operands.append(buffer)
        specs.append(pl.BlockSpec(memory_space=pl.ANY))
    return pl.pallas_call(
        kernel,
        grid=(steps,),
        in_specs=specs,
        out_specs=pl.BlockSpec((1,) + block, lambda i: (layer,) + place(i)),
        out_shape=jax.ShapeDtypeStruct(shape, WIDE),
        input_output_aliases={} if buffer is None else {len(terms): 0},
        compiler_params=pltpu.CompilerParams(vmem_limit_bytes=48 * 1024 * 1024),
        cost_estimate=work(1e9),
        name=name,
    )(*operands)


def finish_matrix(buffer, layer, terms, name):
    rows, columns = terms[0].shape
    block = (rows // 4, columns)
    place = lambda i: (i, 0)
    out = ((LAYERS, rows, columns), block, place)
    make = lambda *t: total_of(t)[None]
    return finish(buffer, layer, terms, make, 4, [(block, place)] * len(terms), out, name)


def finish_projections(buffer, layer, terms):
    rows, columns = terms[0].shape
    width = columns // 3
    out = ((LAYERS, 3, rows, width), (1, rows, width), lambda i: (i, 0, 0))
    make = lambda *t: total_of(t)[None, None]
    ins = [((rows, width), lambda i: (0, i))] * len(terms)
    return finish(buffer, layer, terms, make, 3, ins, out, "finish_qkv")


def finish_gate_up(buffer, layer, gate_terms, up_terms):
    rows, columns = gate_terms[0].shape
    steps = 8
    block = (rows // steps, columns)
    out = ((LAYERS, rows, 2, columns), (rows // steps, 2, columns), lambda i: (i, 0, 0))
    count = len(gate_terms)
    make = lambda *t: jnp.stack([total_of(t[:count]), total_of(t[count:])], axis=1)[None]
    ins = [(block, lambda i: (i, 0))] * (2 * count)
    return finish(buffer, layer, gate_terms + up_terms, make, steps, ins, out, "finish_gate_up")


def bits_of(count):
    return [1 << k for k in range(count.bit_length() - 1)]


def swapped(value, axis, mask):
    count = lax.axis_size(axis)
    return lax.ppermute(value, axis, [(i, i ^ mask) for i in range(count)])


def joined(pieces, axis):
    return pieces[0] if len(pieces) == 1 else jnp.concatenate(pieces, axis=axis)


class Line:
    def __init__(self, own_rows):
        n_tensor, n_ctx = lax.axis_size("tensor"), lax.axis_size("ctx")
        tensor, ctx = lax.axis_index("tensor"), lax.axis_index("ctx")
        self.count, self.tensor = n_tensor, tensor
        row = jnp.arange(own_rows, dtype=jnp.int32)
        chip = (tensor + jnp.arange(n_tensor, dtype=jnp.int32)) % n_tensor
        place = (chip[:, None] * own_rows + row[None, :]).reshape(-1)
        block = n_tensor * own_rows
        self.places = ctx * block + place
        self.far_places = [
            jnp.where(ctx >= s, (ctx - s) * block + place, 1 << 30) for s in range(1, n_ctx)
        ]
        self.own_rows = own_rows

    def gather_rows(self, low):
        count, t = self.count, self.tensor
        send = lambda v, *route: lax.ppermute(v, "tensor", list(route))
        if count == 4:
            far = send(low, (0, 2), (2, 0), (1, 3), (3, 1))
            above = send(low, (0, 1), (1, 2), (2, 3))
            below = send(low, (1, 0), (2, 1), (3, 2))
            end = send(far, (2, 3), (1, 0))
            found = [low, jnp.where(t == 3, end, below), far, jnp.where(t == 0, end, above)]
        else:
            found = [low] + [
                send(low, *[((i + d) % count, i) for i in range(count)]) for d in range(1, count)
            ]
        return jnp.concatenate(found, axis=0)

    def sum_rows(self, low, *jobs):
        rows, count, t = self.own_rows, self.count, self.tensor
        terms = [low[d * rows : (d + 1) * rows] for d in range(count)]
        send = lambda v, *route: lax.ppermute(v, "tensor", list(route))
        wide = lambda v: v.astype(WIDE)
        if count == 4:
            end = send(jnp.where(t == 0, terms[3], terms[1]), (0, 1), (3, 2))
            above = send(terms[1], (0, 1), (1, 2), (2, 3))
            below = send(terms[3], (3, 2), (2, 1), (1, 0))
            far = meanwhile((wide(terms[2]) + wide(end)).astype(LOW), *jobs)
            got = [send(far, (0, 2), (2, 0), (1, 3), (3, 1)), above, below]
        else:
            got = [
                send(terms[d], *[(i, (i + d) % count) for i in range(count)])
                for d in range(1, count)
            ]
        return (low, *got)

    def sum_of(self, terms):
        return total_of([terms[0][: self.own_rows].astype(WIDE)] + [t.astype(WIDE) for t in terms[1:]])

    def owner(self, low):
        count = lax.axis_size("ctx")
        if count != 2:
            return (lax.psum(low, "ctx") if count > 1 else low,)
        got = yield swapped(low, "ctx", 1)
        return (low, got)

    def far_keys(self, value):
        count = lax.axis_size("ctx")
        return [
            lax.ppermute(value, "ctx", [(i, i + s) for i in range(count - s)])
            for s in range(1, count)
        ]

    def far_key_grads(self, values):
        count = lax.axis_size("ctx")
        return [
            lax.ppermute(values[s - 1], "ctx", [(i + s, i) for i in range(count - s)])
            for s in range(1, count)
        ]


def weight_stages(shard):
    shard = yield shard
    return (yield lax.all_gather(shard, "dp"))


def grad_stages(plan, value, axis):
    got = yield lax.psum_scatter(value.astype(LOW), "dp", scatter_dimension=axis, tiled=True)
    return (yield from plan.owner(got))


def low_first(count):
    width = count.bit_length() - 1
    return sorted(range(count), key=lambda r: int(format(r, "b").zfill(width)[::-1] or "0", 2))


def pair_stages(plan, terms_of, axis):
    count = lax.axis_size("dp")

    def term(parts):
        factors = [terms_of(r) for r in parts]
        a = joined([f[0] for f in factors], 1) if axis == 0 else factors[0][0]
        b = joined([f[1] for f in factors], 1) if axis == 1 else factors[0][1]
        return outer(a, b)

    order = low_first(count)
    kept = None
    for bit in bits_of(count):
        if kept is None:
            sent = yield term(order[count // 2 :])
        else:
            kept, sent = jnp.split(kept, 2, axis=axis)
        got = yield swapped(sent.astype(LOW), "dp", bit)
        kept = (term(order[: count // 2]).astype(WIDE) if kept is None else kept) + got.astype(WIDE)
    return (yield from plan.owner(kept.astype(LOW)))


class Job:
    def __init__(self, stages):
        self.stages, self.value, self.result, self.done = stages, None, None, False
        self.advance(None)

    def advance(self, value):
        try:
            self.value = self.stages.send(value)
        except StopIteration as end:
            self.done, self.result, self.value = True, end.value, None

    def finish(self):
        while not self.done:
            self.advance(self.value)
        return self.result


def meanwhile(value, *jobs):
    open_jobs = [j for j in jobs if j is not None and not j.done]
    if not open_jobs:
        return value
    value, held = lax.optimization_barrier((value, tuple(j.value for j in open_jobs)))
    for job, got in zip(open_jobs, held):
        job.advance(got)
    return value


def held(value, *jobs):
    open_jobs = [j for j in jobs if j is not None and not j.done]
    if not open_jobs:
        return value
    value, kept = lax.optimization_barrier((value, tuple(j.value for j in open_jobs)))
    for job, got in zip(open_jobs, kept):
        job.value = got
    return value


def shards(
    tokens,
    cotangent,
    norm_gains,
    norm_biases,
    qkv_weight,
    qkv_bias,
    out_weight,
    gate_up_weight,
    down_weight,
):
    own_rows = tokens.shape[1]
    model = tokens.shape[2]
    heads_width = qkv_weight.shape[3]
    plan = Line(own_rows)
    tables = rotary_tables(plan.places)
    tables_back = (tables[0], -tables[1], -tables[2])
    qpos = plan.places[:, None]
    near_places = plan.places[None, None, :]
    far_places = jnp.stack(plan.far_places)[:, None, :]
    gains = (norm_gains)
    biases = (norm_biases)
    qkv_bias_own = lax.dynamic_slice_in_dim(qkv_bias, lax.axis_index("tensor") * heads_width, heads_width, 2)

    def weight_jobs(layer, after):
        (qkv_all, out_all, gate_up_all, down_all), after = lax.optimization_barrier(
            ((qkv_weight, out_weight, gate_up_weight, down_weight), after)
        )
        matrices = {
            "qkv": jnp.transpose(qkv_all[layer], (1, 0, 2)),
            "out": out_all[layer],
            "gate": gate_up_all[layer, :, 0],
            "up": gate_up_all[layer, :, 1],
            "down": down_all[layer],
        }
        return {n: Job(weight_stages(v)) for n, v in matrices.items()}, after

    now, unused = weight_jobs(0, ())
    for name in ("qkv", "out", "gate", "up"):
        now[name].advance(now[name].value)
    stream = tokens[0].astype(WIDE)
    later = {}
    saved = []
    for layer in range(LAYERS):
        last = layer + 1 == LAYERS
        normed_one, unit_one, inverse_one = layer_norm_rows(
            stream, gains[layer, 0], biases[layer, 0]
        )
        rows_one = plan.gather_rows(normed_one.astype(LOW))
        if layer == 0:
            rows_one = meanwhile(rows_one, now["qkv"], now["down"])
        else:
            rows_one = meanwhile(rows_one, now["out"], now["gate"], now["down"])
        qkv_full = now["qkv"].finish()
        queries, keys_values = project(rows_one, qkv_full, qkv_bias_own[layer], tables)
        if layer == 0:
            late_cotangent, queries = lax.optimization_barrier((cotangent[0], queries))
            grad_stream = late_cotangent.astype(WIDE)
            branch = plan.gather_rows(late_cotangent)
        prepared = {}
        if not last:
            prepared, queries = weight_jobs(layer + 1, queries)
        far_kv = plan.far_keys(keys_values)
        near = attend_near(qpos, near_places, queries, keys_values)
        attended, lse = attend_far(qpos, far_places, queries, near, far_kv)
        attended_low = meanwhile(attended.astype(LOW), now["out"])
        attended_low = held(attended_low, *map(prepared.get, ("gate", "up")))
        if layer == 0:
            attended_low, branch = lax.optimization_barrier((attended_low, branch))
        else:
            attended_low = meanwhile(attended_low, now["up"])
        out_full = now["out"].finish()
        mid = stream + plan.sum_of(plan.sum_rows(times_wide(attended_low, out_full, "out")))
        mid = meanwhile(mid, now["gate"])
        if layer > 0:
            mid = meanwhile(mid, now["down"])
        else:
            later = prepared
        normed_two, unit_two, inverse_two = layer_norm_rows(mid, gains[layer, 1], biases[layer, 1])
        rows_two = plan.gather_rows(normed_two.astype(LOW))
        rows_two = meanwhile(rows_two, now["up"], now["down"], later.get("qkv"))
        flat = lambda v: v.reshape(v.shape[0] * v.shape[1], v.shape[2])
        gate_full, up_full = flat(now["gate"].finish()), flat(now["up"].finish())
        gate, up, activated = gate_up_rows(rows_two, gate_full, up_full)
        activated = meanwhile(activated, later.get("out"), later.get("gate"))
        down_full = now["down"].finish()
        if not last:
            stream = mid + plan.sum_of(
                plan.sum_rows(times_wide(activated, down_full, "down"))
            )
            stream = meanwhile(stream, later.get("qkv"), later.get("up"))
        saved.append(
            (
                (qkv_full, out_full, gate_full, up_full, down_full),
                (rows_one, unit_one, inverse_one),
                (queries, keys_values, far_kv, attended, attended_low, lse),
                (rows_two, unit_two, inverse_two),
                (gate, up, activated),
            )
        )
        now = later
    grad_jobs = [None] * LAYERS
    gain_grads = [None] * LAYERS
    bias_grads = [None] * LAYERS
    qkv_bias_grads = [None] * LAYERS
    for layer in range(LAYERS - 1, -1, -1):
        (
            (qkv_full, out_full, gate_full, up_full, down_full),
            (rows_one, unit_one, inverse_one),
            (queries, keys_values, far_kv, attended, attended_low, lse),
            (rows_two, unit_two, inverse_two),
            (gate, up, activated),
        ) = saved[layer]
        mine = {}
        grad_jobs[layer] = mine
        above = grad_jobs[layer + 1] if layer + 1 < LAYERS else {}
        old = lambda *keys: [above.get(k) for k in keys]

        def own_part(value, r):
            index = lax.axis_index("dp") ^ r
            width = value.shape[1] // lax.axis_size("dp")
            return lax.dynamic_slice_in_dim(value, index * width, width, 1)

        def in_job(a, b):
            return Job(grad_stages(plan, outer(a, b), 0))

        def out_job(a, b):
            return Job(grad_stages(plan, outer(a, b), 1))

        if layer + 1 < LAYERS:
            branch = plan.gather_rows(grad_low)
        branch = held(meanwhile(branch, *old("gate", "up", "qkv")), *old("out"))
        if layer == 0:
            down_grad, branch = lax.optimization_barrier(
                (outer(activated, branch), branch)
            )
            mine["down"] = Job(grad_stages(plan, down_grad, 1))
        grad_gate, grad_up = gate_up_back(branch, down_full, gate, up)
        partial_in = gate_up_in(grad_gate, grad_up, gate_full, up_full)
        summed = plan.sum_rows(partial_in)
        summed = meanwhile(summed, *old("up", "out", "qkv"))
        hidden_grad, hidden_low, gain_two, bias_two = norm_back(
            summed, unit_two, inverse_two, gains[layer, 1], grad_stream
        )
        hidden_low, (branch, grad_gate, grad_up) = lax.optimization_barrier(
            (hidden_low, (branch, grad_gate, grad_up))
        )
        if layer > 0:
            mine["down"] = out_job(activated, branch)
        mine["gate"] = in_job(rows_two, grad_gate)
        if layer == 0:
            mine["up"] = in_job(rows_two, grad_up)
        top = layer + 1 == LAYERS
        if top:
            late, hidden_low = lax.optimization_barrier((activated, hidden_low))
            partial_out = times_wide(late, down_full, "down")
        attention = plan.gather_rows(hidden_low)
        attention = meanwhile(attention, *old("out", "qkv"))
        if layer == 0:
            attention = meanwhile(attention, mine["down"])
        if top:
            attention, partial_out = lax.optimization_barrier((attention, partial_out))
            output = (mid + plan.sum_of(plan.sum_rows(partial_out))).astype(LOW)[None]
        grad_attended = out_back(attention, out_full)
        shared = (queries, grad_attended, attended, lse)
        far_queries, far_grads = attend_back(qpos, far_places, *shared, far_kv, LOW, [])
        if layer == 0:
            far_queries = meanwhile(far_queries, mine["down"])
        returned = plan.far_key_grads(far_grads)
        grad_queries, grad_kv = attend_back(
            qpos, near_places, *shared, [keys_values], WIDE, [far_queries]
        )
        if top:
            grad_queries, output = lax.optimization_barrier((grad_queries, output))
        projected, qkv_bias_grads[layer] = project_back(
            grad_queries, grad_kv[0], returned, tables_back
        )
        projected, (attention, grad_up) = lax.optimization_barrier(
            (projected, (attention, grad_up))
        )
        if layer > 0:
            mine["up"] = in_job(rows_two, grad_up)
        mine["out"] = Job(
            pair_stages(plan, lambda r, a=attention: (attended_low, own_part(a, r)), 1)
        )
        if layer > 0:
            mine["up"] = in_job(rows_two, grad_up)
        projected = meanwhile(projected, mine["out"])
        projected = meanwhile(projected, mine["down"] if layer > 0 else None, *old("qkv"))
        if not top:
            above_done, projected = lax.optimization_barrier(
                ({k: j.finish() for k, j in above.items()}, projected)
            )
            sums = above_done
            results = [
                finish_projections(None, layer + 1, sums["qkv"]),
                finish_matrix(None, layer + 1, sums["out"], "finish_out"),
                finish_gate_up(None, layer + 1, sums["gate"], sums["up"]),
                finish_matrix(None, layer + 1, sums["down"], "finish_down"),
            ]
        if layer == 0:
            mine["qkv"] = Job(
                pair_stages(plan, lambda r, b=projected: (own_part(rows_one, r), b), 0)
            )
            projected = meanwhile(projected, mine["qkv"], mine["gate"])
        partial_in = project_in(projected, qkv_full)
        if layer == 0:
            partial_in = held(meanwhile(partial_in, mine["qkv"]), mine["out"])
            summed = plan.sum_rows(partial_in, mine["up"])
        else:
            summed = plan.sum_rows(partial_in)
        if layer > 0:
            summed = meanwhile(summed, mine["down"], mine["out"])
        else:
            summed = meanwhile(summed, *map(mine.get, ("gate", "out", "qkv")))
        grad_stream, grad_low, gain_one, bias_one = norm_back(
            summed, unit_one, inverse_one, gains[layer, 0], hidden_grad
        )
        if layer > 0:
            grad_low, projected = lax.optimization_barrier((grad_low, projected))
            mine["qkv"] = Job(
                pair_stages(plan, lambda r, a=rows_one, b=projected: (own_part(a, r), b), 0)
            )
            grad_low = meanwhile(grad_low, mine["gate"], mine["qkv"])
        gain_grads[layer] = jnp.stack([gain_one, gain_two])
        bias_grads[layer] = jnp.stack([bias_one, bias_two])

    tokens_grad = grad_low[None]
    padded_bias = lax.dynamic_update_slice_in_dim(
        jnp.zeros((LAYERS, 3, qkv_bias.shape[2]), WIDE),
        jnp.stack(qkv_bias_grads),
        lax.axis_index("tensor") * heads_width,
        2,
    )
    small = jnp.concatenate(
        [
            (jnp.stack(gain_grads)).reshape(LAYERS * 2, model),
            (jnp.stack(bias_grads)).reshape(LAYERS * 2, model),
            padded_bias.reshape(LAYERS * 3, qkv_bias.shape[2]),
        ],
        axis=0,
    )
    for axis in ("ctx", "dp", "tensor"):
        for bit in bits_of(lax.axis_size(axis)):
            small = small + swapped(small, axis, bit)
        small, results = lax.optimization_barrier((small, results))
    sums = {k: j.finish() for k, j in grad_jobs[0].items()}
    results = [
        finish_projections(results[0], 0, sums["qkv"]),
        finish_matrix(results[1], 0, sums["out"], "finish_out"),
        finish_gate_up(results[2], 0, sums["gate"], sums["up"]),
        finish_matrix(results[3], 0, sums["down"], "finish_down"),
    ]
    return (
        output,
        tokens_grad,
        small[: LAYERS * 2].reshape(LAYERS, 2, model),
        small[LAYERS * 2 : LAYERS * 4].reshape(LAYERS, 2, model),
        jnp.transpose(results[0], (0, 2, 1, 3)),
        small[LAYERS * 4 :].reshape(LAYERS, 3, qkv_bias.shape[2]),
        *results[1:],
    )


def solution(mesh):
    rows = P("dp", ("ctx", "tensor"), None)
    wide = P(None, "dp", None, "tensor")
    tall = P(None, "tensor", "dp")
    return jax.shard_map(
        shards,
        mesh=mesh,
        in_specs=(rows, rows, P(), P(), wide, P(), tall, wide, tall),
        out_specs=(rows, rows, P(), P(), wide, P(), tall, wide, tall),
        check_vma=False,
    )
```

```python
import functools

import jax
import jax.numpy as jnp
from jax import lax
from jax.experimental import pallas as pl
from jax.experimental.pallas import tpu as pltpu
from jax.sharding import PartitionSpec as P

HD = 64
ROT = 16
LAYERS = 2

MASKED = -1e30
EPSILON = 1e-05
LOW = jnp.bfloat16
WIDE = jnp.float32


def layer_norm_rows(stream, gain, bias):
    row_mean = jnp.mean(stream, axis=-1, keepdims=True)
    centered = stream - row_mean
    inverse = lax.rsqrt(jnp.mean(centered * centered, axis=-1, keepdims=True) + EPSILON)
    unit_rows = centered * inverse
    return (unit_rows * gain + bias, unit_rows, inverse)


def rotary_tables(positions):
    half_rot = ROT // 2
    frequency = 10000.0 ** (-(jnp.arange(half_rot, dtype=jnp.float32) * 2.0) / ROT)
    angles = positions.astype(jnp.float32)[:, None] * frequency[None, :]
    cosine, sine = jnp.cos(angles), jnp.sin(angles)
    rest = jnp.zeros((angles.shape[0], HD - ROT), WIDE)
    none = jnp.zeros_like(sine)
    heads = lambda *parts: jnp.tile(jnp.concatenate(parts, axis=1), (1, PAIR // HD))
    return (
        heads(cosine, cosine, rest + 1.0),
        heads(-sine, none, rest),
        heads(none, sine, rest),
    )


def rotated(flat, cos_ref, right_ref, left_ref):
    shift = ROT // 2
    found = []
    for start in range(0, flat.shape[1], PAIR):
        v = flat[:, start : start + PAIR]
        right, left = pltpu.roll(v, PAIR - shift, 1), pltpu.roll(v, shift, 1)
        found.append(v * cos_ref[...] + right * right_ref[...] + left * left_ref[...])
    return jnp.concatenate(found, axis=1)


def dot(a, b, dims):
    return lax.dot_general(a, b, (dims, ((), ())), preferred_element_type=WIDE)


PAIR = 128


NN = ((1,), (0,))
NT = ((1,), (1,))
TN = ((0,), (0,))


def total_of(terms):
    return functools.reduce(lambda a, b: a + b, terms)


def work(flops):
    return pl.CostEstimate(flops=int(flops), bytes_accessed=0, transcendentals=0)


TILE = 512


def tiled(kernel, name, steps, ins, outs, flops):
    return pl.pallas_call(
        kernel,
        grid=(steps,),
        in_specs=[pl.BlockSpec(block, index) for _, block, index in ins],
        out_specs=[pl.BlockSpec(block, index) for _, block, index in outs],
        out_shape=[shape for shape, _, _ in outs],
        compiler_params=pltpu.CompilerParams(vmem_limit_bytes=48 * 1024 * 1024),
        cost_estimate=work(2.5 * flops),
        name=name,
    )(*[array for array, _, _ in ins])


def whole_block(array):
    return (array, array.shape, lambda i: (0,) * array.ndim)


def column_block(array):
    return (array, (array.shape[0], TILE), lambda i: (0, i))


def row_block(array):
    return (array, (TILE, array.shape[1]), lambda i: (i, 0))


def gate_up_kernel(rows_ref, gate_w_ref, up_w_ref, gate_ref, up_ref, activated_ref):
    rows = rows_ref[...]
    gate = dot(rows, gate_w_ref[...], NN)
    up = dot(rows, up_w_ref[...], NN)
    gate_ref[...] = gate
    up_ref[...] = up
    activated_ref[...] = (gate * jax.nn.sigmoid(gate) * up).astype(LOW)


def gate_up_rows(rows, gate_weight, up_weight):
    count, hidden = rows.shape[0], gate_weight.shape[1]
    shapes = [jax.ShapeDtypeStruct((count, hidden), t) for t in (WIDE, WIDE, LOW)]
    return tiled(
        gate_up_kernel,
        "gate_up",
        pl.cdiv(hidden, TILE),
        [whole_block(rows), column_block(gate_weight), column_block(up_weight)],
        [column_block(s) for s in shapes],
        4 * rows.size * hidden,
    )


def back_sum(rows, weight_ref):
    width = weight_ref.shape[2]
    return total_of(
        dot(rows[:, r * width : (r + 1) * width], weight_ref[r], NT)
        for r in range(weight_ref.shape[0])
    )


def tall_block(array):
    return (array, (array.shape[0], TILE, array.shape[2]), lambda i: (0, i, 0))


def gate_up_back_kernel(rows_ref, weight_ref, gate_ref, up_ref, grad_gate_ref, grad_up_ref):
    grad = back_sum(rows_ref[...], weight_ref)
    gate, up = gate_ref[...], up_ref[...]
    s = jax.nn.sigmoid(gate)
    grad_gate_ref[...] = (grad * up * s * (1.0 + gate * (1.0 - s))).astype(LOW)
    grad_up_ref[...] = (grad * (gate * s)).astype(LOW)


def gate_up_back(rows, down_weight, gate, up):
    count, hidden = gate.shape
    shape = jax.ShapeDtypeStruct((count, hidden), LOW)
    return tiled(
        gate_up_back_kernel,
        "gate_up_back",
        pl.cdiv(hidden, TILE),
        [whole_block(rows), tall_block(down_weight), column_block(gate), column_block(up)],
        [column_block(shape)] * 2,
        2 * rows.size * hidden,
    )


def out_back_kernel(rows_ref, weight_ref, out_ref):
    out_ref[...] = back_sum(rows_ref[...], weight_ref).astype(LOW)


def out_back(rows, weight):
    shape = jax.ShapeDtypeStruct((rows.shape[0], weight.shape[1]), LOW)
    return tiled(
        out_back_kernel,
        "out_back",
        shape.shape[1] // TILE,
        [whole_block(rows), tall_block(weight)],
        [column_block(shape)],
        2 * rows.size * shape.shape[1],
    )[0]


def wide_kernel(rows_ref, weight_ref, out_ref):
    out_ref[...] = dot(rows_ref[...], weight_ref[0], NN).astype(LOW)


def times_wide(rows, weight, name):
    blocks, depth, width = weight.shape
    per = width // TILE
    shape = jax.ShapeDtypeStruct((rows.shape[0], blocks * width), LOW)
    return tiled(
        wide_kernel,
        name,
        blocks * per,
        [whole_block(rows), (weight, (1, depth, TILE), lambda i: (i // per, 0, i % per))],
        [column_block(shape)],
        2 * rows.size * blocks * width,
    )[0]


def gate_up_in_kernel(gate_ref, up_ref, gate_w_ref, up_w_ref, out_ref):
    total = dot(gate_ref[...], gate_w_ref[...], NT) + dot(up_ref[...], up_w_ref[...], NT)
    out_ref[...] = total.astype(LOW)


def gate_up_in(grad_gate, grad_up, gate_weight, up_weight):
    shape = jax.ShapeDtypeStruct((grad_gate.shape[0], gate_weight.shape[0]), LOW)
    return tiled(
        gate_up_in_kernel,
        "gate_up_in",
        shape.shape[1] // TILE,
        [whole_block(grad_gate), whole_block(grad_up), row_block(gate_weight), row_block(up_weight)],
        [column_block(shape)],
        4 * grad_gate.size * shape.shape[1],
    )[0]


def project_in_kernel(rows_ref, weight_ref, out_ref):
    width = weight_ref.shape[3]
    out_ref[...] = total_of(
        dot(rows_ref[:, c * width : (c + 1) * width], weight_ref[0, c], NT) for c in range(3)
    ).astype(LOW)


def project_in(rows, weight):
    blocks, three, depth, width = weight.shape
    per = depth // TILE
    shape = jax.ShapeDtypeStruct((rows.shape[0], blocks * depth), LOW)
    return tiled(
        project_in_kernel,
        "project_in",
        blocks * per,
        [whole_block(rows), (weight, (1, three, TILE, width), lambda i: (i // per, 0, i % per, 0))],
        [column_block(shape)],
        2 * rows.size * blocks * depth,
    )[0]


def outer_kernel(a_ref, b_ref, out_ref):
    out_ref[...] = dot(a_ref[...], b_ref[...], TN).astype(LOW)


def outer(a, b):
    shape = jax.ShapeDtypeStruct((a.shape[1], b.shape[1]), LOW)
    return tiled(
        outer_kernel,
        "outer",
        pl.cdiv(a.shape[1], TILE),
        [column_block(a), whole_block(b)],
        [row_block(shape)],
        a.size * b.shape[1] * 0.8,
    )[0]


def project_kernel(rows_ref, weight_ref, bias_ref, cos_ref, right_ref, left_ref, q_ref, kv_ref):
    blocks, _, depth, width = weight_ref.shape
    flat = dot(rows_ref[...], weight_ref[...].reshape(blocks * depth, width), NN) + bias_ref[0]
    step = pl.program_id(0)

    @pl.when(step == 0)
    def _():
        kv_ref[...] = rotated(flat, cos_ref, right_ref, left_ref).astype(LOW)

    @pl.when(step == 1)
    def _():
        kv_ref[...] = flat.astype(LOW)

    @pl.when(step == 2)
    def _():
        q_ref[...] = rotated(flat, cos_ref, right_ref, left_ref).astype(LOW)


def project(rows, weight, bias, tables):
    count = rows.shape[0]
    blocks, _, depth, width = weight.shape
    fixed = lambda i: (0, 0)
    shapes = [jax.ShapeDtypeStruct((k * count, width), LOW) for k in (1, 2)]
    return tiled(
        project_kernel,
        "project",
        3,
        [
            whole_block(rows),
            (weight, (blocks, 1, depth, width), lambda i: (0, (i + 1) % 3, 0, 0)),
            (bias[:, None, :], (1, 1, width), lambda i: ((i + 1) % 3, 0, 0)),
        ]
        + [(t, (count, PAIR), fixed) for t in tables],
        [
            (shapes[0], (count, width), fixed),
            (shapes[1], (count, width), lambda i: (jnp.minimum(i, 1), 0)),
        ],
        6 * rows.size * width,
    )


def project_back_kernel(far, dq_ref, dkv_ref, *refs):
    far_refs = refs[:far]
    cos_ref, right_ref, left_ref, out_ref, sum_ref = refs[far:]
    step = pl.program_id(0)

    def put(value):
        out_ref[...] = value.astype(LOW)
        sum_ref[0] = jnp.sum(value, axis=0, keepdims=True)

    def key_value():
        return total_of([dkv_ref[...]] + [r[...].astype(WIDE) for r in far_refs])

    @pl.when(step == 0)
    def _():
        put(rotated(dq_ref[...], cos_ref, right_ref, left_ref))

    @pl.when(step == 1)
    def _():
        put(rotated(key_value(), cos_ref, right_ref, left_ref))

    @pl.when(step == 2)
    def _():
        put(key_value())


def project_back(dq, dkv, far, tables):
    count, width = dq.shape
    fixed = lambda i: (0, 0)
    lower = pl.BlockSpec((count, width), lambda i: (jnp.maximum(i - 1, 0), 0))
    out, sums = pl.pallas_call(
        functools.partial(project_back_kernel, len(far)),
        grid=(3,),
        in_specs=[pl.BlockSpec((count, width), fixed)]
        + [lower] * (1 + len(far))
        + [pl.BlockSpec((count, PAIR), fixed)] * 3,
        out_specs=[
            pl.BlockSpec((count, width), lambda i: (0, i)),
            pl.BlockSpec((1, 1, width), lambda i: (i, 0, 0)),
        ],
        out_shape=[
            jax.ShapeDtypeStruct((count, 3 * width), LOW),
            jax.ShapeDtypeStruct((3, 1, width), WIDE),
        ],
        compiler_params=pltpu.CompilerParams(vmem_limit_bytes=32 * 1024 * 1024),
        cost_estimate=work(14000 * count * width),
        name="project_back",
    )(dq, dkv, *far, *tables)
    return out, sums[:, 0]


def attend_near_kernel(qpos_ref, kpos_ref, q_ref, key_ref, value_ref, acc_ref, top_ref, total_ref):
    allowed = kpos_ref[0] <= qpos_ref[...]
    for half in range(PAIR // HD):
        lanes = slice(half * HD, (half + 1) * HD)
        q = q_ref[:, lanes] * jnp.asarray(HD**-0.5, LOW)
        s = jnp.where(allowed, dot(q, key_ref[:, lanes], NT), MASKED)
        top = jnp.max(s, axis=1, keepdims=True)
        p = jnp.exp(s - top)
        spread = (top.shape[0], HD)
        top_ref[:, lanes] = jnp.broadcast_to(top, spread)
        total_ref[:, lanes] = jnp.broadcast_to(jnp.sum(p, axis=1, keepdims=True), spread)
        acc_ref[:, lanes] = dot(p.astype(LOW), value_ref[:, lanes], NN)


def attend_far_kernel(blocks, qpos_ref, kpos_ref, q_ref, acc_in_ref, top_in_ref, total_in_ref, *refs):
    keys, values = refs[: 2 * blocks : 2], refs[1 : 2 * blocks : 2]
    out_ref, lse_ref = refs[2 * blocks :]
    allowed = [kpos_ref[b] <= qpos_ref[...] for b in range(blocks)]
    for half in range(PAIR // HD):
        lanes = slice(half * HD, (half + 1) * HD)
        q = q_ref[:, lanes] * jnp.asarray(HD**-0.5, LOW)
        first = slice(half * HD, half * HD + 1)
        top, total, acc = top_in_ref[:, first], total_in_ref[:, first], acc_in_ref[:, lanes]
        for b in range(blocks):
            s = jnp.where(allowed[b], dot(q, keys[b][:, lanes], NT), MASKED)
            new_top = jnp.maximum(top, jnp.max(s, axis=1, keepdims=True))
            p = jnp.exp(s - new_top)
            factor = jnp.exp(top - new_top)
            total = total * factor + jnp.sum(p, axis=1, keepdims=True)
            acc = acc * factor + dot(p.astype(LOW), values[b][:, lanes], NN)
            top = new_top
        out_ref[:, lanes] = acc / total
        lse_ref[:, lanes] = jnp.broadcast_to(top + jnp.log(total), acc.shape)


def pair_call(kernel, name, rows, width, kpos, operands, stacked, outs, flops):
    blocks, _, key_rows = kpos.shape
    column = lambda i: (0, i)
    specs = {
        "row": pl.BlockSpec((rows, PAIR), column),
        "keys": pl.BlockSpec((2 * key_rows, PAIR), column),
    }
    shapes = {"row": (rows, width), "keys": (2 * key_rows, width)}
    halves = [pl.BlockSpec((key_rows, PAIR), lambda i, c=c: (c, i)) for c in range(2)]
    common = [
        pl.BlockSpec((rows, 1), lambda i: (0, 0)),
        pl.BlockSpec((blocks, 1, key_rows), lambda i: (0, 0, 0)),
    ]
    return pl.pallas_call(
        kernel,
        grid=(width // PAIR,),
        in_specs=common + [specs["row"]] * (len(operands) - 1) + halves * len(stacked),
        out_specs=[specs[k] for k, _ in outs],
        out_shape=[jax.ShapeDtypeStruct(shapes[k], t) for k, t in outs],
        compiler_params=pltpu.CompilerParams(vmem_limit_bytes=40 * 1024 * 1024),
        cost_estimate=work(flops * rows * key_rows * blocks * width),
        name=name,
    )(operands[0], kpos, *operands[1:], *[s for s in stacked for c in range(2)])


def attend_near(qpos, kpos, q, own):
    rows, width = q.shape
    outs = [("row", WIDE)] * 3
    return pair_call(attend_near_kernel, "attend_near", rows, width, kpos, [qpos, q], [own], outs, 43)


def attend_far(qpos, kpos, q, near, far):
    rows, width = q.shape
    return pair_call(
        functools.partial(attend_far_kernel, len(far)),
        "attend_far",
        rows,
        width,
        kpos,
        [qpos, q, *near],
        far,
        [("row", WIDE)] * 2,
        43,
    )


def attend_back_kernel(blocks, more, qpos_ref, kpos_ref, q_ref, grad_ref, out_ref, lse_ref, *refs):
    before, refs = refs[:more], refs[more:]
    keys, values = refs[: 2 * blocks : 2], refs[1 : 2 * blocks : 2]
    dq_ref = refs[2 * blocks]
    dboth = refs[2 * blocks + 1 :]
    key_rows = keys[0].shape[0]
    allowed = [kpos_ref[b] <= qpos_ref[...] for b in range(blocks)]
    scale = HD**-0.5
    for half in range(PAIR // HD):
        lanes = slice(half * HD, (half + 1) * HD)
        q = q_ref[:, lanes] * jnp.asarray(scale, LOW)
        grad = grad_ref[:, lanes]
        lse = lse_ref[:, half * HD : half * HD + 1]
        delta = jnp.sum(grad.astype(WIDE) * out_ref[:, lanes], axis=1, keepdims=True)
        dq = []
        for b in range(blocks):
            k = keys[b][:, lanes]
            s = jnp.where(allowed[b], dot(q, k, NT), MASKED)
            p = jnp.exp(s - lse)
            dp = dot(grad, values[b][:, lanes], NT)
            ds = (p * (dp - delta)).astype(LOW)
            kind = dboth[b].dtype
            dboth[b][key_rows:, lanes] = dot(p.astype(LOW), grad, TN).astype(kind)
            dboth[b][:key_rows, lanes] = dot(ds, q, TN).astype(kind)
            dq.append(dot(ds, k, NN))
        dq_ref[:, lanes] = total_of([total_of(dq) * scale] + [r[:, lanes] for r in before])


def attend_back(qpos, kpos, q, grad, out, lse, stacked, kind, before):
    rows, width = q.shape
    results = pair_call(
        functools.partial(attend_back_kernel, len(stacked), len(before)),
        "attend_back",
        rows,
        width,
        kpos,
        [qpos, q, grad, out, lse, *before],
        stacked,
        [("row", WIDE)] + [("keys", kind)] * len(stacked),
        75,
    )
    return results[0], results[1:]


def norm_back_kernel(count, *refs):
    terms = refs[:count]
    unit_ref, inverse_ref, gain_ref, base_ref = refs[count : count + 4]
    grad_ref, low_ref, gain_out_ref, bias_out_ref = refs[count + 4 :]
    grad_rows = total_of([t[...].astype(WIDE) for t in terms])
    unit = unit_ref[...]
    grad_unit = grad_rows * gain_ref[...]
    first_mean = jnp.mean(grad_unit, axis=-1, keepdims=True)
    second_mean = jnp.mean(grad_unit * unit, axis=-1, keepdims=True)
    total = base_ref[...] + inverse_ref[...] * (grad_unit - first_mean - unit * second_mean)
    grad_ref[...] = total
    low_ref[...] = total.astype(LOW)
    gain_out_ref[...] = jnp.sum(grad_rows * unit, axis=0, keepdims=True)
    bias_out_ref[...] = jnp.sum(grad_rows, axis=0, keepdims=True)


def norm_back(terms, unit, inverse, gain, base):
    rows, model = unit.shape
    fixed = lambda i: (0, 0)
    line = (1, model)
    operands = [*terms, unit, inverse, gain[None], base]
    shapes = [(rows, model)] * (len(terms) + 1) + [(rows, 1), line, (rows, model)]
    outs = [((rows, model), WIDE), ((rows, model), LOW), (line, WIDE), (line, WIDE)]
    results = tiled(
        functools.partial(norm_back_kernel, len(terms)),
        "norm_back",
        1,
        [(o, s, fixed) for o, s in zip(operands, shapes)],
        [(jax.ShapeDtypeStruct(s, t), s, fixed) for s, t in outs],
        1e9,
    )
    return results[0], results[1], results[2][0], results[3][0]


def finish(buffer, layer, terms, make, steps, ins, out, name):
    shape, block, place = out

    def kernel(*refs):
        refs[-1][...] = make(*[r[...].astype(WIDE) for r in refs[: len(terms)]])

    operands = list(terms)
    specs = [pl.BlockSpec(b, index) for b, index in ins]
    if buffer is not None:
        operands.append(buffer)
        specs.append(pl.BlockSpec(memory_space=pl.ANY))
    return pl.pallas_call(
        kernel,
        grid=(steps,),
        in_specs=specs,
        out_specs=pl.BlockSpec((1,) + block, lambda i: (layer,) + place(i)),
        out_shape=jax.ShapeDtypeStruct(shape, WIDE),
        input_output_aliases={} if buffer is None else {len(terms): 0},
        compiler_params=pltpu.CompilerParams(vmem_limit_bytes=48 * 1024 * 1024),
        cost_estimate=work(len(terms) * terms[0].size * 3.5e3),
        name=name,
    )(*operands)


def finish_matrix(buffer, layer, terms, name):
    rows, columns = terms[0].shape
    block = (rows // 4, columns)
    place = lambda i: (i, 0)
    out = ((LAYERS, rows, columns), block, place)
    make = lambda *t: total_of(t)[None]
    return finish(buffer, layer, terms, make, 4, [(block, place)] * len(terms), out, name)


def finish_projections(buffer, layer, terms):
    rows, columns = terms[0].shape
    width = columns // 3
    out = ((LAYERS, 3, rows, width), (1, rows, width), lambda i: (i, 0, 0))
    make = lambda *t: total_of(t)[None, None]
    ins = [((rows, width), lambda i: (0, i))] * len(terms)
    return finish(buffer, layer, terms, make, 3, ins, out, "finish_qkv")


def finish_gate_up(buffer, layer, gate_terms, up_terms):
    rows, columns = gate_terms[0].shape
    steps = 8
    block = (rows // steps, columns)
    out = ((LAYERS, rows, 2, columns), (rows // steps, 2, columns), lambda i: (i, 0, 0))
    count = len(gate_terms)
    make = lambda *t: jnp.stack([total_of(t[:count]), total_of(t[count:])], axis=1)[None]
    ins = [(block, lambda i: (i, 0))] * (2 * count)
    return finish(buffer, layer, gate_terms + up_terms, make, steps, ins, out, "finish_gate_up")


def bits_of(count):
    return [1 << k for k in range(count.bit_length() - 1)]


def swapped(value, axis, mask):
    count = lax.axis_size(axis)
    return lax.ppermute(value, axis, [(i, i ^ mask) for i in range(count)])


def joined(pieces, axis):
    return pieces[0] if len(pieces) == 1 else jnp.concatenate(pieces, axis=axis)


class Line:
    def __init__(self, own_rows):
        n_tensor, n_ctx = lax.axis_size("tensor"), lax.axis_size("ctx")
        tensor, ctx = lax.axis_index("tensor"), lax.axis_index("ctx")
        self.count, self.tensor = n_tensor, tensor
        row = jnp.arange(own_rows, dtype=jnp.int32)
        chip = (tensor + jnp.arange(n_tensor, dtype=jnp.int32)) % n_tensor
        place = (chip[:, None] * own_rows + row[None, :]).reshape(-1)
        block = n_tensor * own_rows
        self.places = ctx * block + place
        self.far_places = [
            jnp.where(ctx >= s, (ctx - s) * block + place, 1 << 30) for s in range(1, n_ctx)
        ]
        self.own_rows = own_rows

    def gather_rows(self, low):
        count, t = self.count, self.tensor
        send = lambda v, *route: lax.ppermute(v, "tensor", list(route))
        if count == 4:
            far = send(low, (0, 2), (2, 0), (1, 3), (3, 1))
            above = send(low, (0, 1), (1, 2), (2, 3))
            below = send(low, (1, 0), (2, 1), (3, 2))
            end = send(far, (2, 3), (1, 0))
            found = [low, jnp.where(t == 3, end, below), far, jnp.where(t == 0, end, above)]
        else:
            found = [low] + [
                send(low, *[((i + d) % count, i) for i in range(count)]) for d in range(1, count)
            ]
        return jnp.concatenate(found, axis=0)

    def sum_rows(self, low, *jobs):
        rows, count, t = self.own_rows, self.count, self.tensor
        terms = [low[d * rows : (d + 1) * rows] for d in range(count)]
        send = lambda v, *route: lax.ppermute(v, "tensor", list(route))
        wide = lambda v: v.astype(WIDE)
        if count == 4:
            end = send(jnp.where(t == 0, terms[3], terms[1]), (0, 1), (3, 2))
            above = send(terms[1], (0, 1), (1, 2), (2, 3))
            below = send(terms[3], (3, 2), (2, 1), (1, 0))
            far = meanwhile((wide(terms[2]) + wide(end)).astype(LOW), *jobs)
            got = [send(far, (0, 2), (2, 0), (1, 3), (3, 1)), above, below]
        else:
            got = [
                send(terms[d], *[(i, (i + d) % count) for i in range(count)])
                for d in range(1, count)
            ]
        return (low, *got)

    def sum_of(self, terms):
        return total_of([terms[0][: self.own_rows].astype(WIDE)] + [t.astype(WIDE) for t in terms[1:]])

    def owner(self, low):
        count = lax.axis_size("ctx")
        if count != 2:
            return (lax.psum(low, "ctx") if count > 1 else low,)
        got = yield swapped(low, "ctx", 1)
        return (low, got)

    def far_keys(self, value):
        count = lax.axis_size("ctx")
        return [
            lax.ppermute(value, "ctx", [(i, i + s) for i in range(count - s)])
            for s in range(1, count)
        ]

    def far_key_grads(self, values):
        count = lax.axis_size("ctx")
        return [
            lax.ppermute(values[s - 1], "ctx", [(i + s, i) for i in range(count - s)])
            for s in range(1, count)
        ]


def weight_stages(shard):
    shard = yield shard
    return (yield lax.all_gather(shard, "dp"))


def grad_stages(plan, value, axis):
    got = yield lax.psum_scatter(value.astype(LOW), "dp", scatter_dimension=axis, tiled=True)
    return (yield from plan.owner(got))


def low_first(count):
    width = count.bit_length() - 1
    return sorted(range(count), key=lambda r: int(format(r, "b").zfill(width)[::-1] or "0", 2))


def pair_stages(plan, terms_of, axis):
    count = lax.axis_size("dp")

    def term(parts):
        factors = [terms_of(r) for r in parts]
        a = joined([f[0] for f in factors], 1) if axis == 0 else factors[0][0]
        b = joined([f[1] for f in factors], 1) if axis == 1 else factors[0][1]
        return outer(a, b)

    order = low_first(count)
    kept = None
    for bit in bits_of(count):
        if kept is None:
            sent = yield term(order[count // 2 :])
        else:
            kept, sent = jnp.split(kept, 2, axis=axis)
        got = yield swapped(sent.astype(LOW), "dp", bit)
        kept = (term(order[: count // 2]).astype(WIDE) if kept is None else kept) + got.astype(WIDE)
    return (yield from plan.owner(kept.astype(LOW)))


class Job:
    def __init__(self, stages):
        self.stages, self.value, self.result, self.done = stages, None, None, False
        self.advance(None)

    def advance(self, value):
        try:
            self.value = self.stages.send(value)
        except StopIteration as end:
            self.done, self.result, self.value = True, end.value, None

    def finish(self):
        while not self.done:
            self.advance(self.value)
        return self.result


def meanwhile(value, *jobs):
    open_jobs = [j for j in jobs if j is not None and not j.done]
    if not open_jobs:
        return value
    value, held = lax.optimization_barrier((value, tuple(j.value for j in open_jobs)))
    for job, got in zip(open_jobs, held):
        job.advance(got)
    return value


def held(value, *jobs):
    open_jobs = [j for j in jobs if j is not None and not j.done]
    if not open_jobs:
        return value
    value, kept = lax.optimization_barrier((value, tuple(j.value for j in open_jobs)))
    for job, got in zip(open_jobs, kept):
        job.value = got
    return value


def shards(
    tokens,
    cotangent,
    norm_gains,
    norm_biases,
    qkv_weight,
    qkv_bias,
    out_weight,
    gate_up_weight,
    down_weight,
):
    own_rows = tokens.shape[1]
    model = tokens.shape[2]
    heads_width = qkv_weight.shape[3]
    plan = Line(own_rows)
    tables = rotary_tables(plan.places)
    tables_back = (tables[0], -tables[1], -tables[2])
    qpos = plan.places[:, None]
    near_places = plan.places[None, None, :]
    far_places = jnp.stack(plan.far_places)[:, None, :]
    gains = (norm_gains)
    biases = (norm_biases)
    qkv_bias_own = lax.dynamic_slice_in_dim(qkv_bias, lax.axis_index("tensor") * heads_width, heads_width, 2)

    def weight_jobs(layer, after):
        (qkv_all, out_all, gate_up_all, down_all), after = lax.optimization_barrier(
            ((qkv_weight, out_weight, gate_up_weight, down_weight), after)
        )
        matrices = {
            "qkv": jnp.transpose(qkv_all[layer], (1, 0, 2)),
            "out": out_all[layer],
            "gate": gate_up_all[layer, :, 0],
            "up": gate_up_all[layer, :, 1],
            "down": down_all[layer],
        }
        return {n: Job(weight_stages(v)) for n, v in matrices.items()}, after

    now, unused = weight_jobs(0, ())
    for name in ("qkv", "out", "gate", "up"):
        now[name].advance(now[name].value)
    stream = tokens[0].astype(WIDE)
    later = {}
    saved = []
    for layer in range(LAYERS):
        last = layer + 1 == LAYERS
        normed_one, unit_one, inverse_one = layer_norm_rows(
            stream, gains[layer, 0], biases[layer, 0]
        )
        rows_one = plan.gather_rows(normed_one.astype(LOW))
        if layer == 0:
            rows_one = meanwhile(rows_one, now["qkv"], now["down"])
        else:
            rows_one = meanwhile(rows_one, now["out"], now["gate"], now["down"])
        qkv_full = now["qkv"].finish()
        queries, keys_values = project(rows_one, qkv_full, qkv_bias_own[layer], tables)
        if layer == 0:
            late_cotangent, queries = lax.optimization_barrier((cotangent[0], queries))
            grad_stream = late_cotangent.astype(WIDE)
            branch = plan.gather_rows(late_cotangent)
        prepared = {}
        if not last:
            prepared, queries = weight_jobs(layer + 1, queries)
        far_kv = plan.far_keys(keys_values)
        near = attend_near(qpos, near_places, queries, keys_values)
        attended, lse = attend_far(qpos, far_places, queries, near, far_kv)
        attended_low = meanwhile(attended.astype(LOW), now["out"])
        attended_low = held(attended_low, *map(prepared.get, ("gate", "up")))
        if layer == 0:
            attended_low, branch = lax.optimization_barrier((attended_low, branch))
        else:
            attended_low = meanwhile(attended_low, now["up"])
        out_full = now["out"].finish()
        mid = stream + plan.sum_of(plan.sum_rows(times_wide(attended_low, out_full, "out")))
        mid = meanwhile(mid, now["gate"])
        if layer > 0:
            mid = meanwhile(mid, now["down"])
        else:
            later = prepared
        normed_two, unit_two, inverse_two = layer_norm_rows(mid, gains[layer, 1], biases[layer, 1])
        rows_two = plan.gather_rows(normed_two.astype(LOW))
        rows_two = meanwhile(rows_two, now["up"], now["down"], later.get("qkv"))
        flat = lambda v: v.reshape(v.shape[0] * v.shape[1], v.shape[2])
        gate_full, up_full = flat(now["gate"].finish()), flat(now["up"].finish())
        gate, up, activated = gate_up_rows(rows_two, gate_full, up_full)
        activated = meanwhile(activated, later.get("out"), later.get("gate"))
        down_full = now["down"].finish()
        if not last:
            stream = mid + plan.sum_of(
                plan.sum_rows(times_wide(activated, down_full, "down"))
            )
            stream = meanwhile(stream, later.get("qkv"), later.get("up"))
        saved.append(
            (
                (qkv_full, out_full, gate_full, up_full, down_full),
                (rows_one, unit_one, inverse_one),
                (queries, keys_values, far_kv, attended, attended_low, lse),
                (rows_two, unit_two, inverse_two),
                (gate, up, activated),
            )
        )
        now = later
    grad_jobs = [None] * LAYERS
    gain_grads = [None] * LAYERS
    bias_grads = [None] * LAYERS
    qkv_bias_grads = [None] * LAYERS
    for layer in range(LAYERS - 1, -1, -1):
        (
            (qkv_full, out_full, gate_full, up_full, down_full),
            (rows_one, unit_one, inverse_one),
            (queries, keys_values, far_kv, attended, attended_low, lse),
            (rows_two, unit_two, inverse_two),
            (gate, up, activated),
        ) = saved[layer]
        mine = {}
        grad_jobs[layer] = mine
        above = grad_jobs[layer + 1] if layer + 1 < LAYERS else {}
        old = lambda *keys: [above.get(k) for k in keys]

        def own_part(value, r):
            index = lax.axis_index("dp") ^ r
            width = value.shape[1] // lax.axis_size("dp")
            return lax.dynamic_slice_in_dim(value, index * width, width, 1)

        def in_job(a, b):
            return Job(grad_stages(plan, outer(a, b), 0))

        def out_job(a, b):
            return Job(grad_stages(plan, outer(a, b), 1))

        if layer + 1 < LAYERS:
            branch = plan.gather_rows(grad_low)
        branch = held(meanwhile(branch, *old("gate", "up", "qkv")), *old("out"))
        if layer == 0:
            down_grad, branch = lax.optimization_barrier(
                (outer(activated, branch), branch)
            )
            mine["down"] = Job(grad_stages(plan, down_grad, 1))
        grad_gate, grad_up = gate_up_back(branch, down_full, gate, up)
        partial_in = gate_up_in(grad_gate, grad_up, gate_full, up_full)
        summed = plan.sum_rows(partial_in)
        summed = meanwhile(summed, *old("up", "out", "qkv"))
        hidden_grad, hidden_low, gain_two, bias_two = norm_back(
            summed, unit_two, inverse_two, gains[layer, 1], grad_stream
        )
        hidden_low, (branch, grad_gate, grad_up) = lax.optimization_barrier(
            (hidden_low, (branch, grad_gate, grad_up))
        )
        if layer > 0:
            mine["down"] = out_job(activated, branch)
        mine["gate"] = in_job(rows_two, grad_gate)
        if layer == 0:
            hidden_low = meanwhile(hidden_low, mine["down"])
        top = layer + 1 == LAYERS
        if top:
            late, hidden_low = lax.optimization_barrier((activated, hidden_low))
            partial_out = times_wide(late, down_full, "down")
        attention = plan.gather_rows(hidden_low)
        attention = meanwhile(attention, *old("out", "qkv"))
        if top:
            attention, partial_out = lax.optimization_barrier((attention, partial_out))
            output = (mid + plan.sum_of(plan.sum_rows(partial_out))).astype(LOW)[None]
        grad_attended = out_back(attention, out_full)
        shared = (queries, grad_attended, attended, lse)
        far_queries, far_grads = attend_back(qpos, far_places, *shared, far_kv, LOW, [])
        if layer == 0:
            far_queries, grad_up = lax.optimization_barrier((far_queries, grad_up))
            mine["up"] = in_job(rows_two, grad_up)
            far_queries = meanwhile(far_queries, mine["down"])
        returned = plan.far_key_grads(far_grads)
        grad_queries, grad_kv = attend_back(
            qpos, near_places, *shared, [keys_values], WIDE, [far_queries]
        )
        if top:
            grad_queries, output = lax.optimization_barrier((grad_queries, output))
        projected, qkv_bias_grads[layer] = project_back(
            grad_queries, grad_kv[0], returned, tables_back
        )
        projected, (attention, grad_up) = lax.optimization_barrier(
            (projected, (attention, grad_up))
        )
        if layer > 0:
            mine["up"] = in_job(rows_two, grad_up)
        mine["out"] = Job(
            pair_stages(plan, lambda r, a=attention: (attended_low, own_part(a, r)), 1)
        )
        if layer > 0:
            mine["up"] = in_job(rows_two, grad_up)
        projected = meanwhile(projected, mine["out"])
        projected = meanwhile(projected, mine["down"] if layer > 0 else None, *old("qkv"))
        if not top:
            above_done, projected = lax.optimization_barrier(
                ({k: j.finish() for k, j in above.items()}, projected)
            )
        if layer == 0:
            mine["qkv"] = Job(
                pair_stages(plan, lambda r, b=projected: (own_part(rows_one, r), b), 0)
            )
            projected = meanwhile(projected, mine["qkv"], mine["gate"])
        partial_in = project_in(projected, qkv_full)
        if layer == 0:
            partial_in = held(meanwhile(partial_in, mine["qkv"]), mine["out"])
            summed = plan.sum_rows(partial_in, mine["up"])
        else:
            summed = plan.sum_rows(partial_in)
        if layer > 0:
            summed = meanwhile(summed, mine["down"], mine["out"])
        else:
            summed = meanwhile(summed, *map(mine.get, ("gate", "out", "qkv")))
        grad_stream, grad_low, gain_one, bias_one = norm_back(
            summed, unit_one, inverse_one, gains[layer, 0], hidden_grad
        )
        if layer == 0:
            gain_one = meanwhile(gain_one, mine["up"])
        else:
            grad_low, projected = lax.optimization_barrier((grad_low, projected))
            mine["qkv"] = Job(
                pair_stages(plan, lambda r, a=rows_one, b=projected: (own_part(a, r), b), 0)
            )
            grad_low = meanwhile(grad_low, mine["gate"], mine["qkv"])
        gain_grads[layer] = jnp.stack([gain_one, gain_two])
        bias_grads[layer] = jnp.stack([bias_one, bias_two])

    tokens_grad = grad_low[None]
    padded_bias = lax.dynamic_update_slice_in_dim(
        jnp.zeros((LAYERS, 3, qkv_bias.shape[2]), WIDE),
        jnp.stack(qkv_bias_grads),
        lax.axis_index("tensor") * heads_width,
        2,
    )
    small = jnp.concatenate(
        [
            (jnp.stack(gain_grads)).reshape(LAYERS * 2, model),
            (jnp.stack(bias_grads)).reshape(LAYERS * 2, model),
            padded_bias.reshape(LAYERS * 3, qkv_bias.shape[2]),
        ],
        axis=0,
    )
    above_done, down_done, small = lax.optimization_barrier(
        (above_done, grad_jobs[0]["down"].finish(), small)
    )
    for axis in ("dp", "tensor", "ctx"):
        for bit in bits_of(lax.axis_size(axis)):
            small = small + swapped(small, axis, bit)
    results = [None] * 4
    for layer, sums in ((1, above_done), (0, grad_jobs[0])):
        if layer == 0:
            sums = {k: j.finish() for k, j in sums.items()}
            sums["down"] = down_done
        results = [
            finish_projections(results[0], layer, sums["qkv"]),
            finish_matrix(results[1], layer, sums["out"], "finish_out"),
            finish_gate_up(results[2], layer, sums["gate"], sums["up"]),
            finish_matrix(results[3], layer, sums["down"], "finish_down"),
        ]
    return (
        output,
        tokens_grad,
        small[: LAYERS * 2].reshape(LAYERS, 2, model),
        small[LAYERS * 2 : LAYERS * 4].reshape(LAYERS, 2, model),
        jnp.transpose(results[0], (0, 2, 1, 3)),
        small[LAYERS * 4 :].reshape(LAYERS, 3, qkv_bias.shape[2]),
        *results[1:],
    )


def solution(mesh):
    rows = P("dp", ("ctx", "tensor"), None)
    wide = P(None, "dp", None, "tensor")
    tall = P(None, "tensor", "dp")
    return jax.shard_map(
        shards,
        mesh=mesh,
        in_specs=(rows, rows, P(), P(), wide, P(), tall, wide, tall),
        out_specs=(rows, rows, P(), P(), wide, P(), tall, wide, tall),
        check_vma=False,
    )
```

```python
import functools

import jax
import jax.numpy as jnp
from jax import lax
from jax.experimental import pallas as pl
from jax.experimental.pallas import tpu as pltpu
from jax.sharding import PartitionSpec as P

HD = 64
ROT = 16
LAYERS = 2

MASKED = -1e30
EPSILON = 1e-05
LOW = jnp.bfloat16
WIDE = jnp.float32


def layer_norm_rows(stream, gain, bias):
    row_mean = jnp.mean(stream, axis=-1, keepdims=True)
    centered = stream - row_mean
    inverse = lax.rsqrt(jnp.mean(centered * centered, axis=-1, keepdims=True) + EPSILON)
    unit_rows = centered * inverse
    return (unit_rows * gain + bias, unit_rows, inverse)


def rotary_tables(positions):
    half_rot = ROT // 2
    frequency = 10000.0 ** (-(jnp.arange(half_rot, dtype=jnp.float32) * 2.0) / ROT)
    angles = positions.astype(jnp.float32)[:, None] * frequency[None, :]
    cosine, sine = jnp.cos(angles), jnp.sin(angles)
    rest = jnp.zeros((angles.shape[0], HD - ROT), WIDE)
    none = jnp.zeros_like(sine)
    heads = lambda *parts: jnp.tile(jnp.concatenate(parts, axis=1), (1, PAIR // HD))
    return (
        heads(cosine, cosine, rest + 1.0),
        heads(-sine, none, rest),
        heads(none, sine, rest),
    )


def rotated(flat, cos_ref, right_ref, left_ref):
    shift = ROT // 2
    found = []
    for start in range(0, flat.shape[1], PAIR):
        v = flat[:, start : start + PAIR]
        right, left = pltpu.roll(v, PAIR - shift, 1), pltpu.roll(v, shift, 1)
        found.append(v * cos_ref[...] + right * right_ref[...] + left * left_ref[...])
    return jnp.concatenate(found, axis=1)


def dot(a, b, dims):
    return lax.dot_general(a, b, (dims, ((), ())), preferred_element_type=WIDE)


PAIR = 128


NN = ((1,), (0,))
NT = ((1,), (1,))
TN = ((0,), (0,))


def total_of(terms):
    return functools.reduce(lambda a, b: a + b, terms)


def work(flops):
    return pl.CostEstimate(flops=int(flops), bytes_accessed=0, transcendentals=0)


TILE = 512


def tiled(kernel, name, steps, ins, outs, flops):
    return pl.pallas_call(
        kernel,
        grid=(steps,),
        in_specs=[pl.BlockSpec(block, index) for _, block, index in ins],
        out_specs=[pl.BlockSpec(block, index) for _, block, index in outs],
        out_shape=[shape for shape, _, _ in outs],
        compiler_params=pltpu.CompilerParams(vmem_limit_bytes=48 * 1024 * 1024),
        cost_estimate=work(2.5 * flops),
        name=name,
    )(*[array for array, _, _ in ins])


def whole_block(array):
    return (array, array.shape, lambda i: (0,) * array.ndim)


def column_block(array):
    return (array, (array.shape[0], TILE), lambda i: (0, i))


def row_block(array):
    return (array, (TILE, array.shape[1]), lambda i: (i, 0))


def gate_up_kernel(rows_ref, gate_w_ref, up_w_ref, gate_ref, up_ref, activated_ref):
    rows = rows_ref[...]
    gate = dot(rows, gate_w_ref[...], NN)
    up = dot(rows, up_w_ref[...], NN)
    gate_ref[...] = gate
    up_ref[...] = up
    activated_ref[...] = (gate * jax.nn.sigmoid(gate) * up).astype(LOW)


def gate_up_rows(rows, gate_weight, up_weight):
    count, hidden = rows.shape[0], gate_weight.shape[1]
    shapes = [jax.ShapeDtypeStruct((count, hidden), t) for t in (WIDE, WIDE, LOW)]
    return tiled(
        gate_up_kernel,
        "gate_up",
        pl.cdiv(hidden, TILE),
        [whole_block(rows), column_block(gate_weight), column_block(up_weight)],
        [column_block(s) for s in shapes],
        4 * rows.size * hidden,
    )


def back_sum(rows, weight_ref):
    width = weight_ref.shape[2]
    return total_of(
        dot(rows[:, r * width : (r + 1) * width], weight_ref[r], NT)
        for r in range(weight_ref.shape[0])
    )


def tall_block(array):
    return (array, (array.shape[0], TILE, array.shape[2]), lambda i: (0, i, 0))


def gate_up_back_kernel(rows_ref, weight_ref, gate_ref, up_ref, grad_gate_ref, grad_up_ref):
    grad = back_sum(rows_ref[...], weight_ref)
    gate, up = gate_ref[...], up_ref[...]
    s = jax.nn.sigmoid(gate)
    grad_gate_ref[...] = (grad * up * s * (1.0 + gate * (1.0 - s))).astype(LOW)
    grad_up_ref[...] = (grad * (gate * s)).astype(LOW)


def gate_up_back(rows, down_weight, gate, up):
    count, hidden = gate.shape
    shape = jax.ShapeDtypeStruct((count, hidden), LOW)
    return tiled(
        gate_up_back_kernel,
        "gate_up_back",
        pl.cdiv(hidden, TILE),
        [whole_block(rows), tall_block(down_weight), column_block(gate), column_block(up)],
        [column_block(shape)] * 2,
        2 * rows.size * hidden,
    )


def out_back_kernel(rows_ref, weight_ref, out_ref):
    out_ref[...] = back_sum(rows_ref[...], weight_ref).astype(LOW)


def out_back(rows, weight):
    shape = jax.ShapeDtypeStruct((rows.shape[0], weight.shape[1]), LOW)
    return tiled(
        out_back_kernel,
        "out_back",
        shape.shape[1] // TILE,
        [whole_block(rows), tall_block(weight)],
        [column_block(shape)],
        2 * rows.size * shape.shape[1],
    )[0]


def wide_kernel(rows_ref, weight_ref, out_ref):
    out_ref[...] = dot(rows_ref[...], weight_ref[0], NN).astype(LOW)


def times_wide(rows, weight, name):
    blocks, depth, width = weight.shape
    per = width // TILE
    shape = jax.ShapeDtypeStruct((rows.shape[0], blocks * width), LOW)
    return tiled(
        wide_kernel,
        name,
        blocks * per,
        [whole_block(rows), (weight, (1, depth, TILE), lambda i: (i // per, 0, i % per))],
        [column_block(shape)],
        2 * rows.size * blocks * width,
    )[0]


def gate_up_in_kernel(gate_ref, up_ref, gate_w_ref, up_w_ref, out_ref):
    total = dot(gate_ref[...], gate_w_ref[...], NT) + dot(up_ref[...], up_w_ref[...], NT)
    out_ref[...] = total.astype(LOW)


def gate_up_in(grad_gate, grad_up, gate_weight, up_weight):
    shape = jax.ShapeDtypeStruct((grad_gate.shape[0], gate_weight.shape[0]), LOW)
    return tiled(
        gate_up_in_kernel,
        "gate_up_in",
        shape.shape[1] // TILE,
        [whole_block(grad_gate), whole_block(grad_up), row_block(gate_weight), row_block(up_weight)],
        [column_block(shape)],
        4 * grad_gate.size * shape.shape[1],
    )[0]


def project_in_kernel(rows_ref, weight_ref, out_ref):
    width = weight_ref.shape[3]
    out_ref[...] = total_of(
        dot(rows_ref[:, c * width : (c + 1) * width], weight_ref[0, c], NT) for c in range(3)
    ).astype(LOW)


def project_in(rows, weight):
    blocks, three, depth, width = weight.shape
    per = depth // TILE
    shape = jax.ShapeDtypeStruct((rows.shape[0], blocks * depth), LOW)
    return tiled(
        project_in_kernel,
        "project_in",
        blocks * per,
        [whole_block(rows), (weight, (1, three, TILE, width), lambda i: (i // per, 0, i % per, 0))],
        [column_block(shape)],
        2 * rows.size * blocks * depth,
    )[0]


def outer_kernel(a_ref, b_ref, out_ref):
    out_ref[...] = dot(a_ref[...], b_ref[...], TN).astype(LOW)


def outer(a, b):
    shape = jax.ShapeDtypeStruct((a.shape[1], b.shape[1]), LOW)
    return tiled(
        outer_kernel,
        "outer",
        pl.cdiv(a.shape[1], TILE),
        [column_block(a), whole_block(b)],
        [row_block(shape)],
        a.size * b.shape[1] * 0.8,
    )[0]


def project_kernel(rows_ref, weight_ref, bias_ref, cos_ref, right_ref, left_ref, q_ref, kv_ref):
    blocks, _, depth, width = weight_ref.shape
    flat = dot(rows_ref[...], weight_ref[...].reshape(blocks * depth, width), NN) + bias_ref[0]
    step = pl.program_id(0)

    @pl.when(step == 0)
    def _():
        kv_ref[...] = rotated(flat, cos_ref, right_ref, left_ref).astype(LOW)

    @pl.when(step == 1)
    def _():
        kv_ref[...] = flat.astype(LOW)

    @pl.when(step == 2)
    def _():
        q_ref[...] = rotated(flat, cos_ref, right_ref, left_ref).astype(LOW)


def project(rows, weight, bias, tables):
    count = rows.shape[0]
    blocks, _, depth, width = weight.shape
    fixed = lambda i: (0, 0)
    shapes = [jax.ShapeDtypeStruct((k * count, width), LOW) for k in (1, 2)]
    return tiled(
        project_kernel,
        "project",
        3,
        [
            whole_block(rows),
            (weight, (blocks, 1, depth, width), lambda i: (0, (i + 1) % 3, 0, 0)),
            (bias[:, None, :], (1, 1, width), lambda i: ((i + 1) % 3, 0, 0)),
        ]
        + [(t, (count, PAIR), fixed) for t in tables],
        [
            (shapes[0], (count, width), fixed),
            (shapes[1], (count, width), lambda i: (jnp.minimum(i, 1), 0)),
        ],
        6 * rows.size * width,
    )


def project_back_kernel(far, dq_ref, dkv_ref, *refs):
    far_refs = refs[:far]
    cos_ref, right_ref, left_ref, out_ref, sum_ref = refs[far:]
    step = pl.program_id(0)

    def put(value):
        out_ref[...] = value.astype(LOW)
        sum_ref[0] = jnp.sum(value, axis=0, keepdims=True)

    def key_value():
        return total_of([dkv_ref[...]] + [r[...].astype(WIDE) for r in far_refs])

    @pl.when(step == 0)
    def _():
        put(rotated(dq_ref[...], cos_ref, right_ref, left_ref))

    @pl.when(step == 1)
    def _():
        put(rotated(key_value(), cos_ref, right_ref, left_ref))

    @pl.when(step == 2)
    def _():
        put(key_value())


def project_back(dq, dkv, far, tables):
    count, width = dq.shape
    fixed = lambda i: (0, 0)
    lower = pl.BlockSpec((count, width), lambda i: (jnp.maximum(i - 1, 0), 0))
    out, sums = pl.pallas_call(
        functools.partial(project_back_kernel, len(far)),
        grid=(3,),
        in_specs=[pl.BlockSpec((count, width), fixed)]
        + [lower] * (1 + len(far))
        + [pl.BlockSpec((count, PAIR), fixed)] * 3,
        out_specs=[
            pl.BlockSpec((count, width), lambda i: (0, i)),
            pl.BlockSpec((1, 1, width), lambda i: (i, 0, 0)),
        ],
        out_shape=[
            jax.ShapeDtypeStruct((count, 3 * width), LOW),
            jax.ShapeDtypeStruct((3, 1, width), WIDE),
        ],
        compiler_params=pltpu.CompilerParams(vmem_limit_bytes=32 * 1024 * 1024),
        cost_estimate=work(14000 * count * width),
        name="project_back",
    )(dq, dkv, *far, *tables)
    return out, sums[:, 0]


GROUP = 256


def attend_kernel(blocks, qpos_ref, kpos_ref, q_ref, *refs):
    keys, values = refs[: 2 * blocks : 2], refs[1 : 2 * blocks : 2]
    out_ref, lse_ref = refs[2 * blocks :]
    allowed = [kpos_ref[b] <= qpos_ref[...] for b in range(blocks)]
    for half in range(q_ref.shape[1] // HD):
        lanes = slice(half * HD, (half + 1) * HD)
        q = q_ref[:, lanes] * jnp.asarray(HD**-0.5, LOW)
        top, total, acc = None, None, None
        for b in range(blocks):
            s = jnp.where(allowed[b], dot(q, keys[b][:, lanes], NT), MASKED)
            block_top = jnp.max(s, axis=1, keepdims=True)
            new_top = block_top if b == 0 else jnp.maximum(top, block_top)
            p = jnp.exp(s - new_top)
            block_total = jnp.sum(p, axis=1, keepdims=True)
            block_acc = dot(p.astype(LOW), values[b][:, lanes], NN)
            if b == 0:
                total, acc = block_total, block_acc
            else:
                factor = jnp.exp(top - new_top)
                total = total * factor + block_total
                acc = acc * factor + block_acc
            top = new_top
        out_ref[:, lanes] = acc / total
        lse_ref[:, lanes] = jnp.broadcast_to(top + jnp.log(total), acc.shape)


def group_call(kernel, name, rows, width, kpos, operands, stacked, outs, flops):
    blocks, _, key_rows = kpos.shape
    group = GROUP if blocks <= 2 else PAIR
    column = lambda i: (0, i)
    specs = {
        "row": pl.BlockSpec((rows, group), column),
        "keys": pl.BlockSpec((2 * key_rows, group), column),
    }
    shapes = {"row": (rows, width), "keys": (2 * key_rows, width)}
    halves = [pl.BlockSpec((key_rows, group), lambda i, c=c: (c, i)) for c in range(2)]
    common = [
        pl.BlockSpec((rows, 1), lambda i: (0, 0)),
        pl.BlockSpec((blocks, 1, key_rows), lambda i: (0, 0, 0)),
    ]
    return pl.pallas_call(
        kernel,
        grid=(width // group,),
        in_specs=common + [specs["row"]] * (len(operands) - 1) + halves * len(stacked),
        out_specs=[specs[k] for k, _ in outs],
        out_shape=[jax.ShapeDtypeStruct(shapes[k], t) for k, t in outs],
        compiler_params=pltpu.CompilerParams(vmem_limit_bytes=40 * 1024 * 1024),
        cost_estimate=work(flops * rows * key_rows * blocks * width),
        name=name,
    )(operands[0], kpos, *operands[1:], *[s for s in stacked for c in range(2)])


def attend(qpos, kpos, q, stacked):
    rows, width = q.shape
    kernel = functools.partial(attend_kernel, len(stacked))
    outs = [("row", WIDE)] * 2
    return group_call(kernel, "attend", rows, width, kpos, [qpos, q], stacked, outs, 43)


def attend_back_kernel(blocks, more, qpos_ref, kpos_ref, q_ref, grad_ref, out_ref, lse_ref, *refs):
    before, refs = refs[:more], refs[more:]
    keys, values = refs[: 2 * blocks : 2], refs[1 : 2 * blocks : 2]
    dq_ref = refs[2 * blocks]
    dboth = refs[2 * blocks + 1 :]
    key_rows = keys[0].shape[0]
    allowed = [kpos_ref[b] <= qpos_ref[...] for b in range(blocks)]
    scale = HD**-0.5
    for half in range(q_ref.shape[1] // HD):
        lanes = slice(half * HD, (half + 1) * HD)
        q = q_ref[:, lanes] * jnp.asarray(scale, LOW)
        grad = grad_ref[:, lanes]
        lse = lse_ref[:, half * HD : half * HD + 1]
        delta = jnp.sum(grad.astype(WIDE) * out_ref[:, lanes], axis=1, keepdims=True)
        dq = []
        for b in range(blocks):
            k = keys[b][:, lanes]
            s = jnp.where(allowed[b], dot(q, k, NT), MASKED)
            p = jnp.exp(s - lse)
            dp = dot(grad, values[b][:, lanes], NT)
            ds = (p * (dp - delta)).astype(LOW)
            kind = dboth[b].dtype
            dboth[b][key_rows:, lanes] = dot(p.astype(LOW), grad, TN).astype(kind)
            dboth[b][:key_rows, lanes] = dot(ds, q, TN).astype(kind)
            dq.append(dot(ds, k, NN))
        dq_ref[:, lanes] = total_of([total_of(dq) * scale] + [r[:, lanes] for r in before])


def attend_back(qpos, kpos, q, grad, out, lse, stacked, kind, before):
    rows, width = q.shape
    results = group_call(
        functools.partial(attend_back_kernel, len(stacked), len(before)),
        "attend_back",
        rows,
        width,
        kpos,
        [qpos, q, grad, out, lse, *before],
        stacked,
        [("row", WIDE)] + [("keys", kind)] * len(stacked),
        75,
    )
    return results[0], results[1:]


def norm_back_kernel(count, *refs):
    terms = refs[:count]
    unit_ref, inverse_ref, gain_ref, base_ref = refs[count : count + 4]
    grad_ref, low_ref, gain_out_ref, bias_out_ref = refs[count + 4 :]
    grad_rows = total_of([t[...].astype(WIDE) for t in terms])
    unit = unit_ref[...]
    grad_unit = grad_rows * gain_ref[...]
    first_mean = jnp.mean(grad_unit, axis=-1, keepdims=True)
    second_mean = jnp.mean(grad_unit * unit, axis=-1, keepdims=True)
    total = base_ref[...] + inverse_ref[...] * (grad_unit - first_mean - unit * second_mean)
    grad_ref[...] = total
    low_ref[...] = total.astype(LOW)
    gain_out_ref[...] = jnp.sum(grad_rows * unit, axis=0, keepdims=True)
    bias_out_ref[...] = jnp.sum(grad_rows, axis=0, keepdims=True)


def norm_back(terms, unit, inverse, gain, base):
    rows, model = unit.shape
    fixed = lambda i: (0, 0)
    line = (1, model)
    operands = [*terms, unit, inverse, gain[None], base]
    shapes = [(rows, model)] * (len(terms) + 1) + [(rows, 1), line, (rows, model)]
    outs = [((rows, model), WIDE), ((rows, model), LOW), (line, WIDE), (line, WIDE)]
    results = tiled(
        functools.partial(norm_back_kernel, len(terms)),
        "norm_back",
        1,
        [(o, s, fixed) for o, s in zip(operands, shapes)],
        [(jax.ShapeDtypeStruct(s, t), s, fixed) for s, t in outs],
        1e9,
    )
    return results[0], results[1], results[2][0], results[3][0]


def finish(buffer, layer, terms, make, steps, ins, out, name):
    shape, block, place = out

    def kernel(*refs):
        refs[-1][...] = make(*[r[...].astype(WIDE) for r in refs[: len(terms)]])

    operands = list(terms)
    specs = [pl.BlockSpec(b, index) for b, index in ins]
    if buffer is not None:
        operands.append(buffer)
        specs.append(pl.BlockSpec(memory_space=pl.ANY))
    return pl.pallas_call(
        kernel,
        grid=(steps,),
        in_specs=specs,
        out_specs=pl.BlockSpec((1,) + block, lambda i: (layer,) + place(i)),
        out_shape=jax.ShapeDtypeStruct(shape, WIDE),
        input_output_aliases={} if buffer is None else {len(terms): 0},
        compiler_params=pltpu.CompilerParams(vmem_limit_bytes=48 * 1024 * 1024),
        cost_estimate=work(1e9),
        name=name,
    )(*operands)


def finish_matrix(buffer, layer, terms, name):
    rows, columns = terms[0].shape
    block = (rows // 4, columns)
    place = lambda i: (i, 0)
    out = ((LAYERS, rows, columns), block, place)
    make = lambda *t: total_of(t)[None]
    return finish(buffer, layer, terms, make, 4, [(block, place)] * len(terms), out, name)


def finish_projections(buffer, layer, terms):
    rows, columns = terms[0].shape
    width = columns // 3
    out = ((LAYERS, 3, rows, width), (1, rows, width), lambda i: (i, 0, 0))
    make = lambda *t: total_of(t)[None, None]
    ins = [((rows, width), lambda i: (0, i))] * len(terms)
    return finish(buffer, layer, terms, make, 3, ins, out, "finish_qkv")


def finish_gate_up(buffer, layer, gate_terms, up_terms):
    rows, columns = gate_terms[0].shape
    steps = 8
    block = (rows // steps, columns)
    out = ((LAYERS, rows, 2, columns), (rows // steps, 2, columns), lambda i: (i, 0, 0))
    count = len(gate_terms)
    make = lambda *t: jnp.stack([total_of(t[:count]), total_of(t[count:])], axis=1)[None]
    ins = [(block, lambda i: (i, 0))] * (2 * count)
    return finish(buffer, layer, gate_terms + up_terms, make, steps, ins, out, "finish_gate_up")


def bits_of(count):
    return [1 << k for k in range(count.bit_length() - 1)]


def swapped(value, axis, mask):
    count = lax.axis_size(axis)
    return lax.ppermute(value, axis, [(i, i ^ mask) for i in range(count)])


def joined(pieces, axis):
    return pieces[0] if len(pieces) == 1 else jnp.concatenate(pieces, axis=axis)


class Line:
    def __init__(self, own_rows):
        n_tensor, n_ctx = lax.axis_size("tensor"), lax.axis_size("ctx")
        tensor, ctx = lax.axis_index("tensor"), lax.axis_index("ctx")
        self.count, self.tensor = n_tensor, tensor
        row = jnp.arange(own_rows, dtype=jnp.int32)
        chip = (tensor + jnp.arange(n_tensor, dtype=jnp.int32)) % n_tensor
        place = (chip[:, None] * own_rows + row[None, :]).reshape(-1)
        block = n_tensor * own_rows
        self.places = ctx * block + place
        self.far_places = [
            jnp.where(ctx >= s, (ctx - s) * block + place, 1 << 30) for s in range(1, n_ctx)
        ]
        self.own_rows = own_rows

    def gather_rows(self, low):
        count, t = self.count, self.tensor
        send = lambda v, *route: lax.ppermute(v, "tensor", list(route))
        if count == 4:
            far = send(low, (0, 2), (2, 0), (1, 3), (3, 1))
            above = send(low, (0, 1), (1, 2), (2, 3))
            below = send(low, (1, 0), (2, 1), (3, 2))
            end = send(far, (2, 3), (1, 0))
            found = [low, jnp.where(t == 3, end, below), far, jnp.where(t == 0, end, above)]
        else:
            found = [low] + [
                send(low, *[((i + d) % count, i) for i in range(count)]) for d in range(1, count)
            ]
        return jnp.concatenate(found, axis=0)

    def sum_rows(self, low):
        rows, count, t = self.own_rows, self.count, self.tensor
        terms = [low[d * rows : (d + 1) * rows] for d in range(count)]
        send = lambda v, *route: lax.ppermute(v, "tensor", list(route))
        wide = lambda v: v.astype(WIDE)
        if count == 4:
            end = send(jnp.where(t == 0, terms[3], terms[1]), (0, 1), (3, 2))
            above = send(terms[1], (0, 1), (1, 2), (2, 3))
            below = send(terms[3], (3, 2), (2, 1), (1, 0))
            far = (wide(terms[2]) + wide(end)).astype(LOW)
            got = [send(far, (0, 2), (2, 0), (1, 3), (3, 1)), above, below]
        else:
            got = [
                send(terms[d], *[(i, (i + d) % count) for i in range(count)])
                for d in range(1, count)
            ]
        return (low, *got)

    def sum_of(self, terms):
        return total_of([terms[0][: self.own_rows].astype(WIDE)] + [t.astype(WIDE) for t in terms[1:]])

    def owner(self, low):
        count = lax.axis_size("ctx")
        if count != 2:
            return (lax.psum(low, "ctx") if count > 1 else low,)
        got = yield swapped(low, "ctx", 1)
        return (low, got)

    def far_keys(self, value):
        count = lax.axis_size("ctx")
        return [
            lax.ppermute(value, "ctx", [(i, i + s) for i in range(count - s)])
            for s in range(1, count)
        ]

    def far_key_grads(self, values):
        count = lax.axis_size("ctx")
        return [
            lax.ppermute(values[s - 1], "ctx", [(i + s, i) for i in range(count - s)])
            for s in range(1, count)
        ]


def weight_stages(shard):
    shard = yield shard
    return (yield lax.all_gather(shard, "dp"))


def grad_stages(plan, value, axis):
    got = yield lax.psum_scatter(value.astype(LOW), "dp", scatter_dimension=axis, tiled=True)
    return (yield from plan.owner(got))


def low_first(count):
    width = count.bit_length() - 1
    return sorted(range(count), key=lambda r: int(format(r, "b").zfill(width)[::-1] or "0", 2))


def pair_stages(plan, terms_of, axis):
    count = lax.axis_size("dp")

    def term(parts):
        factors = [terms_of(r) for r in parts]
        a = joined([f[0] for f in factors], 1) if axis == 0 else factors[0][0]
        b = joined([f[1] for f in factors], 1) if axis == 1 else factors[0][1]
        return outer(a, b)

    order = low_first(count)
    kept = None
    for bit in bits_of(count):
        if kept is None:
            sent = yield term(order[count // 2 :])
        else:
            kept, sent = jnp.split(kept, 2, axis=axis)
        got = yield swapped(sent.astype(LOW), "dp", bit)
        kept = (term(order[: count // 2]).astype(WIDE) if kept is None else kept) + got.astype(WIDE)
    return (yield from plan.owner(kept.astype(LOW)))


class Job:
    def __init__(self, stages):
        self.stages, self.value, self.result, self.done = stages, None, None, False
        self.advance(None)

    def advance(self, value):
        try:
            self.value = self.stages.send(value)
        except StopIteration as end:
            self.done, self.result, self.value = True, end.value, None

    def finish(self):
        while not self.done:
            self.advance(self.value)
        return self.result


def meanwhile(value, *jobs):
    open_jobs = [j for j in jobs if j is not None and not j.done]
    if not open_jobs:
        return value
    value, held = lax.optimization_barrier((value, tuple(j.value for j in open_jobs)))
    for job, got in zip(open_jobs, held):
        job.advance(got)
    return value


def held(value, *jobs):
    open_jobs = [j for j in jobs if j is not None and not j.done]
    if not open_jobs:
        return value
    value, kept = lax.optimization_barrier((value, tuple(j.value for j in open_jobs)))
    for job, got in zip(open_jobs, kept):
        job.value = got
    return value


def shards(
    tokens,
    cotangent,
    norm_gains,
    norm_biases,
    qkv_weight,
    qkv_bias,
    out_weight,
    gate_up_weight,
    down_weight,
):
    own_rows = tokens.shape[1]
    model = tokens.shape[2]
    heads_width = qkv_weight.shape[3]
    plan = Line(own_rows)
    tables = rotary_tables(plan.places)
    tables_back = (tables[0], -tables[1], -tables[2])
    qpos = plan.places[:, None]
    near_places = plan.places[None, None, :]
    far_places = jnp.stack(plan.far_places)[:, None, :]
    all_places = jnp.concatenate([near_places, far_places])
    gains = (norm_gains)
    biases = (norm_biases)
    qkv_bias_own = lax.dynamic_slice_in_dim(qkv_bias, lax.axis_index("tensor") * heads_width, heads_width, 2)

    def weight_jobs(layer, after):
        (qkv_all, out_all, gate_up_all, down_all), after = lax.optimization_barrier(
            ((qkv_weight, out_weight, gate_up_weight, down_weight), after)
        )
        matrices = {
            "qkv": jnp.transpose(qkv_all[layer], (1, 0, 2)),
            "out": out_all[layer],
            "gate": gate_up_all[layer, :, 0],
            "up": gate_up_all[layer, :, 1],
            "down": down_all[layer],
        }
        return {n: Job(weight_stages(v)) for n, v in matrices.items()}, after

    now, unused = weight_jobs(0, ())
    for name in ("qkv", "out", "gate", "up"):
        now[name].advance(now[name].value)
    stream = tokens[0].astype(WIDE)
    later = {}
    saved = []
    for layer in range(LAYERS):
        last = layer + 1 == LAYERS
        normed_one, unit_one, inverse_one = layer_norm_rows(
            stream, gains[layer, 0], biases[layer, 0]
        )
        rows_one = plan.gather_rows(normed_one.astype(LOW))
        if layer == 0:
            rows_one = meanwhile(rows_one, now["qkv"], now["down"])
        else:
            rows_one = meanwhile(rows_one, now["out"], now["gate"], now["down"])
        qkv_full = now["qkv"].finish()
        queries, keys_values = project(rows_one, qkv_full, qkv_bias_own[layer], tables)
        if layer == 0:
            late_cotangent, queries = lax.optimization_barrier((cotangent[0], queries))
            grad_stream = late_cotangent.astype(WIDE)
            branch = plan.gather_rows(late_cotangent)
        prepared = {}
        if not last:
            prepared, queries = weight_jobs(layer + 1, queries)
        far_kv = plan.far_keys(keys_values)
        attended, lse = attend(qpos, all_places, queries, [keys_values, *far_kv])
        attended_low = meanwhile(attended.astype(LOW), now["out"])
        attended_low = held(attended_low, *map(prepared.get, ("gate", "up")))
        if layer == 0:
            attended_low, branch = lax.optimization_barrier((attended_low, branch))
        else:
            attended_low = meanwhile(attended_low, now["up"])
        out_full = now["out"].finish()
        mid = stream + plan.sum_of(plan.sum_rows(times_wide(attended_low, out_full, "out")))
        mid = meanwhile(mid, now["gate"])
        if layer > 0:
            mid = meanwhile(mid, now["down"])
        else:
            later = prepared
        normed_two, unit_two, inverse_two = layer_norm_rows(mid, gains[layer, 1], biases[layer, 1])
        rows_two = plan.gather_rows(normed_two.astype(LOW))
        rows_two = meanwhile(rows_two, now["up"], now["down"], later.get("qkv"))
        flat = lambda v: v.reshape(v.shape[0] * v.shape[1], v.shape[2])
        gate_full, up_full = flat(now["gate"].finish()), flat(now["up"].finish())
        gate, up, activated = gate_up_rows(rows_two, gate_full, up_full)
        activated = meanwhile(activated, later.get("out"), later.get("gate"))
        down_full = now["down"].finish()
        if not last:
            stream = mid + plan.sum_of(
                plan.sum_rows(times_wide(activated, down_full, "down"))
            )
            stream = meanwhile(stream, later.get("qkv"), later.get("up"))
        saved.append(
            (
                (qkv_full, out_full, gate_full, up_full, down_full),
                (rows_one, unit_one, inverse_one),
                (queries, keys_values, far_kv, attended, attended_low, lse),
                (rows_two, unit_two, inverse_two),
                (gate, up, activated),
            )
        )
        now = later
    grad_jobs = [None] * LAYERS
    gain_grads = [None] * LAYERS
    bias_grads = [None] * LAYERS
    qkv_bias_grads = [None] * LAYERS
    for layer in range(LAYERS - 1, -1, -1):
        (
            (qkv_full, out_full, gate_full, up_full, down_full),
            (rows_one, unit_one, inverse_one),
            (queries, keys_values, far_kv, attended, attended_low, lse),
            (rows_two, unit_two, inverse_two),
            (gate, up, activated),
        ) = saved[layer]
        mine = {}
        grad_jobs[layer] = mine
        above = grad_jobs[layer + 1] if layer + 1 < LAYERS else {}
        old = lambda *keys: [above.get(k) for k in keys]

        def own_part(value, r):
            index = lax.axis_index("dp") ^ r
            width = value.shape[1] // lax.axis_size("dp")
            return lax.dynamic_slice_in_dim(value, index * width, width, 1)

        def in_job(a, b):
            return Job(grad_stages(plan, outer(a, b), 0))

        def out_job(a, b):
            return Job(grad_stages(plan, outer(a, b), 1))

        if layer + 1 < LAYERS:
            branch = plan.gather_rows(grad_low)
        branch = meanwhile(branch, *old("gate", "up", "out"))
        if layer == 0:
            down_grad, branch = lax.optimization_barrier(
                (outer(activated, branch), branch)
            )
            mine["down"] = Job(grad_stages(plan, down_grad, 1))
        grad_gate, grad_up = gate_up_back(branch, down_full, gate, up)
        partial_in = gate_up_in(grad_gate, grad_up, gate_full, up_full)
        summed = plan.sum_rows(partial_in)
        summed = meanwhile(summed, *old("up", "out", "qkv"))
        hidden_grad, hidden_low, gain_two, bias_two = norm_back(
            summed, unit_two, inverse_two, gains[layer, 1], grad_stream
        )
        hidden_low, (branch, grad_gate, grad_up) = lax.optimization_barrier(
            (hidden_low, (branch, grad_gate, grad_up))
        )
        if layer > 0:
            mine["down"] = out_job(activated, branch)
        mine["gate"] = in_job(rows_two, grad_gate)
        if layer == 0:
            mine["up"] = in_job(rows_two, grad_up)
        top = layer + 1 == LAYERS
        if top:
            late, hidden_low = lax.optimization_barrier((activated, hidden_low))
            partial_out = times_wide(late, down_full, "down")
        attention = plan.gather_rows(hidden_low)
        attention = meanwhile(attention, *old("qkv"))
        if layer == 0:
            attention = meanwhile(attention, mine["down"])
        if top:
            attention, partial_out = lax.optimization_barrier((attention, partial_out))
            output = (mid + plan.sum_of(plan.sum_rows(partial_out))).astype(LOW)[None]
        grad_attended = out_back(attention, out_full)
        shared = (queries, grad_attended, attended, lse)
        far_queries, far_grads = attend_back(qpos, far_places, *shared, far_kv, LOW, [])
        returned = plan.far_key_grads(far_grads)
        grad_queries, grad_kv = attend_back(
            qpos, near_places, *shared, [keys_values], WIDE, [far_queries]
        )
        if top:
            grad_queries, output = lax.optimization_barrier((grad_queries, output))
        projected, qkv_bias_grads[layer] = project_back(
            grad_queries, grad_kv[0], returned, tables_back
        )
        projected, (attention, grad_up) = lax.optimization_barrier(
            (projected, (attention, grad_up))
        )
        if layer > 0:
            mine["up"] = in_job(rows_two, grad_up)
        if layer == 0:
            mine["out"] = Job(
                pair_stages(plan, lambda r, a=attention: (attended_low, own_part(a, r)), 1)
            )
        else:
            mine["out"] = out_job(attended_low, attention)
        projected = meanwhile(projected, mine["down"] if layer > 0 else None, *old("qkv"))
        if not top:
            above_done, projected = lax.optimization_barrier(
                ({k: j.finish() for k, j in above.items()}, projected)
            )
            sums = above_done
            results = [
                finish_projections(None, layer + 1, sums["qkv"]),
                finish_matrix(None, layer + 1, sums["out"], "finish_out"),
                finish_gate_up(None, layer + 1, sums["gate"], sums["up"]),
                finish_matrix(None, layer + 1, sums["down"], "finish_down"),
            ]
        if layer == 0:
            mine["qkv"] = Job(
                pair_stages(plan, lambda r, b=projected: (own_part(rows_one, r), b), 0)
            )
            projected = meanwhile(projected, *map(mine.get, ("qkv", "out", "gate")))
        partial_in = project_in(projected, qkv_full)
        if layer == 0:
            partial_in = meanwhile(partial_in, *map(mine.get, ("down", "up", "qkv")))
            partial_in = held(partial_in, mine["out"])
        summed = plan.sum_rows(partial_in)
        if layer > 0:
            summed = meanwhile(summed, mine["down"])
        else:
            summed = meanwhile(summed, *map(mine.get, ("gate", "out", "qkv")))
        grad_stream, grad_low, gain_one, bias_one = norm_back(
            summed, unit_one, inverse_one, gains[layer, 0], hidden_grad
        )
        if layer > 0:
            grad_low, projected = lax.optimization_barrier((grad_low, projected))
            mine["qkv"] = in_job(rows_one, projected)
            grad_low = meanwhile(grad_low, mine["gate"])
        gain_grads[layer] = jnp.stack([gain_one, gain_two])
        bias_grads[layer] = jnp.stack([bias_one, bias_two])

    tokens_grad = grad_low[None]
    padded_bias = lax.dynamic_update_slice_in_dim(
        jnp.zeros((LAYERS, 3, qkv_bias.shape[2]), WIDE),
        jnp.stack(qkv_bias_grads),
        lax.axis_index("tensor") * heads_width,
        2,
    )
    small = jnp.concatenate(
        [
            (jnp.stack(gain_grads)).reshape(LAYERS * 2, model),
            (jnp.stack(bias_grads)).reshape(LAYERS * 2, model),
            padded_bias.reshape(LAYERS * 3, qkv_bias.shape[2]),
        ],
        axis=0,
    )
    for axis in ("ctx", "dp", "tensor"):
        for bit in bits_of(lax.axis_size(axis)):
            small = small + swapped(small, axis, bit)
        small, results = lax.optimization_barrier((small, results))
    sums = {k: j.finish() for k, j in grad_jobs[0].items()}
    results = [
        finish_projections(results[0], 0, sums["qkv"]),
        finish_matrix(results[1], 0, sums["out"], "finish_out"),
        finish_gate_up(results[2], 0, sums["gate"], sums["up"]),
        finish_matrix(results[3], 0, sums["down"], "finish_down"),
    ]
    return (
        output,
        tokens_grad,
        small[: LAYERS * 2].reshape(LAYERS, 2, model),
        small[LAYERS * 2 : LAYERS * 4].reshape(LAYERS, 2, model),
        jnp.transpose(results[0], (0, 2, 1, 3)),
        small[LAYERS * 4 :].reshape(LAYERS, 3, qkv_bias.shape[2]),
        *results[1:],
    )


def solution(mesh):
    rows = P("dp", ("ctx", "tensor"), None)
    wide = P(None, "dp", None, "tensor")
    tall = P(None, "tensor", "dp")
    return jax.shard_map(
        shards,
        mesh=mesh,
        in_specs=(rows, rows, P(), P(), wide, P(), tall, wide, tall),
        out_specs=(rows, rows, P(), P(), wide, P(), tall, wide, tall),
        check_vma=False,
    )
```

```python
import functools

import jax
import jax.numpy as jnp
from jax import lax
from jax.experimental import pallas as pl
from jax.experimental.pallas import tpu as pltpu
from jax.sharding import PartitionSpec as P

HD = 64
ROT = 16
LAYERS = 2

MASKED = -1e30
EPSILON = 1e-05
LOW = jnp.bfloat16
WIDE = jnp.float32


def layer_norm_rows(stream, gain, bias):
    row_mean = jnp.mean(stream, axis=-1, keepdims=True)
    centered = stream - row_mean
    inverse = lax.rsqrt(jnp.mean(centered * centered, axis=-1, keepdims=True) + EPSILON)
    unit_rows = centered * inverse
    return (unit_rows * gain + bias, unit_rows, inverse)


def rotary_tables(positions):
    half_rot = ROT // 2
    frequency = 10000.0 ** (-(jnp.arange(half_rot, dtype=jnp.float32) * 2.0) / ROT)
    angles = positions.astype(jnp.float32)[:, None] * frequency[None, :]
    cosine, sine = jnp.cos(angles), jnp.sin(angles)
    rest = jnp.zeros((angles.shape[0], HD - ROT), WIDE)
    none = jnp.zeros_like(sine)
    heads = lambda *parts: jnp.tile(jnp.concatenate(parts, axis=1), (1, PAIR // HD))
    return (
        heads(cosine, cosine, rest + 1.0),
        heads(-sine, none, rest),
        heads(none, sine, rest),
    )


def rotated(flat, cos_ref, right_ref, left_ref):
    shift = ROT // 2
    found = []
    for start in range(0, flat.shape[1], PAIR):
        v = flat[:, start : start + PAIR]
        right, left = pltpu.roll(v, PAIR - shift, 1), pltpu.roll(v, shift, 1)
        found.append(v * cos_ref[...] + right * right_ref[...] + left * left_ref[...])
    return jnp.concatenate(found, axis=1)


def dot(a, b, dims):
    return lax.dot_general(a, b, (dims, ((), ())), preferred_element_type=WIDE)


PAIR = 128


NN = ((1,), (0,))
NT = ((1,), (1,))
TN = ((0,), (0,))


def total_of(terms):
    return functools.reduce(lambda a, b: a + b, terms)


def work(flops):
    return pl.CostEstimate(flops=int(flops), bytes_accessed=0, transcendentals=0)


TILE = 512


def tiled(kernel, name, steps, ins, outs, flops):
    return pl.pallas_call(
        kernel,
        grid=(steps,),
        in_specs=[pl.BlockSpec(block, index) for _, block, index in ins],
        out_specs=[pl.BlockSpec(block, index) for _, block, index in outs],
        out_shape=[shape for shape, _, _ in outs],
        compiler_params=pltpu.CompilerParams(vmem_limit_bytes=48 * 1024 * 1024),
        cost_estimate=work(2.5 * flops),
        name=name,
    )(*[array for array, _, _ in ins])


def whole_block(array):
    return (array, array.shape, lambda i: (0,) * array.ndim)


def column_block(array):
    return (array, (array.shape[0], TILE), lambda i: (0, i))


def row_block(array):
    return (array, (TILE, array.shape[1]), lambda i: (i, 0))


def gate_up_kernel(rows_ref, gate_w_ref, up_w_ref, gate_ref, up_ref, activated_ref):
    rows = rows_ref[...]
    gate = dot(rows, gate_w_ref[...], NN)
    up = dot(rows, up_w_ref[...], NN)
    gate_ref[...] = gate
    up_ref[...] = up
    activated_ref[...] = (gate * jax.nn.sigmoid(gate) * up).astype(LOW)


def gate_up_rows(rows, gate_weight, up_weight):
    count, hidden = rows.shape[0], gate_weight.shape[1]
    shapes = [jax.ShapeDtypeStruct((count, hidden), t) for t in (WIDE, WIDE, LOW)]
    return tiled(
        gate_up_kernel,
        "gate_up",
        pl.cdiv(hidden, TILE),
        [whole_block(rows), column_block(gate_weight), column_block(up_weight)],
        [column_block(s) for s in shapes],
        4 * rows.size * hidden,
    )


def back_sum(rows, weight_ref):
    width = weight_ref.shape[2]
    return total_of(
        dot(rows[:, r * width : (r + 1) * width], weight_ref[r], NT)
        for r in range(weight_ref.shape[0])
    )


def tall_block(array):
    return (array, (array.shape[0], TILE, array.shape[2]), lambda i: (0, i, 0))


def gate_up_back_kernel(rows_ref, weight_ref, gate_ref, up_ref, grad_gate_ref, grad_up_ref):
    grad = back_sum(rows_ref[...], weight_ref)
    gate, up = gate_ref[...], up_ref[...]
    s = jax.nn.sigmoid(gate)
    grad_gate_ref[...] = (grad * up * s * (1.0 + gate * (1.0 - s))).astype(LOW)
    grad_up_ref[...] = (grad * (gate * s)).astype(LOW)


def gate_up_back(rows, down_weight, gate, up):
    count, hidden = gate.shape
    shape = jax.ShapeDtypeStruct((count, hidden), LOW)
    return tiled(
        gate_up_back_kernel,
        "gate_up_back",
        pl.cdiv(hidden, TILE),
        [whole_block(rows), tall_block(down_weight), column_block(gate), column_block(up)],
        [column_block(shape)] * 2,
        2 * rows.size * hidden,
    )


def out_back_kernel(rows_ref, weight_ref, out_ref):
    out_ref[...] = back_sum(rows_ref[...], weight_ref).astype(LOW)


def out_back(rows, weight):
    shape = jax.ShapeDtypeStruct((rows.shape[0], weight.shape[1]), LOW)
    return tiled(
        out_back_kernel,
        "out_back",
        shape.shape[1] // TILE,
        [whole_block(rows), tall_block(weight)],
        [column_block(shape)],
        2 * rows.size * shape.shape[1],
    )[0]


def wide_kernel(rows_ref, weight_ref, out_ref):
    out_ref[...] = dot(rows_ref[...], weight_ref[0], NN).astype(LOW)


def times_wide(rows, weight, name):
    blocks, depth, width = weight.shape
    per = width // TILE
    shape = jax.ShapeDtypeStruct((rows.shape[0], blocks * width), LOW)
    return tiled(
        wide_kernel,
        name,
        blocks * per,
        [whole_block(rows), (weight, (1, depth, TILE), lambda i: (i // per, 0, i % per))],
        [column_block(shape)],
        2 * rows.size * blocks * width,
    )[0]


def gate_up_in_kernel(gate_ref, up_ref, gate_w_ref, up_w_ref, out_ref):
    total = dot(gate_ref[...], gate_w_ref[...], NT) + dot(up_ref[...], up_w_ref[...], NT)
    out_ref[...] = total.astype(LOW)


def gate_up_in(grad_gate, grad_up, gate_weight, up_weight):
    shape = jax.ShapeDtypeStruct((grad_gate.shape[0], gate_weight.shape[0]), LOW)
    return tiled(
        gate_up_in_kernel,
        "gate_up_in",
        shape.shape[1] // TILE,
        [whole_block(grad_gate), whole_block(grad_up), row_block(gate_weight), row_block(up_weight)],
        [column_block(shape)],
        4 * grad_gate.size * shape.shape[1],
    )[0]


def project_in_kernel(rows_ref, weight_ref, out_ref):
    width = weight_ref.shape[3]
    out_ref[...] = total_of(
        dot(rows_ref[:, c * width : (c + 1) * width], weight_ref[0, c], NT) for c in range(3)
    ).astype(LOW)


def project_in(rows, weight):
    blocks, three, depth, width = weight.shape
    per = depth // TILE
    shape = jax.ShapeDtypeStruct((rows.shape[0], blocks * depth), LOW)
    return tiled(
        project_in_kernel,
        "project_in",
        blocks * per,
        [whole_block(rows), (weight, (1, three, TILE, width), lambda i: (i // per, 0, i % per, 0))],
        [column_block(shape)],
        2 * rows.size * blocks * depth,
    )[0]


def outer_kernel(a_ref, b_ref, out_ref):
    out_ref[...] = dot(a_ref[...], b_ref[...], TN).astype(LOW)


def outer(a, b):
    shape = jax.ShapeDtypeStruct((a.shape[1], b.shape[1]), LOW)
    return tiled(
        outer_kernel,
        "outer",
        pl.cdiv(a.shape[1], TILE),
        [column_block(a), whole_block(b)],
        [row_block(shape)],
        a.size * b.shape[1] * 0.8,
    )[0]


def project_kernel(rows_ref, weight_ref, bias_ref, cos_ref, right_ref, left_ref, q_ref, kv_ref):
    blocks, _, depth, width = weight_ref.shape
    flat = dot(rows_ref[...], weight_ref[...].reshape(blocks * depth, width), NN) + bias_ref[0]
    step = pl.program_id(0)

    @pl.when(step == 0)
    def _():
        kv_ref[...] = rotated(flat, cos_ref, right_ref, left_ref).astype(LOW)

    @pl.when(step == 1)
    def _():
        kv_ref[...] = flat.astype(LOW)

    @pl.when(step == 2)
    def _():
        q_ref[...] = rotated(flat, cos_ref, right_ref, left_ref).astype(LOW)


def project(rows, weight, bias, tables):
    count = rows.shape[0]
    blocks, _, depth, width = weight.shape
    fixed = lambda i: (0, 0)
    shapes = [jax.ShapeDtypeStruct((k * count, width), LOW) for k in (1, 2)]
    return tiled(
        project_kernel,
        "project",
        3,
        [
            whole_block(rows),
            (weight, (blocks, 1, depth, width), lambda i: (0, (i + 1) % 3, 0, 0)),
            (bias[:, None, :], (1, 1, width), lambda i: ((i + 1) % 3, 0, 0)),
        ]
        + [(t, (count, PAIR), fixed) for t in tables],
        [
            (shapes[0], (count, width), fixed),
            (shapes[1], (count, width), lambda i: (jnp.minimum(i, 1), 0)),
        ],
        6 * rows.size * width,
    )


def project_back_kernel(far, dq_ref, dkv_ref, *refs):
    far_refs = refs[:far]
    cos_ref, right_ref, left_ref, out_ref, sum_ref = refs[far:]
    step = pl.program_id(0)

    def put(value):
        out_ref[...] = value.astype(LOW)
        sum_ref[0] = jnp.sum(value, axis=0, keepdims=True)

    def key_value():
        return total_of([dkv_ref[...]] + [r[...].astype(WIDE) for r in far_refs])

    @pl.when(step == 0)
    def _():
        put(rotated(dq_ref[...], cos_ref, right_ref, left_ref))

    @pl.when(step == 1)
    def _():
        put(rotated(key_value(), cos_ref, right_ref, left_ref))

    @pl.when(step == 2)
    def _():
        put(key_value())


def project_back(dq, dkv, far, tables):
    count, width = dq.shape
    fixed = lambda i: (0, 0)
    lower = pl.BlockSpec((count, width), lambda i: (jnp.maximum(i - 1, 0), 0))
    out, sums = pl.pallas_call(
        functools.partial(project_back_kernel, len(far)),
        grid=(3,),
        in_specs=[pl.BlockSpec((count, width), fixed)]
        + [lower] * (1 + len(far))
        + [pl.BlockSpec((count, PAIR), fixed)] * 3,
        out_specs=[
            pl.BlockSpec((count, width), lambda i: (0, i)),
            pl.BlockSpec((1, 1, width), lambda i: (i, 0, 0)),
        ],
        out_shape=[
            jax.ShapeDtypeStruct((count, 3 * width), LOW),
            jax.ShapeDtypeStruct((3, 1, width), WIDE),
        ],
        compiler_params=pltpu.CompilerParams(vmem_limit_bytes=32 * 1024 * 1024),
        cost_estimate=work(14000 * count * width),
        name="project_back",
    )(dq, dkv, *far, *tables)
    return out, sums[:, 0]


GROUP = 256


def attend_kernel(blocks, qpos_ref, kpos_ref, q_ref, *refs):
    keys, values = refs[: 2 * blocks : 2], refs[1 : 2 * blocks : 2]
    out_ref, lse_ref = refs[2 * blocks :]
    allowed = [kpos_ref[b] <= qpos_ref[...] for b in range(blocks)]
    for half in range(q_ref.shape[1] // HD):
        lanes = slice(half * HD, (half + 1) * HD)
        q = q_ref[:, lanes] * jnp.asarray(HD**-0.5, LOW)
        top, total, acc = None, None, None
        for b in range(blocks):
            s = jnp.where(allowed[b], dot(q, keys[b][:, lanes], NT), MASKED)
            block_top = jnp.max(s, axis=1, keepdims=True)
            new_top = block_top if b == 0 else jnp.maximum(top, block_top)
            p = jnp.exp(s - new_top)
            block_total = jnp.sum(p, axis=1, keepdims=True)
            block_acc = dot(p.astype(LOW), values[b][:, lanes], NN)
            if b == 0:
                total, acc = block_total, block_acc
            else:
                factor = jnp.exp(top - new_top)
                total = total * factor + block_total
                acc = acc * factor + block_acc
            top = new_top
        out_ref[:, lanes] = acc / total
        lse_ref[:, lanes] = jnp.broadcast_to(top + jnp.log(total), acc.shape)


def group_call(kernel, name, rows, width, kpos, operands, stacked, outs, flops):
    blocks, _, key_rows = kpos.shape
    group = GROUP if blocks <= 2 else PAIR
    column = lambda i: (0, i)
    specs = {
        "row": pl.BlockSpec((rows, group), column),
        "keys": pl.BlockSpec((2 * key_rows, group), column),
    }
    shapes = {"row": (rows, width), "keys": (2 * key_rows, width)}
    halves = [pl.BlockSpec((key_rows, group), lambda i, c=c: (c, i)) for c in range(2)]
    common = [
        pl.BlockSpec((rows, 1), lambda i: (0, 0)),
        pl.BlockSpec((blocks, 1, key_rows), lambda i: (0, 0, 0)),
    ]
    return pl.pallas_call(
        kernel,
        grid=(width // group,),
        in_specs=common + [specs["row"]] * (len(operands) - 1) + halves * len(stacked),
        out_specs=[specs[k] for k, _ in outs],
        out_shape=[jax.ShapeDtypeStruct(shapes[k], t) for k, t in outs],
        compiler_params=pltpu.CompilerParams(vmem_limit_bytes=40 * 1024 * 1024),
        cost_estimate=work(flops * rows * key_rows * blocks * width),
        name=name,
    )(operands[0], kpos, *operands[1:], *[s for s in stacked for c in range(2)])


def attend(qpos, kpos, q, stacked):
    rows, width = q.shape
    kernel = functools.partial(attend_kernel, len(stacked))
    outs = [("row", WIDE)] * 2
    return group_call(kernel, "attend", rows, width, kpos, [qpos, q], stacked, outs, 43)


def attend_back_kernel(blocks, more, qpos_ref, kpos_ref, q_ref, grad_ref, out_ref, lse_ref, *refs):
    before, refs = refs[:more], refs[more:]
    keys, values = refs[: 2 * blocks : 2], refs[1 : 2 * blocks : 2]
    dq_ref = refs[2 * blocks]
    dboth = refs[2 * blocks + 1 :]
    key_rows = keys[0].shape[0]
    allowed = [kpos_ref[b] <= qpos_ref[...] for b in range(blocks)]
    scale = HD**-0.5
    for half in range(q_ref.shape[1] // HD):
        lanes = slice(half * HD, (half + 1) * HD)
        q = q_ref[:, lanes] * jnp.asarray(scale, LOW)
        grad = grad_ref[:, lanes]
        lse = lse_ref[:, half * HD : half * HD + 1]
        delta = jnp.sum(grad.astype(WIDE) * out_ref[:, lanes], axis=1, keepdims=True)
        dq = []
        for b in range(blocks):
            k = keys[b][:, lanes]
            s = jnp.where(allowed[b], dot(q, k, NT), MASKED)
            p = jnp.exp(s - lse)
            dp = dot(grad, values[b][:, lanes], NT)
            ds = (p * (dp - delta)).astype(LOW)
            kind = dboth[b].dtype
            dboth[b][key_rows:, lanes] = dot(p.astype(LOW), grad, TN).astype(kind)
            dboth[b][:key_rows, lanes] = dot(ds, q, TN).astype(kind)
            dq.append(dot(ds, k, NN))
        dq_ref[:, lanes] = total_of([total_of(dq) * scale] + [r[:, lanes] for r in before])


def attend_back(qpos, kpos, q, grad, out, lse, stacked, kind, before):
    rows, width = q.shape
    results = group_call(
        functools.partial(attend_back_kernel, len(stacked), len(before)),
        "attend_back",
        rows,
        width,
        kpos,
        [qpos, q, grad, out, lse, *before],
        stacked,
        [("row", WIDE)] + [("keys", kind)] * len(stacked),
        75,
    )
    return results[0], results[1:]


def norm_back_kernel(count, *refs):
    terms = refs[:count]
    unit_ref, inverse_ref, gain_ref, base_ref = refs[count : count + 4]
    grad_ref, low_ref, gain_out_ref, bias_out_ref = refs[count + 4 :]
    grad_rows = total_of([t[...].astype(WIDE) for t in terms])
    unit = unit_ref[...]
    grad_unit = grad_rows * gain_ref[...]
    first_mean = jnp.mean(grad_unit, axis=-1, keepdims=True)
    second_mean = jnp.mean(grad_unit * unit, axis=-1, keepdims=True)
    total = base_ref[...] + inverse_ref[...] * (grad_unit - first_mean - unit * second_mean)
    grad_ref[...] = total
    low_ref[...] = total.astype(LOW)
    gain_out_ref[...] = jnp.sum(grad_rows * unit, axis=0, keepdims=True)
    bias_out_ref[...] = jnp.sum(grad_rows, axis=0, keepdims=True)


def norm_back(terms, unit, inverse, gain, base):
    rows, model = unit.shape
    fixed = lambda i: (0, 0)
    line = (1, model)
    operands = [*terms, unit, inverse, gain[None], base]
    shapes = [(rows, model)] * (len(terms) + 1) + [(rows, 1), line, (rows, model)]
    outs = [((rows, model), WIDE), ((rows, model), LOW), (line, WIDE), (line, WIDE)]
    results = tiled(
        functools.partial(norm_back_kernel, len(terms)),
        "norm_back",
        1,
        [(o, s, fixed) for o, s in zip(operands, shapes)],
        [(jax.ShapeDtypeStruct(s, t), s, fixed) for s, t in outs],
        1e9,
    )
    return results[0], results[1], results[2][0], results[3][0]


def finish(buffer, layer, terms, make, steps, ins, out, name):
    shape, block, place = out

    def kernel(*refs):
        refs[-1][...] = make(*[r[...].astype(WIDE) for r in refs[: len(terms)]])

    operands = list(terms)
    specs = [pl.BlockSpec(b, index) for b, index in ins]
    if buffer is not None:
        operands.append(buffer)
        specs.append(pl.BlockSpec(memory_space=pl.ANY))
    return pl.pallas_call(
        kernel,
        grid=(steps,),
        in_specs=specs,
        out_specs=pl.BlockSpec((1,) + block, lambda i: (layer,) + place(i)),
        out_shape=jax.ShapeDtypeStruct(shape, WIDE),
        input_output_aliases={} if buffer is None else {len(terms): 0},
        compiler_params=pltpu.CompilerParams(vmem_limit_bytes=48 * 1024 * 1024),
        cost_estimate=work(1e9),
        name=name,
    )(*operands)


def finish_matrix(buffer, layer, terms, name):
    rows, columns = terms[0].shape
    block = (rows // 4, columns)
    place = lambda i: (i, 0)
    out = ((LAYERS, rows, columns), block, place)
    make = lambda *t: total_of(t)[None]
    return finish(buffer, layer, terms, make, 4, [(block, place)] * len(terms), out, name)


def finish_projections(buffer, layer, terms):
    rows, columns = terms[0].shape
    width = columns // 3
    out = ((LAYERS, 3, rows, width), (1, rows, width), lambda i: (i, 0, 0))
    make = lambda *t: total_of(t)[None, None]
    ins = [((rows, width), lambda i: (0, i))] * len(terms)
    return finish(buffer, layer, terms, make, 3, ins, out, "finish_qkv")


def finish_gate_up(buffer, layer, gate_terms, up_terms):
    rows, columns = gate_terms[0].shape
    steps = 8
    block = (rows // steps, columns)
    out = ((LAYERS, rows, 2, columns), (rows // steps, 2, columns), lambda i: (i, 0, 0))
    count = len(gate_terms)
    make = lambda *t: jnp.stack([total_of(t[:count]), total_of(t[count:])], axis=1)[None]
    ins = [(block, lambda i: (i, 0))] * (2 * count)
    return finish(buffer, layer, gate_terms + up_terms, make, steps, ins, out, "finish_gate_up")


def bits_of(count):
    return [1 << k for k in range(count.bit_length() - 1)]


def swapped(value, axis, mask):
    count = lax.axis_size(axis)
    return lax.ppermute(value, axis, [(i, i ^ mask) for i in range(count)])


def joined(pieces, axis):
    return pieces[0] if len(pieces) == 1 else jnp.concatenate(pieces, axis=axis)


class Line:
    def __init__(self, own_rows):
        n_tensor, n_ctx = lax.axis_size("tensor"), lax.axis_size("ctx")
        tensor, ctx = lax.axis_index("tensor"), lax.axis_index("ctx")
        self.count, self.tensor = n_tensor, tensor
        row = jnp.arange(own_rows, dtype=jnp.int32)
        chip = (tensor + jnp.arange(n_tensor, dtype=jnp.int32)) % n_tensor
        place = (chip[:, None] * own_rows + row[None, :]).reshape(-1)
        block = n_tensor * own_rows
        self.places = ctx * block + place
        self.far_places = [
            jnp.where(ctx >= s, (ctx - s) * block + place, 1 << 30) for s in range(1, n_ctx)
        ]
        self.own_rows = own_rows

    def gather_rows(self, low):
        count, t = self.count, self.tensor
        send = lambda v, *route: lax.ppermute(v, "tensor", list(route))
        if count == 4:
            far = send(low, (0, 2), (2, 0), (1, 3), (3, 1))
            above = send(low, (0, 1), (1, 2), (2, 3))
            below = send(low, (1, 0), (2, 1), (3, 2))
            end = send(far, (2, 3), (1, 0))
            found = [low, jnp.where(t == 3, end, below), far, jnp.where(t == 0, end, above)]
        else:
            found = [low] + [
                send(low, *[((i + d) % count, i) for i in range(count)]) for d in range(1, count)
            ]
        return jnp.concatenate(found, axis=0)

    def sum_rows(self, low):
        rows, count, t = self.own_rows, self.count, self.tensor
        terms = [low[d * rows : (d + 1) * rows] for d in range(count)]
        send = lambda v, *route: lax.ppermute(v, "tensor", list(route))
        wide = lambda v: v.astype(WIDE)
        if count == 4:
            end = send(jnp.where(t == 0, terms[3], terms[1]), (0, 1), (3, 2))
            above = send(terms[1], (0, 1), (1, 2), (2, 3))
            below = send(terms[3], (3, 2), (2, 1), (1, 0))
            far = (wide(terms[2]) + wide(end)).astype(LOW)
            got = [send(far, (0, 2), (2, 0), (1, 3), (3, 1)), above, below]
        else:
            got = [
                send(terms[d], *[(i, (i + d) % count) for i in range(count)])
                for d in range(1, count)
            ]
        return (low, *got)

    def sum_of(self, terms):
        return total_of([terms[0][: self.own_rows].astype(WIDE)] + [t.astype(WIDE) for t in terms[1:]])

    def owner(self, low):
        count = lax.axis_size("ctx")
        if count != 2:
            return (lax.psum(low, "ctx") if count > 1 else low,)
        got = yield swapped(low, "ctx", 1)
        return (low, got)

    def far_keys(self, value):
        count = lax.axis_size("ctx")
        return [
            lax.ppermute(value, "ctx", [(i, i + s) for i in range(count - s)])
            for s in range(1, count)
        ]

    def far_key_grads(self, values):
        count = lax.axis_size("ctx")
        return [
            lax.ppermute(values[s - 1], "ctx", [(i + s, i) for i in range(count - s)])
            for s in range(1, count)
        ]


def weight_stages(shard):
    shard = yield shard
    return (yield lax.all_gather(shard, "dp"))


def grad_stages(plan, value, axis):
    got = yield lax.psum_scatter(value.astype(LOW), "dp", scatter_dimension=axis, tiled=True)
    return (yield from plan.owner(got))


def low_first(count):
    width = count.bit_length() - 1
    return sorted(range(count), key=lambda r: int(format(r, "b").zfill(width)[::-1] or "0", 2))


def pair_stages(plan, terms_of, axis):
    count = lax.axis_size("dp")

    def term(parts):
        factors = [terms_of(r) for r in parts]
        a = joined([f[0] for f in factors], 1) if axis == 0 else factors[0][0]
        b = joined([f[1] for f in factors], 1) if axis == 1 else factors[0][1]
        return outer(a, b)

    order = low_first(count)
    kept = None
    for bit in bits_of(count):
        if kept is None:
            sent = yield term(order[count // 2 :])
        else:
            kept, sent = jnp.split(kept, 2, axis=axis)
        got = yield swapped(sent.astype(LOW), "dp", bit)
        kept = (term(order[: count // 2]).astype(WIDE) if kept is None else kept) + got.astype(WIDE)
    return (yield from plan.owner(kept.astype(LOW)))


class Job:
    def __init__(self, stages):
        self.stages, self.value, self.result, self.done = stages, None, None, False
        self.advance(None)

    def advance(self, value):
        try:
            self.value = self.stages.send(value)
        except StopIteration as end:
            self.done, self.result, self.value = True, end.value, None

    def finish(self):
        while not self.done:
            self.advance(self.value)
        return self.result


def meanwhile(value, *jobs):
    open_jobs = [j for j in jobs if j is not None and not j.done]
    if not open_jobs:
        return value
    value, held = lax.optimization_barrier((value, tuple(j.value for j in open_jobs)))
    for job, got in zip(open_jobs, held):
        job.advance(got)
    return value


def held(value, *jobs):
    open_jobs = [j for j in jobs if j is not None and not j.done]
    if not open_jobs:
        return value
    value, kept = lax.optimization_barrier((value, tuple(j.value for j in open_jobs)))
    for job, got in zip(open_jobs, kept):
        job.value = got
    return value


def shards(
    tokens,
    cotangent,
    norm_gains,
    norm_biases,
    qkv_weight,
    qkv_bias,
    out_weight,
    gate_up_weight,
    down_weight,
):
    own_rows = tokens.shape[1]
    model = tokens.shape[2]
    heads_width = qkv_weight.shape[3]
    plan = Line(own_rows)
    tables = rotary_tables(plan.places)
    tables_back = (tables[0], -tables[1], -tables[2])
    qpos = plan.places[:, None]
    near_places = plan.places[None, None, :]
    far_places = jnp.stack(plan.far_places)[:, None, :]
    all_places = jnp.concatenate([near_places, far_places])
    gains = (norm_gains)
    biases = (norm_biases)
    qkv_bias_own = lax.dynamic_slice_in_dim(qkv_bias, lax.axis_index("tensor") * heads_width, heads_width, 2)

    def weight_jobs(layer, after):
        (qkv_all, out_all, gate_up_all, down_all), after = lax.optimization_barrier(
            ((qkv_weight, out_weight, gate_up_weight, down_weight), after)
        )
        matrices = {
            "qkv": jnp.transpose(qkv_all[layer], (1, 0, 2)),
            "out": out_all[layer],
            "gate": gate_up_all[layer, :, 0],
            "up": gate_up_all[layer, :, 1],
            "down": down_all[layer],
        }
        return {n: Job(weight_stages(v)) for n, v in matrices.items()}, after

    now, unused = weight_jobs(0, ())
    for name in ("qkv", "out", "gate", "up"):
        now[name].advance(now[name].value)
    stream = tokens[0].astype(WIDE)
    later = {}
    saved = []
    for layer in range(LAYERS):
        last = layer + 1 == LAYERS
        normed_one, unit_one, inverse_one = layer_norm_rows(
            stream, gains[layer, 0], biases[layer, 0]
        )
        rows_one = plan.gather_rows(normed_one.astype(LOW))
        if layer == 0:
            rows_one = meanwhile(rows_one, now["qkv"], now["down"])
        else:
            rows_one = meanwhile(rows_one, now["out"], now["gate"], now["down"])
        qkv_full = now["qkv"].finish()
        queries, keys_values = project(rows_one, qkv_full, qkv_bias_own[layer], tables)
        if layer == 0:
            late_cotangent, queries = lax.optimization_barrier((cotangent[0], queries))
            grad_stream = late_cotangent.astype(WIDE)
            branch = plan.gather_rows(late_cotangent)
        prepared = {}
        if not last:
            prepared, queries = weight_jobs(layer + 1, queries)
        far_kv = plan.far_keys(keys_values)
        attended, lse = attend(qpos, all_places, queries, [keys_values, *far_kv])
        attended_low = meanwhile(attended.astype(LOW), now["out"])
        attended_low = held(attended_low, *map(prepared.get, ("gate", "up")))
        if layer == 0:
            attended_low, branch = lax.optimization_barrier((attended_low, branch))
        else:
            attended_low = meanwhile(attended_low, now["up"])
        out_full = now["out"].finish()
        mid = stream + plan.sum_of(plan.sum_rows(times_wide(attended_low, out_full, "out")))
        mid = meanwhile(mid, now["gate"])
        if layer > 0:
            mid = meanwhile(mid, now["down"])
        else:
            later = prepared
        normed_two, unit_two, inverse_two = layer_norm_rows(mid, gains[layer, 1], biases[layer, 1])
        rows_two = plan.gather_rows(normed_two.astype(LOW))
        rows_two = meanwhile(rows_two, now["up"], now["down"], later.get("qkv"))
        flat = lambda v: v.reshape(v.shape[0] * v.shape[1], v.shape[2])
        gate_full, up_full = flat(now["gate"].finish()), flat(now["up"].finish())
        gate, up, activated = gate_up_rows(rows_two, gate_full, up_full)
        activated = meanwhile(activated, later.get("out"), later.get("gate"))
        down_full = now["down"].finish()
        if not last:
            stream = mid + plan.sum_of(
                plan.sum_rows(times_wide(activated, down_full, "down"))
            )
            stream = meanwhile(stream, later.get("qkv"), later.get("up"))
        saved.append(
            (
                (qkv_full, out_full, gate_full, up_full, down_full),
                (rows_one, unit_one, inverse_one),
                (queries, keys_values, far_kv, attended, attended_low, lse),
                (rows_two, unit_two, inverse_two),
                (gate, up, activated),
            )
        )
        now = later
    grad_jobs = [None] * LAYERS
    gain_grads = [None] * LAYERS
    bias_grads = [None] * LAYERS
    qkv_bias_grads = [None] * LAYERS
    for layer in range(LAYERS - 1, -1, -1):
        (
            (qkv_full, out_full, gate_full, up_full, down_full),
            (rows_one, unit_one, inverse_one),
            (queries, keys_values, far_kv, attended, attended_low, lse),
            (rows_two, unit_two, inverse_two),
            (gate, up, activated),
        ) = saved[layer]
        mine = {}
        grad_jobs[layer] = mine
        above = grad_jobs[layer + 1] if layer + 1 < LAYERS else {}
        old = lambda *keys: [above.get(k) for k in keys]

        def own_part(value, r):
            index = lax.axis_index("dp") ^ r
            width = value.shape[1] // lax.axis_size("dp")
            return lax.dynamic_slice_in_dim(value, index * width, width, 1)

        def in_job(a, b):
            return Job(grad_stages(plan, outer(a, b), 0))

        def out_job(a, b):
            return Job(grad_stages(plan, outer(a, b), 1))

        if layer + 1 < LAYERS:
            branch = plan.gather_rows(grad_low)
        branch = meanwhile(branch, *old("gate", "up", "out"))
        if layer == 0:
            down_grad, branch = lax.optimization_barrier(
                (outer(activated, branch), branch)
            )
            mine["down"] = Job(grad_stages(plan, down_grad, 1))
        grad_gate, grad_up = gate_up_back(branch, down_full, gate, up)
        partial_in = gate_up_in(grad_gate, grad_up, gate_full, up_full)
        summed = plan.sum_rows(partial_in)
        summed = meanwhile(summed, *old("up", "out", "qkv"))
        hidden_grad, hidden_low, gain_two, bias_two = norm_back(
            summed, unit_two, inverse_two, gains[layer, 1], grad_stream
        )
        hidden_low, (branch, grad_gate, grad_up) = lax.optimization_barrier(
            (hidden_low, (branch, grad_gate, grad_up))
        )
        if layer > 0:
            mine["down"] = out_job(activated, branch)
        mine["gate"] = in_job(rows_two, grad_gate)
        if layer == 0:
            mine["up"] = in_job(rows_two, grad_up)
        top = layer + 1 == LAYERS
        if top:
            late, hidden_low = lax.optimization_barrier((activated, hidden_low))
            partial_out = times_wide(late, down_full, "down")
        attention = plan.gather_rows(hidden_low)
        attention = meanwhile(attention, *old("qkv"))
        if layer == 0:
            attention = meanwhile(attention, mine["down"])
        if top:
            attention, partial_out = lax.optimization_barrier((attention, partial_out))
            output = (mid + plan.sum_of(plan.sum_rows(partial_out))).astype(LOW)[None]
        grad_attended = out_back(attention, out_full)
        shared = (queries, grad_attended, attended, lse)
        far_queries, far_grads = attend_back(qpos, far_places, *shared, far_kv, LOW, [])
        if layer == 0:
            far_queries = meanwhile(far_queries, mine["down"])
        returned = plan.far_key_grads(far_grads)
        grad_queries, grad_kv = attend_back(
            qpos, near_places, *shared, [keys_values], WIDE, [far_queries]
        )
        if top:
            grad_queries, output = lax.optimization_barrier((grad_queries, output))
        projected, qkv_bias_grads[layer] = project_back(
            grad_queries, grad_kv[0], returned, tables_back
        )
        projected, (attention, grad_up) = lax.optimization_barrier(
            (projected, (attention, grad_up))
        )
        if layer > 0:
            mine["up"] = in_job(rows_two, grad_up)
        if layer == 0:
            mine["out"] = Job(
                pair_stages(plan, lambda r, a=attention: (attended_low, own_part(a, r)), 1)
            )
        else:
            mine["out"] = out_job(attended_low, attention)
        projected = meanwhile(projected, mine["down"] if layer > 0 else None, *old("qkv"))
        if not top:
            above_done, projected = lax.optimization_barrier(
                ({k: j.finish() for k, j in above.items()}, projected)
            )
            sums = above_done
            results = [
                finish_projections(None, layer + 1, sums["qkv"]),
                finish_matrix(None, layer + 1, sums["out"], "finish_out"),
                finish_gate_up(None, layer + 1, sums["gate"], sums["up"]),
                finish_matrix(None, layer + 1, sums["down"], "finish_down"),
            ]
        if layer == 0:
            mine["qkv"] = Job(
                pair_stages(plan, lambda r, b=projected: (own_part(rows_one, r), b), 0)
            )
            projected = meanwhile(projected, *map(mine.get, ("qkv", "out", "gate")))
        partial_in = project_in(projected, qkv_full)
        if layer == 0:
            partial_in = meanwhile(partial_in, mine["up"], mine["qkv"])
            partial_in = held(partial_in, mine["out"])
        summed = plan.sum_rows(partial_in)
        if layer > 0:
            summed = meanwhile(summed, mine["down"])
        else:
            summed = meanwhile(summed, *map(mine.get, ("gate", "out", "qkv")))
        grad_stream, grad_low, gain_one, bias_one = norm_back(
            summed, unit_one, inverse_one, gains[layer, 0], hidden_grad
        )
        if layer > 0:
            grad_low, projected = lax.optimization_barrier((grad_low, projected))
            mine["qkv"] = in_job(rows_one, projected)
            grad_low = meanwhile(grad_low, mine["gate"])
        gain_grads[layer] = jnp.stack([gain_one, gain_two])
        bias_grads[layer] = jnp.stack([bias_one, bias_two])

    tokens_grad = grad_low[None]
    padded_bias = lax.dynamic_update_slice_in_dim(
        jnp.zeros((LAYERS, 3, qkv_bias.shape[2]), WIDE),
        jnp.stack(qkv_bias_grads),
        lax.axis_index("tensor") * heads_width,
        2,
    )
    small = jnp.concatenate(
        [
            (jnp.stack(gain_grads)).reshape(LAYERS * 2, model),
            (jnp.stack(bias_grads)).reshape(LAYERS * 2, model),
            padded_bias.reshape(LAYERS * 3, qkv_bias.shape[2]),
        ],
        axis=0,
    )
    sums = {k: j.finish() for k, j in grad_jobs[0].items()}
    for axis in ("dp", "tensor", "ctx"):
        if axis == "ctx":
            large = [
                finish_gate_up(results[2], 0, sums["gate"], sums["up"]),
                finish_matrix(results[3], 0, sums["down"], "finish_down"),
            ]
            small, large = lax.optimization_barrier((small, large))
        for bit in bits_of(lax.axis_size(axis)):
            small = small + swapped(small, axis, bit)
        if axis == "dp":
            small, results = lax.optimization_barrier((small, results))
    results = [
        finish_projections(results[0], 0, sums["qkv"]),
        finish_matrix(results[1], 0, sums["out"], "finish_out"),
        *large,
    ]
    return (
        output,
        tokens_grad,
        small[: LAYERS * 2].reshape(LAYERS, 2, model),
        small[LAYERS * 2 : LAYERS * 4].reshape(LAYERS, 2, model),
        jnp.transpose(results[0], (0, 2, 1, 3)),
        small[LAYERS * 4 :].reshape(LAYERS, 3, qkv_bias.shape[2]),
        *results[1:],
    )


def solution(mesh):
    rows = P("dp", ("ctx", "tensor"), None)
    wide = P(None, "dp", None, "tensor")
    tall = P(None, "tensor", "dp")
    return jax.shard_map(
        shards,
        mesh=mesh,
        in_specs=(rows, rows, P(), P(), wide, P(), tall, wide, tall),
        out_specs=(rows, rows, P(), P(), wide, P(), tall, wide, tall),
        check_vma=False,
    )
```

```python
import functools

import jax
import jax.numpy as jnp
from jax import lax
from jax.experimental import pallas as pl
from jax.experimental.pallas import tpu as pltpu
from jax.sharding import PartitionSpec as P

HD = 64
ROT = 16
LAYERS = 2

MASKED = -1e30
EPSILON = 1e-05
LOW = jnp.bfloat16
WIDE = jnp.float32


def layer_norm_rows(stream, gain, bias):
    row_mean = jnp.mean(stream, axis=-1, keepdims=True)
    centered = stream - row_mean
    inverse = lax.rsqrt(jnp.mean(centered * centered, axis=-1, keepdims=True) + EPSILON)
    unit_rows = centered * inverse
    return (unit_rows * gain + bias, unit_rows, inverse)


def rotary_tables(positions):
    half_rot = ROT // 2
    frequency = 10000.0 ** (-(jnp.arange(half_rot, dtype=jnp.float32) * 2.0) / ROT)
    angles = positions.astype(jnp.float32)[:, None] * frequency[None, :]
    cosine, sine = jnp.cos(angles), jnp.sin(angles)
    rest = jnp.zeros((angles.shape[0], HD - ROT), WIDE)
    none = jnp.zeros_like(sine)
    heads = lambda *parts: jnp.tile(jnp.concatenate(parts, axis=1), (1, PAIR // HD))
    return (
        heads(cosine, cosine, rest + 1.0),
        heads(-sine, none, rest),
        heads(none, sine, rest),
    )


def rotated(flat, cos_ref, right_ref, left_ref):
    shift = ROT // 2
    found = []
    for start in range(0, flat.shape[1], PAIR):
        v = flat[:, start : start + PAIR]
        right, left = pltpu.roll(v, PAIR - shift, 1), pltpu.roll(v, shift, 1)
        found.append(v * cos_ref[...] + right * right_ref[...] + left * left_ref[...])
    return jnp.concatenate(found, axis=1)


def dot(a, b, dims):
    return lax.dot_general(a, b, (dims, ((), ())), preferred_element_type=WIDE)


PAIR = 128


NN = ((1,), (0,))
NT = ((1,), (1,))
TN = ((0,), (0,))


def total_of(terms):
    return functools.reduce(lambda a, b: a + b, terms)


def work(flops):
    return pl.CostEstimate(flops=int(flops), bytes_accessed=0, transcendentals=0)


TILE = 512


def tiled(kernel, name, steps, ins, outs, flops):
    return pl.pallas_call(
        kernel,
        grid=(steps,),
        in_specs=[pl.BlockSpec(block, index) for _, block, index in ins],
        out_specs=[pl.BlockSpec(block, index) for _, block, index in outs],
        out_shape=[shape for shape, _, _ in outs],
        compiler_params=pltpu.CompilerParams(vmem_limit_bytes=48 * 1024 * 1024),
        cost_estimate=work(2.5 * flops),
        name=name,
    )(*[array for array, _, _ in ins])


def whole_block(array):
    return (array, array.shape, lambda i: (0,) * array.ndim)


def column_block(array):
    return (array, (array.shape[0], TILE), lambda i: (0, i))


def row_block(array):
    return (array, (TILE, array.shape[1]), lambda i: (i, 0))


def gate_up_kernel(rows_ref, gate_w_ref, up_w_ref, gate_ref, up_ref, activated_ref):
    rows = rows_ref[...]
    gate = dot(rows, gate_w_ref[...], NN)
    up = dot(rows, up_w_ref[...], NN)
    gate_ref[...] = gate
    up_ref[...] = up
    activated_ref[...] = (gate * jax.nn.sigmoid(gate) * up).astype(LOW)


def gate_up_rows(rows, gate_weight, up_weight):
    count, hidden = rows.shape[0], gate_weight.shape[1]
    shapes = [jax.ShapeDtypeStruct((count, hidden), t) for t in (WIDE, WIDE, LOW)]
    return tiled(
        gate_up_kernel,
        "gate_up",
        pl.cdiv(hidden, TILE),
        [whole_block(rows), column_block(gate_weight), column_block(up_weight)],
        [column_block(s) for s in shapes],
        4 * rows.size * hidden,
    )


def back_sum(rows, weight_ref):
    width = weight_ref.shape[2]
    return total_of(
        dot(rows[:, r * width : (r + 1) * width], weight_ref[r], NT)
        for r in range(weight_ref.shape[0])
    )


def tall_block(array):
    return (array, (array.shape[0], TILE, array.shape[2]), lambda i: (0, i, 0))


def gate_up_back_kernel(rows_ref, weight_ref, gate_ref, up_ref, grad_gate_ref, grad_up_ref):
    grad = back_sum(rows_ref[...], weight_ref)
    gate, up = gate_ref[...], up_ref[...]
    s = jax.nn.sigmoid(gate)
    grad_gate_ref[...] = (grad * up * s * (1.0 + gate * (1.0 - s))).astype(LOW)
    grad_up_ref[...] = (grad * (gate * s)).astype(LOW)


def gate_up_back(rows, down_weight, gate, up):
    count, hidden = gate.shape
    shape = jax.ShapeDtypeStruct((count, hidden), LOW)
    return tiled(
        gate_up_back_kernel,
        "gate_up_back",
        pl.cdiv(hidden, TILE),
        [whole_block(rows), tall_block(down_weight), column_block(gate), column_block(up)],
        [column_block(shape)] * 2,
        2 * rows.size * hidden,
    )


def out_back_kernel(rows_ref, weight_ref, out_ref):
    out_ref[...] = back_sum(rows_ref[...], weight_ref).astype(LOW)


def out_back(rows, weight):
    shape = jax.ShapeDtypeStruct((rows.shape[0], weight.shape[1]), LOW)
    return tiled(
        out_back_kernel,
        "out_back",
        shape.shape[1] // TILE,
        [whole_block(rows), tall_block(weight)],
        [column_block(shape)],
        2 * rows.size * shape.shape[1],
    )[0]


def wide_kernel(rows_ref, weight_ref, out_ref):
    out_ref[...] = dot(rows_ref[...], weight_ref[0], NN).astype(LOW)


def times_wide(rows, weight, name):
    blocks, depth, width = weight.shape
    per = width // TILE
    shape = jax.ShapeDtypeStruct((rows.shape[0], blocks * width), LOW)
    return tiled(
        wide_kernel,
        name,
        blocks * per,
        [whole_block(rows), (weight, (1, depth, TILE), lambda i: (i // per, 0, i % per))],
        [column_block(shape)],
        2 * rows.size * blocks * width,
    )[0]


def gate_up_in_kernel(gate_ref, up_ref, gate_w_ref, up_w_ref, out_ref):
    total = dot(gate_ref[...], gate_w_ref[...], NT) + dot(up_ref[...], up_w_ref[...], NT)
    out_ref[...] = total.astype(LOW)


def gate_up_in(grad_gate, grad_up, gate_weight, up_weight):
    shape = jax.ShapeDtypeStruct((grad_gate.shape[0], gate_weight.shape[0]), LOW)
    return tiled(
        gate_up_in_kernel,
        "gate_up_in",
        shape.shape[1] // TILE,
        [whole_block(grad_gate), whole_block(grad_up), row_block(gate_weight), row_block(up_weight)],
        [column_block(shape)],
        4 * grad_gate.size * shape.shape[1],
    )[0]


def project_in_kernel(rows_ref, weight_ref, out_ref):
    width = weight_ref.shape[3]
    out_ref[...] = total_of(
        dot(rows_ref[:, c * width : (c + 1) * width], weight_ref[0, c], NT) for c in range(3)
    ).astype(LOW)


def project_in(rows, weight):
    blocks, three, depth, width = weight.shape
    per = depth // TILE
    shape = jax.ShapeDtypeStruct((rows.shape[0], blocks * depth), LOW)
    return tiled(
        project_in_kernel,
        "project_in",
        blocks * per,
        [whole_block(rows), (weight, (1, three, TILE, width), lambda i: (i // per, 0, i % per, 0))],
        [column_block(shape)],
        2 * rows.size * blocks * depth,
    )[0]


def outer_kernel(a_ref, b_ref, out_ref):
    out_ref[...] = dot(a_ref[...], b_ref[...], TN).astype(LOW)


def outer(a, b):
    shape = jax.ShapeDtypeStruct((a.shape[1], b.shape[1]), LOW)
    return tiled(
        outer_kernel,
        "outer",
        pl.cdiv(a.shape[1], TILE),
        [column_block(a), whole_block(b)],
        [row_block(shape)],
        a.size * b.shape[1] * 0.8,
    )[0]


def project_kernel(rows_ref, weight_ref, bias_ref, cos_ref, right_ref, left_ref, q_ref, kv_ref):
    blocks, _, depth, width = weight_ref.shape
    flat = dot(rows_ref[...], weight_ref[...].reshape(blocks * depth, width), NN) + bias_ref[0]
    step = pl.program_id(0)

    @pl.when(step == 0)
    def _():
        kv_ref[...] = rotated(flat, cos_ref, right_ref, left_ref).astype(LOW)

    @pl.when(step == 1)
    def _():
        kv_ref[...] = flat.astype(LOW)

    @pl.when(step == 2)
    def _():
        q_ref[...] = rotated(flat, cos_ref, right_ref, left_ref).astype(LOW)


def project(rows, weight, bias, tables):
    count = rows.shape[0]
    blocks, _, depth, width = weight.shape
    fixed = lambda i: (0, 0)
    shapes = [jax.ShapeDtypeStruct((k * count, width), LOW) for k in (1, 2)]
    return tiled(
        project_kernel,
        "project",
        3,
        [
            whole_block(rows),
            (weight, (blocks, 1, depth, width), lambda i: (0, (i + 1) % 3, 0, 0)),
            (bias[:, None, :], (1, 1, width), lambda i: ((i + 1) % 3, 0, 0)),
        ]
        + [(t, (count, PAIR), fixed) for t in tables],
        [
            (shapes[0], (count, width), fixed),
            (shapes[1], (count, width), lambda i: (jnp.minimum(i, 1), 0)),
        ],
        6 * rows.size * width,
    )


def project_back_kernel(far, dq_ref, dkv_ref, *refs):
    far_refs = refs[:far]
    cos_ref, right_ref, left_ref, out_ref, sum_ref = refs[far:]
    step = pl.program_id(0)

    def put(value):
        out_ref[...] = value.astype(LOW)
        sum_ref[0] = jnp.sum(value, axis=0, keepdims=True)

    def key_value():
        return total_of([dkv_ref[...]] + [r[...].astype(WIDE) for r in far_refs])

    @pl.when(step == 0)
    def _():
        put(rotated(dq_ref[...], cos_ref, right_ref, left_ref))

    @pl.when(step == 1)
    def _():
        put(rotated(key_value(), cos_ref, right_ref, left_ref))

    @pl.when(step == 2)
    def _():
        put(key_value())


def project_back(dq, dkv, far, tables):
    count, width = dq.shape
    fixed = lambda i: (0, 0)
    lower = pl.BlockSpec((count, width), lambda i: (jnp.maximum(i - 1, 0), 0))
    out, sums = pl.pallas_call(
        functools.partial(project_back_kernel, len(far)),
        grid=(3,),
        in_specs=[pl.BlockSpec((count, width), fixed)]
        + [lower] * (1 + len(far))
        + [pl.BlockSpec((count, PAIR), fixed)] * 3,
        out_specs=[
            pl.BlockSpec((count, width), lambda i: (0, i)),
            pl.BlockSpec((1, 1, width), lambda i: (i, 0, 0)),
        ],
        out_shape=[
            jax.ShapeDtypeStruct((count, 3 * width), LOW),
            jax.ShapeDtypeStruct((3, 1, width), WIDE),
        ],
        compiler_params=pltpu.CompilerParams(vmem_limit_bytes=32 * 1024 * 1024),
        cost_estimate=work(14000 * count * width),
        name="project_back",
    )(dq, dkv, *far, *tables)
    return out, sums[:, 0]


GROUP = 256


def attend_kernel(blocks, qpos_ref, kpos_ref, q_ref, *refs):
    keys, values = refs[: 2 * blocks : 2], refs[1 : 2 * blocks : 2]
    out_ref, lse_ref = refs[2 * blocks :]
    allowed = [kpos_ref[b] <= qpos_ref[...] for b in range(blocks)]
    for half in range(q_ref.shape[1] // HD):
        lanes = slice(half * HD, (half + 1) * HD)
        q = q_ref[:, lanes] * jnp.asarray(HD**-0.5, LOW)
        top, total, acc = None, None, None
        for b in range(blocks):
            s = jnp.where(allowed[b], dot(q, keys[b][:, lanes], NT), MASKED)
            block_top = jnp.max(s, axis=1, keepdims=True)
            new_top = block_top if b == 0 else jnp.maximum(top, block_top)
            p = jnp.exp(s - new_top)
            block_total = jnp.sum(p, axis=1, keepdims=True)
            block_acc = dot(p.astype(LOW), values[b][:, lanes], NN)
            if b == 0:
                total, acc = block_total, block_acc
            else:
                factor = jnp.exp(top - new_top)
                total = total * factor + block_total
                acc = acc * factor + block_acc
            top = new_top
        out_ref[:, lanes] = acc / total
        lse_ref[:, lanes] = jnp.broadcast_to(top + jnp.log(total), acc.shape)


def group_call(kernel, name, rows, width, kpos, operands, stacked, outs, flops):
    blocks, _, key_rows = kpos.shape
    group = GROUP if blocks <= 2 else PAIR
    column = lambda i: (0, i)
    specs = {
        "row": pl.BlockSpec((rows, group), column),
        "keys": pl.BlockSpec((2 * key_rows, group), column),
    }
    shapes = {"row": (rows, width), "keys": (2 * key_rows, width)}
    halves = [pl.BlockSpec((key_rows, group), lambda i, c=c: (c, i)) for c in range(2)]
    common = [
        pl.BlockSpec((rows, 1), lambda i: (0, 0)),
        pl.BlockSpec((blocks, 1, key_rows), lambda i: (0, 0, 0)),
    ]
    return pl.pallas_call(
        kernel,
        grid=(width // group,),
        in_specs=common + [specs["row"]] * (len(operands) - 1) + halves * len(stacked),
        out_specs=[specs[k] for k, _ in outs],
        out_shape=[jax.ShapeDtypeStruct(shapes[k], t) for k, t in outs],
        compiler_params=pltpu.CompilerParams(vmem_limit_bytes=40 * 1024 * 1024),
        cost_estimate=work(flops * rows * key_rows * blocks * width),
        name=name,
    )(operands[0], kpos, *operands[1:], *[s for s in stacked for c in range(2)])


def attend(qpos, kpos, q, stacked):
    rows, width = q.shape
    kernel = functools.partial(attend_kernel, len(stacked))
    outs = [("row", WIDE)] * 2
    return group_call(kernel, "attend", rows, width, kpos, [qpos, q], stacked, outs, 43)


def attend_back_kernel(blocks, more, qpos_ref, kpos_ref, q_ref, grad_ref, out_ref, lse_ref, *refs):
    before, refs = refs[:more], refs[more:]
    keys, values = refs[: 2 * blocks : 2], refs[1 : 2 * blocks : 2]
    dq_ref = refs[2 * blocks]
    dboth = refs[2 * blocks + 1 :]
    key_rows = keys[0].shape[0]
    allowed = [kpos_ref[b] <= qpos_ref[...] for b in range(blocks)]
    scale = HD**-0.5
    for half in range(q_ref.shape[1] // HD):
        lanes = slice(half * HD, (half + 1) * HD)
        q = q_ref[:, lanes] * jnp.asarray(scale, LOW)
        grad = grad_ref[:, lanes]
        lse = lse_ref[:, half * HD : half * HD + 1]
        delta = jnp.sum(grad.astype(WIDE) * out_ref[:, lanes], axis=1, keepdims=True)
        dq = []
        for b in range(blocks):
            k = keys[b][:, lanes]
            s = jnp.where(allowed[b], dot(q, k, NT), MASKED)
            p = jnp.exp(s - lse)
            dp = dot(grad, values[b][:, lanes], NT)
            ds = (p * (dp - delta)).astype(LOW)
            kind = dboth[b].dtype
            dboth[b][key_rows:, lanes] = dot(p.astype(LOW), grad, TN).astype(kind)
            dboth[b][:key_rows, lanes] = dot(ds, q, TN).astype(kind)
            dq.append(dot(ds, k, NN))
        dq_ref[:, lanes] = total_of([total_of(dq) * scale] + [r[:, lanes] for r in before])


def attend_back(qpos, kpos, q, grad, out, lse, stacked, kind, before):
    rows, width = q.shape
    results = group_call(
        functools.partial(attend_back_kernel, len(stacked), len(before)),
        "attend_back",
        rows,
        width,
        kpos,
        [qpos, q, grad, out, lse, *before],
        stacked,
        [("row", WIDE)] + [("keys", kind)] * len(stacked),
        75,
    )
    return results[0], results[1:]


def norm_back_kernel(count, *refs):
    terms = refs[:count]
    unit_ref, inverse_ref, gain_ref, base_ref = refs[count : count + 4]
    grad_ref, low_ref, gain_out_ref, bias_out_ref = refs[count + 4 :]
    grad_rows = total_of([t[...].astype(WIDE) for t in terms])
    unit = unit_ref[...]
    grad_unit = grad_rows * gain_ref[...]
    first_mean = jnp.mean(grad_unit, axis=-1, keepdims=True)
    second_mean = jnp.mean(grad_unit * unit, axis=-1, keepdims=True)
    total = base_ref[...] + inverse_ref[...] * (grad_unit - first_mean - unit * second_mean)
    grad_ref[...] = total
    low_ref[...] = total.astype(LOW)
    gain_out_ref[...] = jnp.sum(grad_rows * unit, axis=0, keepdims=True)
    bias_out_ref[...] = jnp.sum(grad_rows, axis=0, keepdims=True)


def norm_back(terms, unit, inverse, gain, base):
    rows, model = unit.shape
    fixed = lambda i: (0, 0)
    line = (1, model)
    operands = [*terms, unit, inverse, gain[None], base]
    shapes = [(rows, model)] * (len(terms) + 1) + [(rows, 1), line, (rows, model)]
    outs = [((rows, model), WIDE), ((rows, model), LOW), (line, WIDE), (line, WIDE)]
    results = tiled(
        functools.partial(norm_back_kernel, len(terms)),
        "norm_back",
        1,
        [(o, s, fixed) for o, s in zip(operands, shapes)],
        [(jax.ShapeDtypeStruct(s, t), s, fixed) for s, t in outs],
        1e9,
    )
    return results[0], results[1], results[2][0], results[3][0]


def finish(buffer, layer, terms, make, steps, ins, out, name):
    shape, block, place = out

    def kernel(*refs):
        refs[-1][...] = make(*[r[...].astype(WIDE) for r in refs[: len(terms)]])

    operands = list(terms)
    specs = [pl.BlockSpec(b, index) for b, index in ins]
    if buffer is not None:
        operands.append(buffer)
        specs.append(pl.BlockSpec(memory_space=pl.ANY))
    return pl.pallas_call(
        kernel,
        grid=(steps,),
        in_specs=specs,
        out_specs=pl.BlockSpec((1,) + block, lambda i: (layer,) + place(i)),
        out_shape=jax.ShapeDtypeStruct(shape, WIDE),
        input_output_aliases={} if buffer is None else {len(terms): 0},
        compiler_params=pltpu.CompilerParams(vmem_limit_bytes=48 * 1024 * 1024),
        cost_estimate=work(1e9),
        name=name,
    )(*operands)


def finish_matrix(buffer, layer, terms, name):
    rows, columns = terms[0].shape
    block = (rows // 4, columns)
    place = lambda i: (i, 0)
    out = ((LAYERS, rows, columns), block, place)
    make = lambda *t: total_of(t)[None]
    return finish(buffer, layer, terms, make, 4, [(block, place)] * len(terms), out, name)


def finish_projections(buffer, layer, terms):
    rows, columns = terms[0].shape
    width = columns // 3
    out = ((LAYERS, 3, rows, width), (1, rows, width), lambda i: (i, 0, 0))
    make = lambda *t: total_of(t)[None, None]
    ins = [((rows, width), lambda i: (0, i))] * len(terms)
    return finish(buffer, layer, terms, make, 3, ins, out, "finish_qkv")


def finish_gate_up(buffer, layer, gate_terms, up_terms):
    rows, columns = gate_terms[0].shape
    steps = 8
    block = (rows // steps, columns)
    out = ((LAYERS, rows, 2, columns), (rows // steps, 2, columns), lambda i: (i, 0, 0))
    count = len(gate_terms)
    make = lambda *t: jnp.stack([total_of(t[:count]), total_of(t[count:])], axis=1)[None]
    ins = [(block, lambda i: (i, 0))] * (2 * count)
    return finish(buffer, layer, gate_terms + up_terms, make, steps, ins, out, "finish_gate_up")


def bits_of(count):
    return [1 << k for k in range(count.bit_length() - 1)]


def swapped(value, axis, mask):
    count = lax.axis_size(axis)
    return lax.ppermute(value, axis, [(i, i ^ mask) for i in range(count)])


def joined(pieces, axis):
    return pieces[0] if len(pieces) == 1 else jnp.concatenate(pieces, axis=axis)


class Line:
    def __init__(self, own_rows):
        n_tensor, n_ctx = lax.axis_size("tensor"), lax.axis_size("ctx")
        tensor, ctx = lax.axis_index("tensor"), lax.axis_index("ctx")
        self.count, self.tensor = n_tensor, tensor
        row = jnp.arange(own_rows, dtype=jnp.int32)
        chip = (tensor + jnp.arange(n_tensor, dtype=jnp.int32)) % n_tensor
        place = (chip[:, None] * own_rows + row[None, :]).reshape(-1)
        block = n_tensor * own_rows
        self.places = ctx * block + place
        self.far_places = [
            jnp.where(ctx >= s, (ctx - s) * block + place, 1 << 30) for s in range(1, n_ctx)
        ]
        self.own_rows = own_rows

    def gather_rows(self, low):
        count, t = self.count, self.tensor
        send = lambda v, *route: lax.ppermute(v, "tensor", list(route))
        if count == 4:
            far = send(low, (0, 2), (2, 0), (1, 3), (3, 1))
            above = send(low, (0, 1), (1, 2), (2, 3))
            below = send(low, (1, 0), (2, 1), (3, 2))
            end = send(far, (2, 3), (1, 0))
            found = [low, jnp.where(t == 3, end, below), far, jnp.where(t == 0, end, above)]
        else:
            found = [low] + [
                send(low, *[((i + d) % count, i) for i in range(count)]) for d in range(1, count)
            ]
        return jnp.concatenate(found, axis=0)

    def sum_rows(self, low):
        rows, count, t = self.own_rows, self.count, self.tensor
        terms = [low[d * rows : (d + 1) * rows] for d in range(count)]
        send = lambda v, *route: lax.ppermute(v, "tensor", list(route))
        wide = lambda v: v.astype(WIDE)
        if count == 4:
            end = send(jnp.where(t == 0, terms[3], terms[1]), (0, 1), (3, 2))
            above = send(terms[1], (0, 1), (1, 2), (2, 3))
            below = send(terms[3], (3, 2), (2, 1), (1, 0))
            far = (wide(terms[2]) + wide(end)).astype(LOW)
            got = [send(far, (0, 2), (2, 0), (1, 3), (3, 1)), above, below]
        else:
            got = [
                send(terms[d], *[(i, (i + d) % count) for i in range(count)])
                for d in range(1, count)
            ]
        return (low, *got)

    def sum_of(self, terms):
        return total_of([terms[0][: self.own_rows].astype(WIDE)] + [t.astype(WIDE) for t in terms[1:]])

    def owner(self, low):
        count = lax.axis_size("ctx")
        if count != 2:
            return (lax.psum(low, "ctx") if count > 1 else low,)
        got = yield swapped(low, "ctx", 1)
        return (low, got)

    def far_keys(self, value):
        count = lax.axis_size("ctx")
        return [
            lax.ppermute(value, "ctx", [(i, i + s) for i in range(count - s)])
            for s in range(1, count)
        ]

    def far_key_grads(self, values):
        count = lax.axis_size("ctx")
        return [
            lax.ppermute(values[s - 1], "ctx", [(i + s, i) for i in range(count - s)])
            for s in range(1, count)
        ]


def weight_stages(shard):
    shard = yield shard
    return (yield lax.all_gather(shard, "dp"))


def grad_stages(plan, value, axis):
    got = yield lax.psum_scatter(value.astype(LOW), "dp", scatter_dimension=axis, tiled=True)
    return (yield from plan.owner(got))


def low_first(count):
    width = count.bit_length() - 1
    return sorted(range(count), key=lambda r: int(format(r, "b").zfill(width)[::-1] or "0", 2))


def pair_stages(plan, terms_of, axis):
    count = lax.axis_size("dp")

    def term(parts):
        factors = [terms_of(r) for r in parts]
        a = joined([f[0] for f in factors], 1) if axis == 0 else factors[0][0]
        b = joined([f[1] for f in factors], 1) if axis == 1 else factors[0][1]
        return outer(a, b)

    order = low_first(count)
    kept = None
    for bit in bits_of(count):
        if kept is None:
            sent = yield term(order[count // 2 :])
        else:
            kept, sent = jnp.split(kept, 2, axis=axis)
        got = yield swapped(sent.astype(LOW), "dp", bit)
        kept = (term(order[: count // 2]).astype(WIDE) if kept is None else kept) + got.astype(WIDE)
    return (yield from plan.owner(kept.astype(LOW)))


class Job:
    def __init__(self, stages):
        self.stages, self.value, self.result, self.done = stages, None, None, False
        self.advance(None)

    def advance(self, value):
        try:
            self.value = self.stages.send(value)
        except StopIteration as end:
            self.done, self.result, self.value = True, end.value, None

    def finish(self):
        while not self.done:
            self.advance(self.value)
        return self.result


def meanwhile(value, *jobs):
    open_jobs = [j for j in jobs if j is not None and not j.done]
    if not open_jobs:
        return value
    value, held = lax.optimization_barrier((value, tuple(j.value for j in open_jobs)))
    for job, got in zip(open_jobs, held):
        job.advance(got)
    return value


def held(value, *jobs):
    open_jobs = [j for j in jobs if j is not None and not j.done]
    if not open_jobs:
        return value
    value, kept = lax.optimization_barrier((value, tuple(j.value for j in open_jobs)))
    for job, got in zip(open_jobs, kept):
        job.value = got
    return value


def shards(
    tokens,
    cotangent,
    norm_gains,
    norm_biases,
    qkv_weight,
    qkv_bias,
    out_weight,
    gate_up_weight,
    down_weight,
):
    own_rows = tokens.shape[1]
    model = tokens.shape[2]
    heads_width = qkv_weight.shape[3]
    plan = Line(own_rows)
    tables = rotary_tables(plan.places)
    tables_back = (tables[0], -tables[1], -tables[2])
    qpos = plan.places[:, None]
    near_places = plan.places[None, None, :]
    far_places = jnp.stack(plan.far_places)[:, None, :]
    all_places = jnp.concatenate([near_places, far_places])
    gains = (norm_gains)
    biases = (norm_biases)
    qkv_bias_own = lax.dynamic_slice_in_dim(qkv_bias, lax.axis_index("tensor") * heads_width, heads_width, 2)

    def weight_jobs(layer, after):
        (qkv_all, out_all, gate_up_all, down_all), after = lax.optimization_barrier(
            ((qkv_weight, out_weight, gate_up_weight, down_weight), after)
        )
        matrices = {
            "qkv": jnp.transpose(qkv_all[layer], (1, 0, 2)),
            "out": out_all[layer],
            "gate": gate_up_all[layer, :, 0],
            "up": gate_up_all[layer, :, 1],
            "down": down_all[layer],
        }
        return {n: Job(weight_stages(v)) for n, v in matrices.items()}, after

    now, unused = weight_jobs(0, ())
    for name in ("qkv", "out", "gate", "up"):
        now[name].advance(now[name].value)
    stream = tokens[0].astype(WIDE)
    later = {}
    saved = []
    for layer in range(LAYERS):
        last = layer + 1 == LAYERS
        normed_one, unit_one, inverse_one = layer_norm_rows(
            stream, gains[layer, 0], biases[layer, 0]
        )
        rows_one = plan.gather_rows(normed_one.astype(LOW))
        if layer == 0:
            rows_one = meanwhile(rows_one, now["qkv"], now["down"])
        else:
            rows_one = meanwhile(rows_one, now["out"], now["gate"], now["down"])
        qkv_full = now["qkv"].finish()
        queries, keys_values = project(rows_one, qkv_full, qkv_bias_own[layer], tables)
        if layer == 0:
            late_cotangent, queries = lax.optimization_barrier((cotangent[0], queries))
            grad_stream = late_cotangent.astype(WIDE)
            branch = plan.gather_rows(late_cotangent)
        prepared = {}
        if not last:
            prepared, queries = weight_jobs(layer + 1, queries)
        far_kv = plan.far_keys(keys_values)
        attended, lse = attend(qpos, all_places, queries, [keys_values, *far_kv])
        attended_low = meanwhile(attended.astype(LOW), now["out"])
        attended_low = held(attended_low, *map(prepared.get, ("gate", "up")))
        if layer == 0:
            attended_low, branch = lax.optimization_barrier((attended_low, branch))
        else:
            attended_low = meanwhile(attended_low, now["up"])
        out_full = now["out"].finish()
        mid = stream + plan.sum_of(plan.sum_rows(times_wide(attended_low, out_full, "out")))
        mid = meanwhile(mid, now["gate"])
        if layer > 0:
            mid = meanwhile(mid, now["down"])
        else:
            later = prepared
        normed_two, unit_two, inverse_two = layer_norm_rows(mid, gains[layer, 1], biases[layer, 1])
        rows_two = plan.gather_rows(normed_two.astype(LOW))
        rows_two = meanwhile(rows_two, now["up"], now["down"], later.get("qkv"))
        flat = lambda v: v.reshape(v.shape[0] * v.shape[1], v.shape[2])
        gate_full, up_full = flat(now["gate"].finish()), flat(now["up"].finish())
        gate, up, activated = gate_up_rows(rows_two, gate_full, up_full)
        activated = meanwhile(activated, later.get("out"), later.get("gate"))
        down_full = now["down"].finish()
        if not last:
            stream = mid + plan.sum_of(
                plan.sum_rows(times_wide(activated, down_full, "down"))
            )
            stream = meanwhile(stream, later.get("qkv"), later.get("up"))
        saved.append(
            (
                (qkv_full, out_full, gate_full, up_full, down_full),
                (rows_one, unit_one, inverse_one),
                (queries, keys_values, far_kv, attended, attended_low, lse),
                (rows_two, unit_two, inverse_two),
                (gate, up, activated),
            )
        )
        now = later
    grad_jobs = [None] * LAYERS
    gain_grads = [None] * LAYERS
    bias_grads = [None] * LAYERS
    qkv_bias_grads = [None] * LAYERS
    for layer in range(LAYERS - 1, -1, -1):
        (
            (qkv_full, out_full, gate_full, up_full, down_full),
            (rows_one, unit_one, inverse_one),
            (queries, keys_values, far_kv, attended, attended_low, lse),
            (rows_two, unit_two, inverse_two),
            (gate, up, activated),
        ) = saved[layer]
        mine = {}
        grad_jobs[layer] = mine
        above = grad_jobs[layer + 1] if layer + 1 < LAYERS else {}
        old = lambda *keys: [above.get(k) for k in keys]

        def own_part(value, r):
            index = lax.axis_index("dp") ^ r
            width = value.shape[1] // lax.axis_size("dp")
            return lax.dynamic_slice_in_dim(value, index * width, width, 1)

        def in_job(a, b):
            return Job(grad_stages(plan, outer(a, b), 0))

        def out_job(a, b):
            return Job(grad_stages(plan, outer(a, b), 1))

        if layer + 1 < LAYERS:
            branch = plan.gather_rows(grad_low)
        branch = meanwhile(branch, *old("gate", "up", "out"))
        if layer == 0:
            down_grad, branch = lax.optimization_barrier(
                (outer(activated, branch), branch)
            )
            mine["down"] = Job(grad_stages(plan, down_grad, 1))
        grad_gate, grad_up = gate_up_back(branch, down_full, gate, up)
        partial_in = gate_up_in(grad_gate, grad_up, gate_full, up_full)
        summed = plan.sum_rows(partial_in)
        summed = meanwhile(summed, *old("up", "out", "qkv"))
        hidden_grad, hidden_low, gain_two, bias_two = norm_back(
            summed, unit_two, inverse_two, gains[layer, 1], grad_stream
        )
        hidden_low, (branch, grad_gate, grad_up) = lax.optimization_barrier(
            (hidden_low, (branch, grad_gate, grad_up))
        )
        if layer > 0:
            mine["down"] = out_job(activated, branch)
        mine["gate"] = in_job(rows_two, grad_gate)
        top = layer + 1 == LAYERS
        if top:
            late, hidden_low = lax.optimization_barrier((activated, hidden_low))
            partial_out = times_wide(late, down_full, "down")
        attention = plan.gather_rows(hidden_low)
        attention = meanwhile(attention, *old("qkv"))
        if layer == 0:
            attention = meanwhile(attention, mine["down"])
        if top:
            attention, partial_out = lax.optimization_barrier((attention, partial_out))
            output = (mid + plan.sum_of(plan.sum_rows(partial_out))).astype(LOW)[None]
        grad_attended = out_back(attention, out_full)
        shared = (queries, grad_attended, attended, lse)
        far_queries, far_grads = attend_back(qpos, far_places, *shared, far_kv, LOW, [])
        if layer == 0:
            far_queries, grad_up = lax.optimization_barrier((far_queries, grad_up))
            mine["up"] = in_job(rows_two, grad_up)
            far_queries = meanwhile(far_queries, mine["down"])
        returned = plan.far_key_grads(far_grads)
        grad_queries, grad_kv = attend_back(
            qpos, near_places, *shared, [keys_values], WIDE, [far_queries]
        )
        if top:
            grad_queries, output = lax.optimization_barrier((grad_queries, output))
        projected, qkv_bias_grads[layer] = project_back(
            grad_queries, grad_kv[0], returned, tables_back
        )
        projected, (attention, grad_up) = lax.optimization_barrier(
            (projected, (attention, grad_up))
        )
        if layer > 0:
            mine["up"] = in_job(rows_two, grad_up)
        if layer == 0:
            mine["out"] = Job(
                pair_stages(plan, lambda r, a=attention: (attended_low, own_part(a, r)), 1)
            )
        else:
            mine["out"] = out_job(attended_low, attention)
        projected = meanwhile(projected, mine["down"] if layer > 0 else None, *old("qkv"))
        if not top:
            above_done, projected = lax.optimization_barrier(
                ({k: j.finish() for k, j in above.items()}, projected)
            )
            sums = above_done
            results = [
                finish_projections(None, layer + 1, sums["qkv"]),
                finish_matrix(None, layer + 1, sums["out"], "finish_out"),
                finish_gate_up(None, layer + 1, sums["gate"], sums["up"]),
                finish_matrix(None, layer + 1, sums["down"], "finish_down"),
            ]
        if layer == 0:
            mine["qkv"] = Job(
                pair_stages(plan, lambda r, b=projected: (own_part(rows_one, r), b), 0)
            )
            projected = meanwhile(projected, *map(mine.get, ("qkv", "out", "gate")))
        partial_in = project_in(projected, qkv_full)
        if layer == 0:
            partial_in = meanwhile(partial_in, mine["up"], mine["qkv"])
            partial_in = held(partial_in, mine["out"])
        summed = plan.sum_rows(partial_in)
        if layer > 0:
            summed = meanwhile(summed, mine["down"])
        else:
            summed = meanwhile(summed, *map(mine.get, ("gate", "out", "qkv")))
        grad_stream, grad_low, gain_one, bias_one = norm_back(
            summed, unit_one, inverse_one, gains[layer, 0], hidden_grad
        )
        if layer > 0:
            grad_low, projected = lax.optimization_barrier((grad_low, projected))
            mine["qkv"] = in_job(rows_one, projected)
            grad_low = meanwhile(grad_low, mine["gate"])
        gain_grads[layer] = jnp.stack([gain_one, gain_two])
        bias_grads[layer] = jnp.stack([bias_one, bias_two])

    tokens_grad = grad_low[None]
    padded_bias = lax.dynamic_update_slice_in_dim(
        jnp.zeros((LAYERS, 3, qkv_bias.shape[2]), WIDE),
        jnp.stack(qkv_bias_grads),
        lax.axis_index("tensor") * heads_width,
        2,
    )
    small = jnp.concatenate(
        [
            (jnp.stack(gain_grads)).reshape(LAYERS * 2, model),
            (jnp.stack(bias_grads)).reshape(LAYERS * 2, model),
            padded_bias.reshape(LAYERS * 3, qkv_bias.shape[2]),
        ],
        axis=0,
    )
    sums = {k: j.finish() for k, j in grad_jobs[0].items()}
    for axis in ("dp", "tensor", "ctx"):
        if axis == "ctx":
            large = [
                finish_gate_up(results[2], 0, sums["gate"], sums["up"]),
                finish_matrix(results[3], 0, sums["down"], "finish_down"),
            ]
            small, large = lax.optimization_barrier((small, large))
        for bit in bits_of(lax.axis_size(axis)):
            small = small + swapped(small, axis, bit)
        if axis == "dp":
            small, results = lax.optimization_barrier((small, results))
    results = [
        finish_projections(results[0], 0, sums["qkv"]),
        finish_matrix(results[1], 0, sums["out"], "finish_out"),
        *large,
    ]
    return (
        output,
        tokens_grad,
        small[: LAYERS * 2].reshape(LAYERS, 2, model),
        small[LAYERS * 2 : LAYERS * 4].reshape(LAYERS, 2, model),
        jnp.transpose(results[0], (0, 2, 1, 3)),
        small[LAYERS * 4 :].reshape(LAYERS, 3, qkv_bias.shape[2]),
        *results[1:],
    )


def solution(mesh):
    rows = P("dp", ("ctx", "tensor"), None)
    wide = P(None, "dp", None, "tensor")
    tall = P(None, "tensor", "dp")
    return jax.shard_map(
        shards,
        mesh=mesh,
        in_specs=(rows, rows, P(), P(), wide, P(), tall, wide, tall),
        out_specs=(rows, rows, P(), P(), wide, P(), tall, wide, tall),
        check_vma=False,
    )
```
